256 devices in a mesh: tile: 64 (over z, y, core), view: 4 (over x).
Axes of the slice: x: 4, y: 4, z: 8, core: 2. Of those that a mesh axis runs over, the one named last changes fastest.
Arguments:
- measured: float32 [4, 64, 256, 256], P('view', 'tile'), may hold values from -40 to 40
- shears: int32 [4, 16, 2], P('view'), may hold values from -40 to 40, as said below
- taps: bfloat16 [4, 16, 4], P('view'), may hold values from 0 to 1, as said below
Outputs:
- volume: float32 [64, 16, 256, 256], P('tile')
- residual: float32 [4, 64, 256, 256], P('view', 'tile')
The draws below stay inside these ranges and needn't reach their ends.
Inputs may be any that keep to these rules, and one draw needn't show every extreme that they name: In every draw some view has shears 40 and -40 along both x and y. `taps`: the two weights along x, and the two along y, each sum to one up to rounding.
All inputs are finite; a program needn't handle non-finite values.
Results may differ from the reference program's by a relative error of at most 0.007.
Values may be sent and summed in bfloat16 or wider, within the bound.
A program may use at most 64 MiB of HBM per device.

```python
import jax
import jax.numpy as jnp
from jax import lax

TX = 256
TY = 256
PLANES = 16
SHEAR = 40
GRID_Y = 8
ITERS = 2
TILES = 64
VIEWS = 4
N_TILE = 64


def draw_measured(key, part):
    key = jax.random.fold_in(key, 11)
    key_base = jax.random.fold_in(key, 0)
    tile_pos = jnp.arange(TILES, dtype=jnp.float32) / max(TILES - 1, 1)
    view_pos = jnp.arange(VIEWS, dtype=jnp.float32) / max(VIEWS - 1, 1)
    values = jax.random.normal(key_base, (VIEWS, TILES, TX, TY), jnp.float32)
    growth = (1.0 + 2.0 * tile_pos)[None, :, None, None] * (1.0 + view_pos)[:, None, None, None]
    return jnp.clip(values * growth, -40.0, 40.0)


def draw_shears(key, part):
    key = jax.random.fold_in(key, 5)
    key_vals, key_pick = jax.random.split(key, 2)
    values = jax.random.randint(key_vals, (VIEWS, PLANES, 2), -SHEAR, SHEAR + 1, jnp.int32)
    chosen = jax.random.randint(key_pick, (), 0, VIEWS, jnp.int32)
    values = values.at[chosen, 0, :].set(SHEAR)
    values = values.at[chosen, 1, :].set(-SHEAR)
    return values


def draw_taps(key, part):
    key = jax.random.fold_in(key, 7)
    fraction = jax.random.uniform(key, (VIEWS, PLANES, 2), jnp.float32, 0.1, 0.9)
    return jnp.stack([1.0 - fraction[:, :, 0], fraction[:, :, 0], 1.0 - fraction[:, :, 1], fraction[:, :, 1]], axis=-1).astype(jnp.bfloat16)


def setup_inputs(seed: int = 0) -> dict:
    streams_of = jax.random.split(jax.random.key(seed), 4)
    measured = draw_measured(jax.random.fold_in(streams_of[3], 71), 0)
    shears = draw_shears(jax.random.fold_in(streams_of[3], 71), 0)
    taps = draw_taps(jax.random.fold_in(streams_of[3], 71), 0)
    return {"measured": measured, "shears": shears, "taps": taps}


def volume_to_grid(blocks):
    rows = N_TILE // GRID_Y
    shaped = blocks.reshape(rows, GRID_Y, PLANES, TX, TY)
    return shaped.transpose(2, 0, 3, 1, 4).reshape(PLANES, rows * TX, GRID_Y * TY)


def volume_to_tiles(grid):
    rows = N_TILE // GRID_Y
    shaped = grid.reshape(PLANES, rows, TX, GRID_Y, TY)
    return shaped.transpose(1, 3, 0, 2, 4).reshape(N_TILE, PLANES, TX, TY)


def images_to_grid(blocks):
    rows = N_TILE // GRID_Y
    count = blocks.shape[0]
    shaped = blocks.reshape(count, rows, GRID_Y, TX, TY)
    return shaped.transpose(0, 1, 3, 2, 4).reshape(count, rows * TX, GRID_Y * TY)


def images_to_tiles(grid):
    rows = N_TILE // GRID_Y
    count = grid.shape[0]
    shaped = grid.reshape(count, rows, TX, GRID_Y, TY)
    return shaped.transpose(0, 1, 3, 2, 4).reshape(count, N_TILE, TX, TY)


def project_all(grid, shears, taps):
    margin = SHEAR + 1
    rows_x, rows_y = grid.shape[1], grid.shape[2]
    padded = jnp.pad(grid, ((0, 0), (margin, margin), (margin, margin)))
    tap_values = taps.astype(jnp.float32)

    def one_view(inputs):
        shear, weights_all = inputs

        def one_plane(summed, plane_inputs):
            planes, shift_x, shift_y, weights = plane_inputs
            start_x = (margin - shift_x).astype(jnp.int32)
            upper = lax.dynamic_slice_in_dim(planes, start_x, rows_x, 0).astype(jnp.float32)
            lower = lax.dynamic_slice_in_dim(planes, start_x + 1, rows_x, 0).astype(jnp.float32)
            partial_rows = weights[0] * upper + weights[1] * lower
            partial_rows = lax.optimization_barrier(partial_rows.astype(jnp.bfloat16)).astype(jnp.float32)
            start_y = (margin - shift_y).astype(jnp.int32)
            before = lax.dynamic_slice_in_dim(partial_rows, start_y, rows_y, 1)
            after = lax.dynamic_slice_in_dim(partial_rows, start_y + 1, rows_y, 1)
            return summed + weights[2] * before + weights[3] * after, None

        summed, _ = lax.scan(one_plane, jnp.zeros((rows_x, rows_y), jnp.float32),
                             (padded, shear[:, 0], shear[:, 1], weights_all))
        return summed * (PLANES ** -0.5)

    return lax.map(one_view, (shears, tap_values))


def back_all(images, shears, taps):
    margin = SHEAR + 1
    rows_x, rows_y = images.shape[1], images.shape[2]
    padded = jnp.pad(images, ((0, 0), (margin, margin), (margin, margin)))
    tap_values = taps.astype(jnp.float32)

    def one_view(summed, inputs):
        picture, shear, weights_all = inputs

        def one_plane(plane_inputs):
            shift_x, shift_y, weights = plane_inputs
            start_x = (margin + shift_x).astype(jnp.int32)
            upper = lax.dynamic_slice_in_dim(picture, start_x, rows_x, 0).astype(jnp.float32)
            lower = lax.dynamic_slice_in_dim(picture, start_x - 1, rows_x, 0).astype(jnp.float32)
            partial_rows = weights[0] * upper + weights[1] * lower
            partial_rows = lax.optimization_barrier(partial_rows.astype(jnp.bfloat16)).astype(jnp.float32)
            start_y = (margin + shift_y).astype(jnp.int32)
            before = lax.dynamic_slice_in_dim(partial_rows, start_y, rows_y, 1)
            after = lax.dynamic_slice_in_dim(partial_rows, start_y - 1, rows_y, 1)
            return weights[2] * before + weights[3] * after

        planes = lax.map(one_plane, (shear[:, 0], shear[:, 1], weights_all))
        return summed + planes, None

    summed, _ = lax.scan(one_view, jnp.zeros((PLANES, rows_x, rows_y), jnp.float32),
                         (padded, shears, tap_values))
    return summed * (PLANES ** -0.5)


def reference(measured, shears, taps):
    tiny = 1e-6
    residual = images_to_grid(measured)
    gradient = back_all(residual.astype(jnp.bfloat16), shears, taps)
    direction = gradient
    grad_norm = jnp.sum(gradient * gradient)
    volume = jnp.zeros_like(gradient)
    for rounds in range(ITERS):
        images = project_all(direction.astype(jnp.bfloat16), shears, taps)
        step_size = grad_norm / (jnp.sum(images * images) + tiny)
        volume = volume + step_size * direction
        residual = residual - step_size * images
        if rounds + 1 < ITERS:
            gradient = back_all(residual.astype(jnp.bfloat16), shears, taps)
            new_norm = jnp.sum(gradient * gradient)
            direction = gradient + (new_norm / (grad_norm + tiny)) * direction
            grad_norm = new_norm
    return volume_to_tiles(volume), images_to_tiles(residual)
```

```python
import functools

import jax
import jax.numpy as jnp
from jax import lax
from jax.experimental import pallas as pl
from jax.experimental.pallas import tpu as pltpu
from jax.sharding import PartitionSpec as P

PLANES = 16
VIEWS = 4
GRID_Y = 8
TX = 256
TY = 256
HX = 96
HY = 128
RX = TX + 2 * HX
RY = TY + 2 * HY
VX = 48
VROWS = RX - 2 * VX
WINDOW = 288
T_ROWS = 384
BACK_WINDOW = 272
FAR = 1 << 20
TINY = 1e-6
MESH = pl.DeviceIdType.MESH

X_SEMS = 6
Z_BASE = X_SEMS
Y_BASE = Z_BASE + 2 * VIEWS
N_SEMS = Y_BASE + 8 * VIEWS

PARTS = {"a": (HX, TX // 2), "b": (HX + TX // 2, TX // 2), "top": (0, HX), "bottom": (HX + TX, HX)}
PART_ID = {"a": 0, "b": 1, "top": 2, "bottom": 3}


def ring(index, step, size):
    return lax.rem(index + (step + size), size)


def solve_kernel(
    grid_x,
    meas_ref, sh_ref, tp_ref,
    yext_ref, res_ref, sh_s, tp_s,
    e_refs, f_refs, r_refs, y_ref, x_ref, t_refs, q_ref, h_ref,
    sh_v, tp_v, ra_ref, rb_ref, rc_ref,
    send_sems, recv_sems, p_send, p_recv, p_local, a_send, a_recv,
):
    tile = lax.axis_index("tile")
    view = lax.axis_index("view")
    gx = tile // GRID_Y
    gy = lax.rem(tile, GRID_Y)

    def at(row, col, vw):
        return (row * GRID_Y + col, vw)

    def to_view(step):
        return at(gx, gy, ring(view, step, VIEWS))

    def to_row(step):
        return at(ring(gx, step, grid_x), gy, view)

    def to_col(step):
        return at(gx, ring(gy, step, GRID_Y), view)

    partners = (
        [to_view(s) for s in range(1, VIEWS)]
        + [to_row(s) for s in range(1, grid_x)]
        + [to_col(s) for s in range(1, GRID_Y)]
    )
    barrier = pltpu.get_barrier_semaphore()
    for partner in partners:
        pl.semaphore_signal(barrier, inc=1, device_id=partner, device_id_type=MESH)

    e_refs[0][pl.ds(HX, TX), pl.ds(HY, TY)] = meas_ref[0, 0].astype(jnp.bfloat16)
    sh_v[0] = jnp.zeros((PLANES, 128), jnp.int32)
    sh_v[0, :, 0:2] = sh_ref[0]
    tp_v[0] = jnp.zeros((PLANES, 128), jnp.float32)
    tp_v[0, :, 0:4] = tp_ref[0].astype(jnp.float32)

    pl.semaphore_wait(barrier, len(partners))

    parameter_copies = []
    for step in range(1, VIEWS):
        slot = VIEWS - step
        for which, ref in ((0, sh_v), (1, tp_v)):
            copy = pltpu.make_async_remote_copy(
                src_ref=ref.at[0], dst_ref=ref.at[slot],
                send_sem=p_send.at[which, slot], recv_sem=p_recv.at[which, slot],
                device_id=to_view(step), device_id_type=MESH,
            )
            copy.start()
            parameter_copies.append(copy)

    class Exchange:
        def __init__(self, bufs, which):
            self.bufs, self.which, self.copies = bufs, which, {}

        def send(self, key, sem, src, dst, device):
            copy = pltpu.make_async_remote_copy(
                src_ref=src, dst_ref=dst,
                send_sem=send_sems.at[self.which, sem], recv_sem=recv_sems.at[self.which, sem],
                device_id=device, device_id_type=MESH,
            )
            copy.start()
            self.copies[key] = copy

        def region(self, slot, rows, cols):
            return self.bufs[slot].at[pl.ds(*rows), pl.ds(*cols)]

        def along_view(self, src_slot, dst_slot, part, sem, step):
            rows = PARTS[part]
            self.send(
                ("x", dst_slot, part), sem,
                self.region(src_slot, rows, (HY, TY)), self.region(dst_slot, rows, (HY, TY)),
                to_view(step),
            )

        def begin(self):
            self.along_view(0, 3, "a", 0, 1)
            self.along_view(0, 1, "b", 1, -1)
            self.along_view(0, 3, "b", 2, 1)
            self.along_view(0, 1, "a", 3, -1)
            self.spread(0, "a")
            self.spread(0, "b")

        def columns(self, slot, part):
            rows = PARTS[part]
            sem = Y_BASE + 8 * slot + 2 * PART_ID[part]
            self.send(
                ("y", slot, part, 0), sem,
                self.region(slot, rows, (HY, HY)), self.region(slot, rows, (HY + TY, HY)), to_col(-1),
            )
            self.send(
                ("y", slot, part, 1), sem + 1,
                self.region(slot, rows, (TY, HY)), self.region(slot, rows, (0, HY)), to_col(1),
            )

        def spread(self, slot, part):
            if part == "a":
                self.send(
                    ("z", slot, "bottom"), Z_BASE + 2 * slot,
                    self.region(slot, (HX, HX), (HY, TY)),
                    self.region(slot, (HX + TX, HX), (HY, TY)), to_row(-1),
                )
            else:
                self.send(
                    ("z", slot, "top"), Z_BASE + 2 * slot + 1,
                    self.region(slot, (TX, HX), (HY, TY)),
                    self.region(slot, (0, HX), (HY, TY)), to_row(1),
                )
            self.columns(slot, part)

        def arrive(self, slot, part):
            self.copies["x", slot, part].wait_recv()
            if slot == 3 and part == "a":
                self.along_view(3, 2, "a", 4, 1)
            if slot == 1 and part == "b":
                self.along_view(1, 2, "b", 5, -1)
            self.spread(slot, part)

        def corners(self, slot):
            for part, edge in (("top", 0), ("bottom", grid_x - 1)):
                self.copies["z", slot, part].wait_recv()

                @pl.when(gx == edge)
                def _():
                    start, size = PARTS[part]
                    self.bufs[slot][pl.ds(start, size), pl.ds(HY, TY)] = jnp.zeros((size, TY), jnp.bfloat16)

                self.columns(slot, part)

        def complete(self, slot):
            for part in PARTS:
                for side in (0, 1):
                    self.copies["y", slot, part, side].wait_recv()
            for side, edge in ((0, 0), (HY + TY, GRID_Y - 1)):
                @pl.when(gy == edge)
                def _():
                    self.bufs[slot][:, pl.ds(side, HY)] = jnp.zeros((RX, HY), jnp.bfloat16)

        def finish(self):
            for copy in self.copies.values():
                copy.wait_send()

    first = Exchange(e_refs, 0)
    first.begin()

    def clear(pair, carry):
        y_ref[pair, 0:32, 0:128] = jnp.zeros((32, 128), jnp.bfloat16)
        y_ref[pair, 352:512, 0:128] = jnp.zeros((160, 128), jnp.bfloat16)
        y_ref[pair, 0:160, 128:256] = jnp.zeros((160, 128), jnp.bfloat16)
        y_ref[pair, 480:512, 128:256] = jnp.zeros((32, 128), jnp.bfloat16)
        x_ref[pair, 0:96, 128:256] = jnp.zeros((96, 128), jnp.bfloat16)
        x_ref[pair, 128:224, 128:256] = jnp.zeros((96, 128), jnp.bfloat16)
        return carry

    lax.fori_loop(0, VIEWS * PLANES, clear, 0)
    for t_ref in t_refs:
        t_ref[WINDOW:, :] = jnp.zeros((T_ROWS - WINDOW, TY), jnp.bfloat16)

    for copy in parameter_copies:
        copy.wait_recv()
    local = [pltpu.make_async_copy(sh_v, sh_s, p_local.at[0]), pltpu.make_async_copy(tp_v, tp_s, p_local.at[1])]
    for copy in local:
        copy.start()
    for copy in local:
        copy.wait()

    column_low = jnp.where(gy == 0, 0, -FAR)
    column_high = jnp.where(gy == GRID_Y - 1, TY, FAR)
    row_low = jnp.where(gx == 0, 0, -FAR)
    row_high = jnp.where(gx == grid_x - 1, TX, FAR)

    def build(slot):
        def one(z, carry):
            shear = sh_s[0, z, 1]
            d = sh_s[slot, z, 1] - shear
            a0, a1 = tp_s[0, z, 2], tp_s[0, z, 3]
            b0, b1 = tp_s[slot, z, 2], tp_s[slot, z, 3]
            col = lax.broadcasted_iota(jnp.int32, (1, 128), 1)
            distance = (
                lax.broadcasted_iota(jnp.int32, (320, 128), 0)
                - lax.broadcasted_iota(jnp.int32, (320, 128), 1)
                + (32 - HY)
            )
            hit = [distance == d + k for k in (-1, 0, 1)]
            low, high = shear + column_low, shear + column_high
            for tile_start, in0, in1 in (
                (0, col >= low, col >= low - 1),
                (128, col + 128 < high, col + 128 < high - 1),
            ):
                before = jnp.where(in0, a0 * b1, 0.0)
                middle = jnp.where(in0, a0 * b0, 0.0) + jnp.where(in1, a1 * b1, 0.0)
                after = jnp.where(in1, a1 * b0, 0.0)
                value = jnp.where(hit[0], before, jnp.where(hit[1], middle, jnp.where(hit[2], after, 0.0)))
                y_ref[slot * PLANES + z, pl.ds(32 + tile_start, 320), pl.ds(tile_start, 128)] = value.astype(
                    jnp.bfloat16
                )

            shear = sh_s[0, z, 0]
            first_row = HX - 1 + sh_s[slot, z, 0] - shear
            m = first_row - lax.shift_left(lax.shift_right_logical(first_row, 4), 4)
            a0, a1 = tp_s[0, z, 0] * (1.0 / PLANES), tp_s[0, z, 1] * (1.0 / PLANES)
            b0, b1 = tp_s[slot, z, 0], tp_s[slot, z, 1]
            low, high = shear + row_low, shear + row_high
            for row_start, size, col_start in ((0, 128, 0), (96, 32, 128)):
                row = lax.broadcasted_iota(jnp.int32, (size, 128), 0) + row_start
                distance = lax.broadcasted_iota(jnp.int32, (size, 128), 1) - row + col_start
                hit = [distance == m + k for k in (0, 1, 2)]
                for half, in0, in1 in (
                    (0, row >= low, row >= low - 1),
                    (128, row + 128 < high, row + 128 < high - 1),
                ):
                    before = jnp.where(in0, a0 * b1, 0.0)
                    middle = jnp.where(in0, a0 * b0, 0.0) + jnp.where(in1, a1 * b1, 0.0)
                    after = jnp.where(in1, a1 * b0, 0.0)
                    value = jnp.where(hit[0], before, jnp.where(hit[1], middle, jnp.where(hit[2], after, 0.0)))
                    x_ref[slot * PLANES + z, pl.ds(half + row_start, size), pl.ds(col_start, 128)] = value.astype(
                        jnp.bfloat16
                    )
            return carry

        lax.fori_loop(0, PLANES, one, 0)

    def apply(src_ref, out_ref, slot):
        def group(g, carry):
            top, bottom = out_ref[0:128, :], out_ref[128:256, :]
            for u, t_ref in enumerate(t_refs):
                z = len(t_refs) * g + u
                pair = slot * PLANES + z
                first_row = HX - 1 + sh_s[slot, z, 0] - sh_s[0, z, 0]
                start = lax.shift_right_logical(first_row, 4) * 16
                t_ref[0:WINDOW, :] = jnp.dot(
                    src_ref[pl.ds(start, WINDOW), :], y_ref[pair], preferred_element_type=jnp.float32
                ).astype(jnp.bfloat16)
                top = top + jnp.dot(x_ref[pair, 0:128, :], t_ref[0:256, :], preferred_element_type=jnp.float32)
                bottom = bottom + jnp.dot(
                    x_ref[pair, 128:256, :], t_ref[128:384, :], preferred_element_type=jnp.float32
                )
            out_ref[0:128, :], out_ref[128:256, :] = top, bottom
            return carry

        lax.fori_loop(0, PLANES // len(t_refs), group, 0)

    def lanes(x):
        s = jnp.sum(x, axis=0, keepdims=True)
        return s[:, 0:128] + s[:, 128:256]

    class Sum:
        def __init__(self, which, rows):
            self.which = which
            self.stages = (
                (ra_ref, view, VIEWS, to_view, 0),
                (rb_ref, gy, GRID_Y, to_col, VIEWS),
                (rc_ref, gx, grid_x, to_row, VIEWS + GRID_Y),
            )
            self.copies = []
            pad = jnp.zeros((8 - len(rows), 128), jnp.float32)
            self.value = jnp.concatenate(list(rows) + [pad], axis=0)

        def send(self, stage):
            ref, me, size, to, base = self.stages[stage]
            ref[self.which, me] = self.value
            self.current = []
            for step in range(1, size):
                copy = pltpu.make_async_remote_copy(
                    src_ref=ref.at[self.which, me], dst_ref=ref.at[self.which, me],
                    send_sem=a_send.at[self.which, base + step], recv_sem=a_recv.at[self.which, base + step],
                    device_id=to(step), device_id_type=MESH,
                )
                copy.start()
                self.current.append(copy)
            self.copies += self.current

        def receive(self, stage):
            ref, me, size, to, base = self.stages[stage]
            for copy in self.current:
                copy.wait_recv()
            total = ref[self.which, 0]
            for i in range(1, size):
                total = total + ref[self.which, i]
            self.value = total

        def row(self, i):
            return jnp.sum(self.value[i : i + 1, :], axis=1, keepdims=True)

        def finish(self):
            for copy in self.copies:
                copy.wait_send()

    q_ref[...] = jnp.zeros((TX, TY), jnp.float32)
    h_ref[...] = jnp.zeros((TX, TY), jnp.float32)

    build(0)
    first.arrive(3, "a")
    first.arrive(1, "b")
    first.arrive(3, "b")
    first.arrive(1, "a")
    first.corners(0)
    build(3)
    first.corners(3)
    first.corners(1)
    first.arrive(2, "a")
    first.arrive(2, "b")
    build(1)
    first.corners(2)
    build(2)
    for slot in (0, 3, 1, 2):
        first.complete(slot)
        apply(e_refs[slot], q_ref, slot)

    second = Exchange(f_refs, 1)
    f_refs[0][pl.ds(HX, TX), pl.ds(HY, TY)] = q_ref[...].astype(jnp.bfloat16)
    second.begin()
    q0 = q_ref[...]
    r0 = e_refs[0][pl.ds(HX, TX), pl.ds(HY, TY)].astype(jnp.float32)
    sums = Sum(0, [lanes(r0 * q0), lanes(q0 * q0)])
    sums.send(0)
    sums.receive(0)
    sums.send(1)
    second.arrive(3, "a")
    second.arrive(1, "b")
    second.arrive(3, "b")
    second.arrive(1, "a")
    second.corners(0)
    sums.receive(1)
    sums.send(2)
    second.corners(3)
    second.corners(1)
    second.arrive(2, "a")
    second.arrive(2, "b")
    sums.receive(2)
    gamma0, norm0 = sums.row(0), sums.row(1)
    alpha0 = gamma0 / (norm0 + TINY)
    second.corners(2)

    def update(slot):
        for start in range(0, RX, 64):
            rows = pl.ds(start, 64)
            r_refs[slot][rows, :] = (
                e_refs[slot][rows, :].astype(jnp.float32) - alpha0 * f_refs[slot][rows, :].astype(jnp.float32)
            ).astype(jnp.bfloat16)

    for slot in (0, 3, 1, 2):
        second.complete(slot)
        update(slot)
        apply(r_refs[slot], h_ref, slot)

    h1 = h_ref[...]
    q0 = q_ref[...]
    r1 = r_refs[0][pl.ds(HX, TX), pl.ds(HY, TY)].astype(jnp.float32)
    sums2 = Sum(1, [lanes(r1 * h1), lanes(h1 * h1), lanes(h1 * q0)])
    for stage in range(3):
        sums2.send(stage)
        sums2.receive(stage)
    gamma1 = sums2.row(0)
    beta = gamma1 / (gamma0 + TINY)
    norm1 = sums2.row(1) + 2.0 * beta * sums2.row(2) + beta * beta * norm0
    alpha1 = gamma1 / (norm1 + TINY)
    weight0 = alpha0 + alpha1 * beta

    q0 = q_ref[...]
    res_ref[0, 0] = meas_ref[0, 0] - alpha0 * q0 - alpha1 * (h_ref[...] + beta * q0)
    for slot in range(VIEWS):
        for start in range(0, VROWS, 32):
            rows = pl.ds(VX + start, 32)
            yext_ref[slot, pl.ds(start, 32), :] = (
                weight0 * e_refs[slot][rows, :].astype(jnp.float32)
                + alpha1 * r_refs[slot][rows, :].astype(jnp.float32)
            ).astype(jnp.bfloat16)

    for copy in parameter_copies:
        copy.wait_send()
    first.finish()
    second.finish()
    sums.finish()
    sums2.finish()


def volume_kernel(sh_s, tp_s, y_ref, res_in, vol_ref, res_out, b_ref, x_ref, t_ref):
    view = lax.axis_index("view")
    z = pl.program_id(0)

    @pl.when(z == 0)
    def _():
        b_ref[...] = jnp.zeros(b_ref.shape, jnp.bfloat16)
        x_ref[...] = jnp.zeros(x_ref.shape, jnp.bfloat16)
        t_ref[...] = jnp.zeros(t_ref.shape, jnp.bfloat16)
        res_out[...] = res_in[...]

    top = bottom = None
    for v in range(VIEWS):
        slot = lax.rem(v - view + VIEWS, VIEWS)
        d = sh_s[slot, z, 1]
        distance = (
            lax.broadcasted_iota(jnp.int32, (224, 128), 0)
            - lax.broadcasted_iota(jnp.int32, (224, 128), 1)
            + (80 - HY)
        )
        value = jnp.where(
            distance == d, tp_s[slot, z, 2], jnp.where(distance == d - 1, tp_s[slot, z, 3], 0.0)
        ).astype(jnp.bfloat16)
        b_ref[v, 80:304, 0:128] = value
        b_ref[v, 208:432, 128:256] = value
        first_row = HX - VX - 1 + sh_s[slot, z, 0]
        start = pl.multiple_of(lax.shift_left(lax.shift_right_logical(first_row, 4), 4), 16)
        m = first_row - start
        b0, b1 = tp_s[slot, z, 0] * (PLANES**-0.5), tp_s[slot, z, 1] * (PLANES**-0.5)
        for row_start, size, col_start in ((0, 128, 0), (96, 32, 128)):
            distance = (
                lax.broadcasted_iota(jnp.int32, (size, 128), 1)
                - lax.broadcasted_iota(jnp.int32, (size, 128), 0)
                + (col_start - row_start)
            )
            x_ref[v, pl.ds(row_start, size), pl.ds(col_start, 128)] = jnp.where(
                distance == m, b1, jnp.where(distance == m + 1, b0, 0.0)
            ).astype(jnp.bfloat16)
        t_ref[v, 0:BACK_WINDOW, :] = jnp.dot(
            y_ref[slot, pl.ds(start, BACK_WINDOW), :], b_ref[v], preferred_element_type=jnp.float32
        ).astype(jnp.bfloat16)
        upper = jnp.dot(x_ref[v], t_ref[v, 0:256, :], preferred_element_type=jnp.float32)
        lower = jnp.dot(x_ref[v], t_ref[v, 128:384, :], preferred_element_type=jnp.float32)
        top = upper if top is None else top + upper
        bottom = lower if bottom is None else bottom + lower
    vol_ref[0, 0, 0:128, :] = top
    vol_ref[0, 0, 128:256, :] = bottom


def local(grid_x, measured, shears, taps):
    f32, bf16 = jnp.float32, jnp.bfloat16
    vmem = pl.BlockSpec(memory_space=pltpu.VMEM)
    smem = pl.BlockSpec(memory_space=pltpu.SMEM)
    yext, partial, sh_all, tp_all = pl.pallas_call(
        functools.partial(solve_kernel, grid_x),
        name="solve",
        out_shape=(
            jax.ShapeDtypeStruct((VIEWS, VROWS, RY), bf16),
            jax.ShapeDtypeStruct((1, 1, TX, TY), f32),
            jax.ShapeDtypeStruct((VIEWS, PLANES, 128), jnp.int32),
            jax.ShapeDtypeStruct((VIEWS, PLANES, 128), f32),
        ),
        in_specs=[vmem, vmem, vmem],
        out_specs=(vmem, vmem, smem, smem),
        scratch_shapes=[
            [pltpu.VMEM((RX, RY), bf16)] * VIEWS,
            [pltpu.VMEM((RX, RY), bf16)] * VIEWS,
            [pltpu.VMEM((RX, RY), bf16)] * VIEWS,
            pltpu.VMEM((VIEWS * PLANES, RY, TY), bf16),
            pltpu.VMEM((VIEWS * PLANES, TX, 256), bf16),
            [pltpu.VMEM((T_ROWS, TY), bf16)] * 4,
            pltpu.VMEM((TX, TY), f32),
            pltpu.VMEM((TX, TY), f32),
            pltpu.VMEM((VIEWS, PLANES, 128), jnp.int32),
            pltpu.VMEM((VIEWS, PLANES, 128), f32),
            pltpu.VMEM((2, VIEWS, 8, 128), f32),
            pltpu.VMEM((2, GRID_Y, 8, 128), f32),
            pltpu.VMEM((2, grid_x, 8, 128), f32),
            pltpu.SemaphoreType.DMA((2, N_SEMS)),
            pltpu.SemaphoreType.DMA((2, N_SEMS)),
            pltpu.SemaphoreType.DMA((2, VIEWS)),
            pltpu.SemaphoreType.DMA((2, VIEWS)),
            pltpu.SemaphoreType.DMA((2,)),
            pltpu.SemaphoreType.DMA((2, VIEWS + GRID_Y + grid_x)),
            pltpu.SemaphoreType.DMA((2, VIEWS + GRID_Y + grid_x)),
        ],
        compiler_params=pltpu.CompilerParams(
            collective_id=0, has_side_effects=True, vmem_limit_bytes=48 * 1024 * 1024
        ),
    )(measured, shears, taps)
    volume, residual = pl.pallas_call(
        volume_kernel,
        name="back_project",
        grid=(PLANES,),
        out_shape=(
            jax.ShapeDtypeStruct((1, PLANES, TX, TY), f32),
            jax.ShapeDtypeStruct((1, 1, TX, TY), f32),
        ),
        in_specs=[smem, smem, vmem, vmem],
        out_specs=(
            pl.BlockSpec((1, 1, TX, TY), lambda z: (0, z, 0, 0)),
            pl.BlockSpec((1, 1, TX, TY), lambda z: (0, 0, 0, 0)),
        ),
        scratch_shapes=[
            pltpu.VMEM((VIEWS, RY, TY), bf16),
            pltpu.VMEM((VIEWS, 128, 256), bf16),
            pltpu.VMEM((VIEWS, T_ROWS, TY), bf16),
        ],
        compiler_params=pltpu.CompilerParams(vmem_limit_bytes=32 * 1024 * 1024),
    )(sh_all, tp_all, yext, partial)
    return volume, residual


def solution(mesh):
    placed = (P("view", "tile", None, None), P("view", None, None), P("view", None, None))
    return jax.shard_map(
        functools.partial(local, mesh.shape["tile"] // GRID_Y),
        mesh=mesh,
        in_specs=placed,
        out_specs=(P("tile", None, None, None), P("view", "tile", None, None)),
        check_vma=False,
    )
```

```python
import functools

import jax
import jax.numpy as jnp
from jax import lax
from jax.experimental import pallas as pl
from jax.experimental.pallas import tpu as pltpu
from jax.sharding import PartitionSpec as P

PLANES = 16
VIEWS = 4
GRID_Y = 8
TX = 256
TY = 256
HX = 96
HY = 128
RX = TX + 2 * HX
RY = TY + 2 * HY
VX = 48
VROWS = RX - VX - 32
WINDOW = 288
BACK_WINDOW = 288
STRIP = 160
BACK_PLANES = 4
GROUP = 4
BAND = (
    (0, 0, 0, 128), (0, 1, 96, 32), (1, 1, 0, 96), (1, 2, 64, 64),
    (2, 2, 0, 64), (2, 3, 32, 96), (3, 3, 0, 32), (3, 4, 0, 128),
)
FAR = 1 << 20
TINY = 1e-6
MESH = pl.DeviceIdType.MESH

X_SEMS = 6
Z_BASE = X_SEMS
Y_BASE = Z_BASE + 2 * VIEWS
N_SEMS = Y_BASE + 8 * VIEWS

PARTS = {"a": (HX, TX // 2), "b": (HX + TX // 2, TX // 2), "top": (0, HX), "bottom": (HX + TX, HX)}
PART_ID = {"a": 0, "b": 1, "top": 2, "bottom": 3}


def ring(index, step, size):
    return lax.rem(index + (step + size), size)


def solve_kernel(
    grid_x,
    meas_ref, sh_ref, tp_ref,
    yext_ref, res_ref, sh_s, tp_s,
    e_refs, f_refs, r_refs, y_ref, x_ref, upper_ref, lower_ref, q_ref, h_ref,
    sh_v, tp_v, ra_ref, rb_ref, rc_ref,
    send_sems, recv_sems, p_send, p_recv, p_local, a_send, a_recv,
):
    tile = lax.axis_index("tile")
    view = lax.axis_index("view")
    gx = tile // GRID_Y
    gy = lax.rem(tile, GRID_Y)

    def at(row, col, vw):
        return (row * GRID_Y + col, vw)

    def to_view(step):
        return at(gx, gy, ring(view, step, VIEWS))

    def to_row(step):
        return at(ring(gx, step, grid_x), gy, view)

    def to_col(step):
        return at(gx, ring(gy, step, GRID_Y), view)

    partners = (
        [to_view(s) for s in range(1, VIEWS)]
        + [to_row(s) for s in range(1, grid_x)]
        + [to_col(s) for s in range(1, GRID_Y)]
    )
    barrier = pltpu.get_barrier_semaphore()
    for partner in partners:
        pl.semaphore_signal(barrier, inc=1, device_id=partner, device_id_type=MESH)

    e_refs[0][pl.ds(HX, TX), pl.ds(HY, TY)] = meas_ref[0, 0].astype(jnp.bfloat16)
    sh_v[0] = jnp.zeros((PLANES, 128), jnp.int32)
    sh_v[0, :, 0:2] = sh_ref[0]
    tp_v[0] = jnp.zeros((PLANES, 128), jnp.float32)
    tp_v[0, :, 0:4] = tp_ref[0].astype(jnp.float32)

    pl.semaphore_wait(barrier, len(partners))

    parameter_copies = []
    for step in range(1, VIEWS):
        slot = VIEWS - step
        for which, ref in ((0, sh_v), (1, tp_v)):
            copy = pltpu.make_async_remote_copy(
                src_ref=ref.at[0], dst_ref=ref.at[slot],
                send_sem=p_send.at[which, slot], recv_sem=p_recv.at[which, slot],
                device_id=to_view(step), device_id_type=MESH,
            )
            copy.start()
            parameter_copies.append(copy)

    class Exchange:
        def __init__(self, bufs, which):
            self.bufs, self.which, self.copies = bufs, which, {}

        def send(self, key, sem, src, dst, device):
            copy = pltpu.make_async_remote_copy(
                src_ref=src, dst_ref=dst,
                send_sem=send_sems.at[self.which, sem], recv_sem=recv_sems.at[self.which, sem],
                device_id=device, device_id_type=MESH,
            )
            copy.start()
            self.copies[key] = copy

        def region(self, slot, rows, cols):
            return self.bufs[slot].at[pl.ds(*rows), pl.ds(*cols)]

        def along_view(self, src_slot, dst_slot, part, sem, step):
            rows = PARTS[part]
            self.send(
                ("x", dst_slot, part), sem,
                self.region(src_slot, rows, (HY, TY)), self.region(dst_slot, rows, (HY, TY)),
                to_view(step),
            )

        def begin(self):
            self.along_view(0, 3, "a", 0, 1)
            self.along_view(0, 1, "b", 1, -1)
            self.along_view(0, 3, "b", 2, 1)
            self.along_view(0, 1, "a", 3, -1)
            self.spread(0, "a")
            self.spread(0, "b")

        def columns(self, slot, part):
            rows = PARTS[part]
            sem = Y_BASE + 8 * slot + 2 * PART_ID[part]
            self.send(
                ("y", slot, part, 0), sem,
                self.region(slot, rows, (HY, HY)), self.region(slot, rows, (HY + TY, HY)), to_col(-1),
            )
            self.send(
                ("y", slot, part, 1), sem + 1,
                self.region(slot, rows, (TY, HY)), self.region(slot, rows, (0, HY)), to_col(1),
            )

        def spread(self, slot, part):
            if part == "a":
                self.send(
                    ("z", slot, "bottom"), Z_BASE + 2 * slot,
                    self.region(slot, (HX, HX), (HY, TY)),
                    self.region(slot, (HX + TX, HX), (HY, TY)), to_row(-1),
                )
            else:
                self.send(
                    ("z", slot, "top"), Z_BASE + 2 * slot + 1,
                    self.region(slot, (TX, HX), (HY, TY)),
                    self.region(slot, (0, HX), (HY, TY)), to_row(1),
                )
            self.columns(slot, part)

        def arrive(self, slot, part):
            self.copies["x", slot, part].wait_recv()
            if slot == 3 and part == "a":
                self.along_view(3, 2, "a", 4, 1)
            if slot == 1 and part == "b":
                self.along_view(1, 2, "b", 5, -1)
            self.spread(slot, part)

        def corners(self, slot):
            for part, edge in (("top", 0), ("bottom", grid_x - 1)):
                self.copies["z", slot, part].wait_recv()

                @pl.when(gx == edge)
                def _():
                    start, size = PARTS[part]
                    self.bufs[slot][pl.ds(start, size), pl.ds(HY, TY)] = jnp.zeros((size, TY), jnp.bfloat16)

                self.columns(slot, part)

        def complete(self, slot):
            for part in PARTS:
                for side in (0, 1):
                    self.copies["y", slot, part, side].wait_recv()
            for side, edge in ((0, 0), (HY + TY, GRID_Y - 1)):
                @pl.when(gy == edge)
                def _():
                    self.bufs[slot][:, pl.ds(side, HY)] = jnp.zeros((RX, HY), jnp.bfloat16)

        def finish(self):
            for copy in self.copies.values():
                copy.wait_send()

    first = Exchange(e_refs, 0)
    first.begin()

    def clear(pair, carry):
        y_ref[pair, 0:32, 0:128] = jnp.zeros((32, 128), jnp.bfloat16)
        y_ref[pair, 352:512, 0:128] = jnp.zeros((160, 128), jnp.bfloat16)
        y_ref[pair, 0:160, 128:256] = jnp.zeros((160, 128), jnp.bfloat16)
        y_ref[pair, 480:512, 128:256] = jnp.zeros((32, 128), jnp.bfloat16)
        return carry

    lax.fori_loop(0, VIEWS * PLANES, clear, 0)

    for copy in parameter_copies:
        copy.wait_recv()
    local = [pltpu.make_async_copy(sh_v, sh_s, p_local.at[0]), pltpu.make_async_copy(tp_v, tp_s, p_local.at[1])]
    for copy in local:
        copy.start()
    for copy in local:
        copy.wait()

    column_low = jnp.where(gy == 0, 0, -FAR)
    column_high = jnp.where(gy == GRID_Y - 1, TY, FAR)
    row_low = jnp.where(gx == 0, 0, -FAR)
    row_high = jnp.where(gx == grid_x - 1, TX, FAR)

    def build(slot):
        def one(z, carry):
            shear = sh_s[0, z, 1]
            d = sh_s[slot, z, 1] - shear
            a0, a1 = tp_s[0, z, 2], tp_s[0, z, 3]
            b0, b1 = tp_s[slot, z, 2], tp_s[slot, z, 3]
            col = lax.broadcasted_iota(jnp.int32, (1, 128), 1)
            distance = (
                lax.broadcasted_iota(jnp.int32, (320, 128), 0)
                - lax.broadcasted_iota(jnp.int32, (320, 128), 1)
                + (32 - HY)
            )
            hit = [distance == d + k for k in (-1, 0, 1)]
            low, high = shear + column_low, shear + column_high
            for tile_start, in0, in1 in (
                (0, col >= low, col >= low - 1),
                (128, col + 128 < high, col + 128 < high - 1),
            ):
                before = jnp.where(in0, a0 * b1, 0.0)
                middle = jnp.where(in0, a0 * b0, 0.0) + jnp.where(in1, a1 * b1, 0.0)
                after = jnp.where(in1, a1 * b0, 0.0)
                value = jnp.where(hit[0], before, jnp.where(hit[1], middle, jnp.where(hit[2], after, 0.0)))
                y_ref[slot * PLANES + z, pl.ds(32 + tile_start, 320), pl.ds(tile_start, 128)] = value.astype(
                    jnp.bfloat16
                )
            return carry

        lax.fori_loop(0, PLANES, one, 0)

    def build_rows(slot):
        def one(g, carry):
            scalars = []
            for u in range(GROUP):
                z = GROUP * g + u
                shear = sh_s[0, z, 0]
                first_row = HX - 1 + sh_s[slot, z, 0] - shear
                m = first_row - lax.shift_right_logical(first_row, 4) * 16 + STRIP * u
                a0, a1 = tp_s[0, z, 0] * (1.0 / PLANES), tp_s[0, z, 1] * (1.0 / PLANES)
                b0, b1 = tp_s[slot, z, 0], tp_s[slot, z, 1]
                scalars.append((m, a0 * b1, a0 * b0, a1 * b1, a1 * b0, shear + row_low, shear + row_high))
            for u, block, row_start, size in BAND:
                m, am, az, bz, bp, low, high = scalars[u]
                row = lax.broadcasted_iota(jnp.int32, (size, 128), 0) + row_start
                distance = lax.broadcasted_iota(jnp.int32, (size, 128), 1) - row + 128 * block
                hit = [distance == m + k for k in (0, 1, 2)]
                for half, in0, in1 in (
                    (0, row >= low, row >= low - 1),
                    (1, row + 128 < high, row + 128 < high - 1),
                ):
                    before = jnp.where(in0, am, 0.0)
                    middle = jnp.where(in0, az, 0.0) + jnp.where(in1, bz, 0.0)
                    after = jnp.where(in1, bp, 0.0)
                    value = jnp.where(hit[0], before, jnp.where(hit[1], middle, jnp.where(hit[2], after, 0.0)))
                    x_ref[slot, half, g, pl.ds(row_start, size), pl.ds(128 * block, 128)] = value.astype(jnp.bfloat16)
            return carry

        lax.fori_loop(0, PLANES // GROUP, one, 0)

    def apply(src_ref, out_ref, slot):
        for z in range(PLANES):
            first_row = HX - 1 + sh_s[slot, z, 0] - sh_s[0, z, 0]
            start = lax.shift_right_logical(first_row, 4) * 16
            t = jnp.dot(
                src_ref[pl.ds(start, WINDOW), :], y_ref[slot * PLANES + z], preferred_element_type=jnp.float32
            ).astype(jnp.bfloat16)
            upper_ref[pl.ds(STRIP * z, STRIP), :] = t[0:STRIP]
            lower_ref[pl.ds(STRIP * z, STRIP), :] = t[128 : 128 + STRIP]
        for half, t_ref in enumerate((upper_ref, lower_ref)):
            total = out_ref[pl.ds(128 * half, 128), :]
            for g in range(PLANES // GROUP):
                total = total + jnp.dot(
                    x_ref[slot, half, g],
                    t_ref[pl.ds(GROUP * STRIP * g, GROUP * STRIP), :],
                    preferred_element_type=jnp.float32,
                )
            out_ref[pl.ds(128 * half, 128), :] = total

    def lanes(x):
        s = jnp.sum(x, axis=0, keepdims=True)
        return s[:, 0:128] + s[:, 128:256]

    class Sum:
        def __init__(self, which, rows):
            self.which = which
            self.stages = (
                (ra_ref, view, VIEWS, to_view, 0),
                (rb_ref, gy, GRID_Y, to_col, VIEWS),
                (rc_ref, gx, grid_x, to_row, VIEWS + GRID_Y),
            )
            self.copies = []
            pad = jnp.zeros((8 - len(rows), 128), jnp.float32)
            self.value = jnp.concatenate(list(rows) + [pad], axis=0)

        def send(self, stage):
            ref, me, size, to, base = self.stages[stage]
            ref[self.which, me] = self.value
            self.current = []
            for step in range(1, size):
                copy = pltpu.make_async_remote_copy(
                    src_ref=ref.at[self.which, me], dst_ref=ref.at[self.which, me],
                    send_sem=a_send.at[self.which, base + step], recv_sem=a_recv.at[self.which, base + step],
                    device_id=to(step), device_id_type=MESH,
                )
                copy.start()
                self.current.append(copy)
            self.copies += self.current

        def receive(self, stage):
            ref, me, size, to, base = self.stages[stage]
            for copy in self.current:
                copy.wait_recv()
            total = ref[self.which, 0]
            for i in range(1, size):
                total = total + ref[self.which, i]
            self.value = total

        def row(self, i):
            return jnp.sum(self.value[i : i + 1, :], axis=1, keepdims=True)

        def finish(self):
            for copy in self.copies:
                copy.wait_send()

    q_ref[...] = jnp.zeros((TX, TY), jnp.float32)
    h_ref[...] = jnp.zeros((TX, TY), jnp.float32)

    build(0)
    build_rows(0)
    first.arrive(3, "a")
    first.arrive(1, "b")
    first.arrive(3, "b")
    first.arrive(1, "a")
    first.corners(0)
    build(3)
    build_rows(3)
    first.corners(3)
    first.corners(1)
    first.arrive(2, "a")
    first.arrive(2, "b")
    build(1)
    build_rows(1)
    first.corners(2)
    build(2)
    build_rows(2)
    for slot in (0, 3, 1, 2):
        first.complete(slot)
        apply(e_refs[slot], q_ref, slot)

    second = Exchange(f_refs, 1)
    f_refs[0][pl.ds(HX, TX), pl.ds(HY, TY)] = q_ref[...].astype(jnp.bfloat16)
    second.begin()
    q0 = q_ref[...]
    r0 = e_refs[0][pl.ds(HX, TX), pl.ds(HY, TY)].astype(jnp.float32)
    sums = Sum(0, [lanes(r0 * q0), lanes(q0 * q0)])
    sums.send(0)
    sums.receive(0)
    sums.send(1)
    second.arrive(3, "a")
    second.arrive(1, "b")
    second.arrive(3, "b")
    second.arrive(1, "a")
    second.corners(0)
    sums.receive(1)
    sums.send(2)
    second.corners(3)
    second.corners(1)
    second.arrive(2, "a")
    second.arrive(2, "b")
    sums.receive(2)
    gamma0, norm0 = sums.row(0), sums.row(1)
    alpha0 = gamma0 / (norm0 + TINY)
    second.corners(2)

    def update(slot):
        for start in range(0, RX, 64):
            rows = pl.ds(start, 64)
            r_refs[slot][rows, :] = (
                e_refs[slot][rows, :].astype(jnp.float32) - alpha0 * f_refs[slot][rows, :].astype(jnp.float32)
            ).astype(jnp.bfloat16)

    for slot in (0, 3, 1, 2):
        second.complete(slot)
        update(slot)
        apply(r_refs[slot], h_ref, slot)

    h1 = h_ref[...]
    q0 = q_ref[...]
    r1 = r_refs[0][pl.ds(HX, TX), pl.ds(HY, TY)].astype(jnp.float32)
    sums2 = Sum(1, [lanes(r1 * h1), lanes(h1 * h1), lanes(h1 * q0)])
    for stage in range(3):
        sums2.send(stage)
        sums2.receive(stage)
    gamma1 = sums2.row(0)
    beta = gamma1 / (gamma0 + TINY)
    norm1 = sums2.row(1) + 2.0 * beta * sums2.row(2) + beta * beta * norm0
    alpha1 = gamma1 / (norm1 + TINY)
    weight0 = alpha0 + alpha1 * beta

    q0 = q_ref[...]
    res_ref[0, 0] = meas_ref[0, 0] - alpha0 * q0 - alpha1 * (h_ref[...] + beta * q0)
    for slot in range(VIEWS):
        for start in range(0, VROWS, 16):
            rows = pl.ds(VX + start, 16)
            yext_ref[slot, pl.ds(start, 16), :] = (
                weight0 * e_refs[slot][rows, :].astype(jnp.float32)
                + alpha1 * r_refs[slot][rows, :].astype(jnp.float32)
            ).astype(jnp.bfloat16)

    for copy in parameter_copies:
        copy.wait_send()
    first.finish()
    second.finish()
    sums.finish()
    sums2.finish()


def volume_kernel(sh_s, tp_s, y_ref, res_in, vol_ref, res_out, b_ref, x_ref, upper_ref, lower_ref):
    view = lax.axis_index("view")
    step = pl.program_id(0)

    @pl.when(step == 0)
    def _():
        b_ref[...] = jnp.zeros(b_ref.shape, jnp.bfloat16)
        res_out[...] = res_in[...]

    for p in range(BACK_PLANES):
        z = step * BACK_PLANES + p
        rows = []
        for v in range(VIEWS):
            slot = lax.rem(v - view + VIEWS, VIEWS)
            d = sh_s[slot, z, 1]
            distance = (
                lax.broadcasted_iota(jnp.int32, (224, 128), 0)
                - lax.broadcasted_iota(jnp.int32, (224, 128), 1)
                + (80 - HY)
            )
            value = jnp.where(
                distance == d, tp_s[slot, z, 2], jnp.where(distance == d - 1, tp_s[slot, z, 3], 0.0)
            ).astype(jnp.bfloat16)
            pair = p * VIEWS + v
            b_ref[pair, 80:304, 0:128] = value
            b_ref[pair, 208:432, 128:256] = value
            first_row = HX - VX - 1 + sh_s[slot, z, 0]
            start = lax.shift_right_logical(first_row, 4) * 16
            b0, b1 = tp_s[slot, z, 0] * (PLANES**-0.5), tp_s[slot, z, 1] * (PLANES**-0.5)
            rows.append((first_row - start + STRIP * v, b0, b1))
            t = jnp.dot(
                y_ref[slot, pl.ds(start, BACK_WINDOW), :], b_ref[pair], preferred_element_type=jnp.float32
            ).astype(jnp.bfloat16)
            upper_ref[p, pl.ds(STRIP * v, STRIP), :] = t[0:STRIP]
            lower_ref[p, pl.ds(STRIP * v, STRIP), :] = t[128 : 128 + STRIP]
        for v, block, row_start, size in BAND:
            m, b0, b1 = rows[v]
            distance = (
                lax.broadcasted_iota(jnp.int32, (size, 128), 1)
                - lax.broadcasted_iota(jnp.int32, (size, 128), 0)
                + (128 * block - row_start)
            )
            x_ref[p, pl.ds(row_start, size), pl.ds(128 * block, 128)] = jnp.where(
                distance == m, b1, jnp.where(distance == m + 1, b0, 0.0)
            ).astype(jnp.bfloat16)
    for p in range(BACK_PLANES):
        vol_ref[0, p, 0:128, :] = jnp.dot(x_ref[p], upper_ref[p], preferred_element_type=jnp.float32)
        vol_ref[0, p, 128:256, :] = jnp.dot(x_ref[p], lower_ref[p], preferred_element_type=jnp.float32)


def local(grid_x, measured, shears, taps):
    f32, bf16 = jnp.float32, jnp.bfloat16
    vmem = pl.BlockSpec(memory_space=pltpu.VMEM)
    smem = pl.BlockSpec(memory_space=pltpu.SMEM)
    yext, partial, sh_all, tp_all = pl.pallas_call(
        functools.partial(solve_kernel, grid_x),
        name="solve",
        out_shape=(
            jax.ShapeDtypeStruct((VIEWS, VROWS, RY), bf16),
            jax.ShapeDtypeStruct((1, 1, TX, TY), f32),
            jax.ShapeDtypeStruct((VIEWS, PLANES, 128), jnp.int32),
            jax.ShapeDtypeStruct((VIEWS, PLANES, 128), f32),
        ),
        in_specs=[vmem, vmem, vmem],
        out_specs=(vmem, vmem, smem, smem),
        scratch_shapes=[
            [pltpu.VMEM((RX, RY), bf16)] * VIEWS,
            [pltpu.VMEM((RX, RY), bf16)] * VIEWS,
            [pltpu.VMEM((RX, RY), bf16)] * VIEWS,
            pltpu.VMEM((VIEWS * PLANES, RY, TY), bf16),
            pltpu.VMEM((VIEWS, 2, PLANES // GROUP, 128, GROUP * STRIP), bf16),
            pltpu.VMEM((PLANES * STRIP, TY), bf16),
            pltpu.VMEM((PLANES * STRIP, TY), bf16),
            pltpu.VMEM((TX, TY), f32),
            pltpu.VMEM((TX, TY), f32),
            pltpu.VMEM((VIEWS, PLANES, 128), jnp.int32),
            pltpu.VMEM((VIEWS, PLANES, 128), f32),
            pltpu.VMEM((2, VIEWS, 8, 128), f32),
            pltpu.VMEM((2, GRID_Y, 8, 128), f32),
            pltpu.VMEM((2, grid_x, 8, 128), f32),
            pltpu.SemaphoreType.DMA((2, N_SEMS)),
            pltpu.SemaphoreType.DMA((2, N_SEMS)),
            pltpu.SemaphoreType.DMA((2, VIEWS)),
            pltpu.SemaphoreType.DMA((2, VIEWS)),
            pltpu.SemaphoreType.DMA((2,)),
            pltpu.SemaphoreType.DMA((2, VIEWS + GRID_Y + grid_x)),
            pltpu.SemaphoreType.DMA((2, VIEWS + GRID_Y + grid_x)),
        ],
        compiler_params=pltpu.CompilerParams(
            collective_id=0, has_side_effects=True, vmem_limit_bytes=48 * 1024 * 1024
        ),
    )(measured, shears, taps)
    volume, residual = pl.pallas_call(
        volume_kernel,
        name="back_project",
        grid=(PLANES // BACK_PLANES,),
        out_shape=(
            jax.ShapeDtypeStruct((1, PLANES, TX, TY), f32),
            jax.ShapeDtypeStruct((1, 1, TX, TY), f32),
        ),
        in_specs=[smem, smem, vmem, vmem],
        out_specs=(
            pl.BlockSpec((1, BACK_PLANES, TX, TY), lambda z: (0, z, 0, 0)),
            pl.BlockSpec((1, 1, TX, TY), lambda z: (0, 0, 0, 0)),
        ),
        scratch_shapes=[
            pltpu.VMEM((BACK_PLANES * VIEWS, RY, TY), bf16),
            pltpu.VMEM((BACK_PLANES, 128, VIEWS * STRIP), bf16),
            pltpu.VMEM((BACK_PLANES, VIEWS * STRIP, TY), bf16),
            pltpu.VMEM((BACK_PLANES, VIEWS * STRIP, TY), bf16),
        ],
        compiler_params=pltpu.CompilerParams(vmem_limit_bytes=32 * 1024 * 1024),
    )(sh_all, tp_all, yext, partial)
    return volume, residual


def solution(mesh):
    placed = (P("view", "tile", None, None), P("view", None, None), P("view", None, None))
    return jax.shard_map(
        functools.partial(local, mesh.shape["tile"] // GRID_Y),
        mesh=mesh,
        in_specs=placed,
        out_specs=(P("tile", None, None, None), P("view", "tile", None, None)),
        check_vma=False,
    )
```

```python
import functools

import jax
import jax.numpy as jnp
from jax import lax
from jax.experimental import pallas as pl
from jax.experimental.pallas import tpu as pltpu
from jax.sharding import PartitionSpec as P

PLANES = 16
VIEWS = 4
GRID_Y = 8
TX = 256
TY = 256
HX = 96
HY = 128
RX = TX + 2 * HX
RY = TY + 2 * HY
WINDOW = 288
STRIP = 160
GROUP = 4
BAND = (
    (0, 0, 0, 128), (0, 1, 96, 32), (1, 1, 0, 96), (1, 2, 64, 64),
    (2, 2, 0, 64), (2, 3, 32, 96), (3, 3, 0, 32), (3, 4, 0, 128),
)
FAR = 1 << 20
TINY = 1e-6
MESH = pl.DeviceIdType.MESH

X_SEMS = 6
Z_BASE = X_SEMS
Y_BASE = Z_BASE + 2 * VIEWS
N_SEMS = Y_BASE + 8 * VIEWS

PARTS = {"a": (HX, TX // 2), "b": (HX + TX // 2, TX // 2), "top": (0, HX), "bottom": (HX + TX, HX)}
PART_ID = {"a": 0, "b": 1, "top": 2, "bottom": 3}


def ring(index, step, size):
    return lax.rem(index + (step + size), size)


def solve_kernel(
    grid_x,
    meas_hbm, sh_ref, tp_ref,
    vol_ref, res_ref,
    meas_ref, e_refs, f_refs, y_ref, x_ref, upper_ref, lower_ref, q_ref, p_ref, back_ref, by_ref, bx_ref, strip_refs,
    sh_v, tp_v, sh_s, tp_s, ra_ref, rb_ref, rc_ref,
    send_sems, recv_sems, p_send, p_recv, p_local, a_send, a_recv,
):
    tile = lax.axis_index("tile")
    view = lax.axis_index("view")
    gx = tile // GRID_Y
    gy = lax.rem(tile, GRID_Y)

    def at(row, col, vw):
        return (row * GRID_Y + col, vw)

    def to_view(step):
        return at(gx, gy, ring(view, step, VIEWS))

    def to_row(step):
        return at(ring(gx, step, grid_x), gy, view)

    def to_col(step):
        return at(gx, ring(gy, step, GRID_Y), view)

    partners = (
        [to_view(s) for s in range(1, VIEWS)]
        + [to_row(s) for s in range(1, grid_x)]
        + [to_col(s) for s in range(1, GRID_Y)]
    )
    barrier = pltpu.get_barrier_semaphore()
    for partner in partners:
        pl.semaphore_signal(barrier, inc=1, device_id=partner, device_id_type=MESH)

    loading = pltpu.make_async_copy(meas_hbm.at[0, 0], meas_ref, p_local.at[2])
    loading.start()
    sh_v[0] = jnp.zeros((8, 128), jnp.int32)
    sh_v[0, 0:2, 0:PLANES] = sh_ref[0]
    tp_v[0] = jnp.zeros((8, 128), jnp.float32)
    tp_v[0, 0:4, 0:PLANES] = tp_ref[0].astype(jnp.float32)
    loading.wait()
    e_refs[0][pl.ds(HX, TX), pl.ds(HY, TY)] = meas_ref[...].astype(jnp.bfloat16)

    pl.semaphore_wait(barrier, len(partners))

    parameter_copies = []
    for step in range(1, VIEWS):
        slot = VIEWS - step
        for which, ref in ((0, sh_v), (1, tp_v)):
            copy = pltpu.make_async_remote_copy(
                src_ref=ref.at[0], dst_ref=ref.at[slot],
                send_sem=p_send.at[which, slot], recv_sem=p_recv.at[which, slot],
                device_id=to_view(step), device_id_type=MESH,
            )
            copy.start()
            parameter_copies.append(copy)

    class Exchange:
        def __init__(self, bufs, which):
            self.bufs, self.which, self.copies = bufs, which, {}

        def send(self, key, sem, src, dst, device):
            copy = pltpu.make_async_remote_copy(
                src_ref=src, dst_ref=dst,
                send_sem=send_sems.at[self.which, sem], recv_sem=recv_sems.at[self.which, sem],
                device_id=device, device_id_type=MESH,
            )
            copy.start()
            self.copies[key] = copy

        def region(self, slot, rows, cols):
            return self.bufs[slot].at[pl.ds(*rows), pl.ds(*cols)]

        def along_view(self, src_slot, dst_slot, part, sem, step):
            rows = PARTS[part]
            self.send(
                ("x", dst_slot, part), sem,
                self.region(src_slot, rows, (HY, TY)), self.region(dst_slot, rows, (HY, TY)),
                to_view(step),
            )

        def begin(self):
            self.along_view(0, 3, "a", 0, 1)
            self.along_view(0, 1, "b", 1, -1)
            self.along_view(0, 3, "b", 2, 1)
            self.along_view(0, 1, "a", 3, -1)
            self.spread(0, "a")
            self.spread(0, "b")

        def columns(self, slot, part):
            rows = PARTS[part]
            sem = Y_BASE + 8 * slot + 2 * PART_ID[part]
            self.send(
                ("y", slot, part, 0), sem,
                self.region(slot, rows, (HY, HY)), self.region(slot, rows, (HY + TY, HY)), to_col(-1),
            )
            self.send(
                ("y", slot, part, 1), sem + 1,
                self.region(slot, rows, (TY, HY)), self.region(slot, rows, (0, HY)), to_col(1),
            )

        def spread(self, slot, part):
            if part == "a":
                self.send(
                    ("z", slot, "bottom"), Z_BASE + 2 * slot,
                    self.region(slot, (HX, HX), (HY, TY)),
                    self.region(slot, (HX + TX, HX), (HY, TY)), to_row(-1),
                )
            else:
                self.send(
                    ("z", slot, "top"), Z_BASE + 2 * slot + 1,
                    self.region(slot, (TX, HX), (HY, TY)),
                    self.region(slot, (0, HX), (HY, TY)), to_row(1),
                )
            self.columns(slot, part)

        def arrive(self, slot, part):
            self.copies["x", slot, part].wait_recv()
            if slot == 3 and part == "a":
                self.along_view(3, 2, "a", 4, 1)
            if slot == 1 and part == "b":
                self.along_view(1, 2, "b", 5, -1)
            self.spread(slot, part)

        def corners(self, slot):
            for part, edge in (("top", 0), ("bottom", grid_x - 1)):
                self.copies["z", slot, part].wait_recv()

                @pl.when(gx == edge)
                def _():
                    start, size = PARTS[part]
                    self.bufs[slot][pl.ds(start, size), pl.ds(HY, TY)] = jnp.zeros((size, TY), jnp.bfloat16)

                self.columns(slot, part)

        def complete(self, slot):
            for part in PARTS:
                for side in (0, 1):
                    self.copies["y", slot, part, side].wait_recv()
            for side, edge in ((0, 0), (HY + TY, GRID_Y - 1)):
                @pl.when(gy == edge)
                def _():
                    self.bufs[slot][:, pl.ds(side, HY)] = jnp.zeros((RX, HY), jnp.bfloat16)

        def finish(self):
            for copy in self.copies.values():
                copy.wait_send()

    first = Exchange(e_refs, 0)
    first.begin()

    def clear(pair, carry):
        y_ref[pair, 0:32, 0:128] = jnp.zeros((32, 128), jnp.bfloat16)
        y_ref[pair, 352:512, 0:128] = jnp.zeros((160, 128), jnp.bfloat16)
        y_ref[pair, 0:160, 128:256] = jnp.zeros((160, 128), jnp.bfloat16)
        y_ref[pair, 480:512, 128:256] = jnp.zeros((32, 128), jnp.bfloat16)
        return carry

    lax.fori_loop(0, VIEWS * PLANES, clear, 0)

    for copy in parameter_copies:
        copy.wait_recv()
    local = [pltpu.make_async_copy(sh_v, sh_s, p_local.at[0]), pltpu.make_async_copy(tp_v, tp_s, p_local.at[1])]
    for copy in local:
        copy.start()
    for copy in local:
        copy.wait()

    column_low = jnp.where(gy == 0, 0, -FAR)
    column_high = jnp.where(gy == GRID_Y - 1, TY, FAR)
    row_low = jnp.where(gx == 0, 0, -FAR)
    row_high = jnp.where(gx == grid_x - 1, TX, FAR)

    def build(slot):
        def one(z, carry):
            shear = sh_s[0, 1, z]
            d = sh_s[slot, 1, z] - shear
            a0, a1 = tp_s[0, 2, z], tp_s[0, 3, z]
            b0, b1 = tp_s[slot, 2, z], tp_s[slot, 3, z]
            col = lax.broadcasted_iota(jnp.int32, (1, 128), 1)
            distance = (
                lax.broadcasted_iota(jnp.int32, (320, 128), 0)
                - lax.broadcasted_iota(jnp.int32, (320, 128), 1)
                + (32 - HY)
            )
            hit = [distance == d + k for k in (-1, 0, 1)]
            low, high = shear + column_low, shear + column_high
            for tile_start, in0, in1 in (
                (0, col >= low, col >= low - 1),
                (128, col + 128 < high, col + 128 < high - 1),
            ):
                before = jnp.where(in0, a0 * b1, 0.0)
                middle = jnp.where(in0, a0 * b0, 0.0) + jnp.where(in1, a1 * b1, 0.0)
                after = jnp.where(in1, a1 * b0, 0.0)
                value = jnp.where(hit[0], before, jnp.where(hit[1], middle, jnp.where(hit[2], after, 0.0)))
                y_ref[slot * PLANES + z, pl.ds(32 + tile_start, 320), pl.ds(tile_start, 128)] = value.astype(
                    jnp.bfloat16
                )
            return carry

        lax.fori_loop(0, PLANES, one, 0)

    def build_rows(slot):
        def one(g, carry):
            scalars = []
            for u in range(GROUP):
                z = GROUP * g + u
                shear = sh_s[0, 0, z]
                first_row = HX - 1 + sh_s[slot, 0, z] - shear
                m = first_row - lax.shift_right_logical(first_row, 4) * 16 + STRIP * u
                a0, a1 = tp_s[0, 0, z] * (1.0 / PLANES), tp_s[0, 1, z] * (1.0 / PLANES)
                b0, b1 = tp_s[slot, 0, z], tp_s[slot, 1, z]
                scalars.append((m, a0 * b1, a0 * b0, a1 * b1, a1 * b0, shear + row_low, shear + row_high))
            for u, block, row_start, size in BAND:
                m, am, az, bz, bp, low, high = scalars[u]
                row = lax.broadcasted_iota(jnp.int32, (size, 128), 0) + row_start
                distance = lax.broadcasted_iota(jnp.int32, (size, 128), 1) - row + 128 * block
                hit = [distance == m + k for k in (0, 1, 2)]
                for half, in0, in1 in (
                    (0, row >= low, row >= low - 1),
                    (1, row + 128 < high, row + 128 < high - 1),
                ):
                    before = jnp.where(in0, am, 0.0)
                    middle = jnp.where(in0, az, 0.0) + jnp.where(in1, bz, 0.0)
                    after = jnp.where(in1, bp, 0.0)
                    value = jnp.where(hit[0], before, jnp.where(hit[1], middle, jnp.where(hit[2], after, 0.0)))
                    x_ref[slot, half, g, pl.ds(row_start, size), pl.ds(128 * block, 128)] = value.astype(jnp.bfloat16)
            return carry

        lax.fori_loop(0, PLANES // GROUP, one, 0)

    def apply(src_ref, out_ref, slot):
        for z in range(PLANES):
            first_row = HX - 1 + sh_s[slot, 0, z] - sh_s[0, 0, z]
            start = lax.shift_right_logical(first_row, 4) * 16
            t = jnp.dot(
                src_ref[pl.ds(start, WINDOW), :], y_ref[slot * PLANES + z], preferred_element_type=jnp.float32
            ).astype(jnp.bfloat16)
            upper_ref[pl.ds(STRIP * z, STRIP), :] = t[0:STRIP]
            lower_ref[pl.ds(STRIP * z, STRIP), :] = t[128 : 128 + STRIP]
        for half, t_ref in enumerate((upper_ref, lower_ref)):
            total = out_ref[pl.ds(128 * half, 128), :]
            for g in range(PLANES // GROUP):
                total = total + jnp.dot(
                    x_ref[slot, half, g],
                    t_ref[pl.ds(GROUP * STRIP * g, GROUP * STRIP), :],
                    preferred_element_type=jnp.float32,
                )
            out_ref[pl.ds(128 * half, 128), :] = total

    def lanes(x):
        s = jnp.sum(x, axis=0, keepdims=True)
        return s[:, 0:128] + s[:, 128:256]

    class Sum:
        def __init__(self, rows):
            self.stages = (
                (ra_ref, view, VIEWS, to_view, 0),
                (rb_ref, gy, GRID_Y, to_col, VIEWS),
                (rc_ref, gx, grid_x, to_row, VIEWS + GRID_Y),
            )
            self.copies = []
            pad = jnp.zeros((8 - len(rows), 128), jnp.float32)
            self.value = jnp.concatenate(list(rows) + [pad], axis=0)

        def send(self, stage):
            ref, me, size, to, base = self.stages[stage]
            ref[me] = self.value
            self.current = []
            for step in sorted(range(1, size), key=lambda k: -min(k, size - k)):
                copy = pltpu.make_async_remote_copy(
                    src_ref=ref.at[me], dst_ref=ref.at[me],
                    send_sem=a_send.at[base + step], recv_sem=a_recv.at[base + step],
                    device_id=to(step), device_id_type=MESH,
                )
                copy.start()
                self.current.append(copy)
            self.copies += self.current

        def receive(self, stage):
            ref, me, size, to, base = self.stages[stage]
            for copy in self.current:
                copy.wait_recv()
            total = ref[0]
            for i in range(1, size):
                total = total + ref[i]
            self.value = total

        def row(self, i):
            return jnp.sum(self.value[i : i + 1, :], axis=1, keepdims=True)

        def finish(self):
            for copy in self.copies:
                copy.wait_send()

    by_ref[...] = jnp.zeros(by_ref.shape, jnp.bfloat16)

    def back(chunk):
        for u in range(GROUP):
            z = GROUP * chunk + u
            for slot in range(VIEWS):
                place = lax.rem(view + slot, VIEWS)
                d = sh_s[slot, 1, z]
                distance = (
                    lax.broadcasted_iota(jnp.int32, (224, 128), 0)
                    - lax.broadcasted_iota(jnp.int32, (224, 128), 1)
                    + (80 - HY)
                )
                value = jnp.where(
                    distance == d, tp_s[slot, 2, z], jnp.where(distance == d - 1, tp_s[slot, 3, z], 0.0)
                ).astype(jnp.bfloat16)
                pair = VIEWS * u + slot
                by_ref[pair, 80:304, 0:128] = value
                by_ref[pair, 208:432, 128:256] = value
                start = lax.shift_right_logical(HX - 1 + sh_s[slot, 0, z], 4) * 16
                both = jnp.concatenate(
                    [e_refs[slot][pl.ds(start, WINDOW), :], f_refs[slot][pl.ds(start, WINDOW), :]], axis=0
                )
                t = jnp.dot(both, by_ref[pair], preferred_element_type=jnp.float32).astype(jnp.bfloat16)
                for k, first in enumerate((0, 128, WINDOW, WINDOW + 128)):
                    strip_refs[k][u, pl.ds(STRIP * place, STRIP), :] = t[first : first + STRIP]
            for v, block, row_start, size in BAND:
                slot = lax.rem(v - view + VIEWS, VIEWS)
                first_row = HX - 1 + sh_s[slot, 0, z]
                m = first_row - lax.shift_right_logical(first_row, 4) * 16 + STRIP * v
                b0, b1 = tp_s[slot, 0, z] * (PLANES**-0.5), tp_s[slot, 1, z] * (PLANES**-0.5)
                distance = (
                    lax.broadcasted_iota(jnp.int32, (size, 128), 1)
                    - lax.broadcasted_iota(jnp.int32, (size, 128), 0)
                    + (128 * block - row_start)
                )
                bx_ref[u, pl.ds(row_start, size), pl.ds(128 * block, 128)] = jnp.where(
                    distance == m, b1, jnp.where(distance == m + 1, b0, 0.0)
                ).astype(jnp.bfloat16)
        for u in range(GROUP):
            z = GROUP * chunk + u
            for k, (ref, first) in enumerate(((vol_ref, 0), (vol_ref, 128), (back_ref, 0), (back_ref, 128))):
                ref[0, z, pl.ds(first, 128), :] = jnp.dot(
                    bx_ref[u], strip_refs[k][u], preferred_element_type=jnp.float32
                )

    q_ref[...] = jnp.zeros((TX, TY), jnp.float32)
    p_ref[...] = jnp.zeros((TX, TY), jnp.float32)

    build(0)
    build_rows(0)
    for slot, part in ((3, "a"), (1, "b"), (3, "b"), (1, "a")):
        first.arrive(slot, part)
    first.corners(0)
    build(3)
    build_rows(3)
    first.arrive(2, "a")
    first.arrive(2, "b")
    first.corners(3)
    first.corners(1)
    build(1)
    build_rows(1)
    first.corners(2)
    build(2)
    build_rows(2)
    for slot in (0, 3, 1, 2):
        first.complete(slot)
        apply(e_refs[slot], q_ref, slot)

    second = Exchange(f_refs, 1)
    f_refs[0][pl.ds(HX, TX), pl.ds(HY, TY)] = q_ref[...].astype(jnp.bfloat16)
    second.begin()
    second.corners(0)
    for slot, part in ((3, "a"), (1, "b"), (3, "b"), (1, "a")):
        second.arrive(slot, part)
    second.complete(0)
    apply(f_refs[0], p_ref, 0)
    second.arrive(2, "a")
    second.arrive(2, "b")
    second.corners(3)
    second.corners(1)
    second.corners(2)
    for slot in (3, 1, 2):
        second.complete(slot)
        apply(f_refs[slot], p_ref, slot)

    r0 = e_refs[0][pl.ds(HX, TX), pl.ds(HY, TY)].astype(jnp.float32)
    q0, p = q_ref[...], p_ref[...]
    sums = Sum([lanes(r0 * q0), lanes(q0 * q0), lanes(r0 * p), lanes(q0 * p), lanes(p * p)])
    for stage in range(3):
        sums.send(stage)
        back(stage)
        sums.receive(stage)
    back(3)
    r0q0, q0q0, r0p, q0p, pp = [sums.row(i) for i in range(5)]
    gamma0 = r0q0
    alpha0 = gamma0 / (q0q0 + TINY)
    gamma1 = r0q0 - alpha0 * (r0p + q0q0) + alpha0 * alpha0 * q0p
    beta = gamma1 / (gamma0 + TINY)
    h1h1 = q0q0 - 2.0 * alpha0 * q0p + alpha0 * alpha0 * pp
    h1q0 = q0q0 - alpha0 * q0p
    alpha1 = gamma1 / (h1h1 + 2.0 * beta * h1q0 + beta * beta * q0q0 + TINY)

    weight0 = alpha0 + alpha1 * beta + alpha1
    weight1 = alpha1 * alpha0

    def combine(z, carry):
        vol_ref[0, z] = weight0 * vol_ref[0, z] - weight1 * back_ref[0, z]
        return carry

    lax.fori_loop(0, PLANES, combine, 0)
    q0, p = q_ref[...], p_ref[...]
    res_ref[0, 0] = meas_ref[...] - alpha0 * q0 - alpha1 * ((q0 - alpha0 * p) + beta * q0)

    for copy in parameter_copies:
        copy.wait_send()
    first.finish()
    second.finish()
    sums.finish()


def local(grid_x, measured, shears, taps):
    f32, bf16 = jnp.float32, jnp.bfloat16
    vmem = pl.BlockSpec(memory_space=pltpu.VMEM)
    partners = VIEWS + GRID_Y + grid_x
    return pl.pallas_call(
        functools.partial(solve_kernel, grid_x),
        name="solve",
        out_shape=(
            jax.ShapeDtypeStruct((1, PLANES, TX, TY), f32),
            jax.ShapeDtypeStruct((1, 1, TX, TY), f32),
        ),
        in_specs=[pl.BlockSpec(memory_space=pl.ANY), vmem, vmem],
        out_specs=(vmem, vmem),
        scratch_shapes=[
            pltpu.VMEM((TX, TY), f32),
            [pltpu.VMEM((RX, RY), bf16)] * VIEWS,
            [pltpu.VMEM((RX, RY), bf16)] * VIEWS,
            pltpu.VMEM((VIEWS * PLANES, RY, TY), bf16),
            pltpu.VMEM((VIEWS, 2, PLANES // GROUP, 128, GROUP * STRIP), bf16),
            pltpu.VMEM((PLANES * STRIP, TY), bf16),
            pltpu.VMEM((PLANES * STRIP, TY), bf16),
            pltpu.VMEM((TX, TY), f32),
            pltpu.VMEM((TX, TY), f32),
            pltpu.VMEM((1, PLANES, TX, TY), f32),
            pltpu.VMEM((GROUP * VIEWS, RY, TY), bf16),
            pltpu.VMEM((GROUP, 128, VIEWS * STRIP), bf16),
            [pltpu.VMEM((GROUP, VIEWS * STRIP, TY), bf16)] * 4,
            pltpu.VMEM((VIEWS, 8, 128), jnp.int32),
            pltpu.VMEM((VIEWS, 8, 128), f32),
            pltpu.SMEM((VIEWS, 8, 128), jnp.int32),
            pltpu.SMEM((VIEWS, 8, 128), f32),
            pltpu.VMEM((VIEWS, 8, 128), f32),
            pltpu.VMEM((GRID_Y, 8, 128), f32),
            pltpu.VMEM((grid_x, 8, 128), f32),
            pltpu.SemaphoreType.DMA((2, N_SEMS)),
            pltpu.SemaphoreType.DMA((2, N_SEMS)),
            pltpu.SemaphoreType.DMA((2, VIEWS)),
            pltpu.SemaphoreType.DMA((2, VIEWS)),
            pltpu.SemaphoreType.DMA((3,)),
            pltpu.SemaphoreType.DMA((partners,)),
            pltpu.SemaphoreType.DMA((partners,)),
        ],
        compiler_params=pltpu.CompilerParams(
            collective_id=0, has_side_effects=True, vmem_limit_bytes=50 * 1024 * 1024
        ),
    )(measured, jnp.transpose(shears, (0, 2, 1)), jnp.transpose(taps, (0, 2, 1)))


def solution(mesh):
    placed = (P("view", "tile", None, None), P("view", None, None), P("view", None, None))
    return jax.shard_map(
        functools.partial(local, mesh.shape["tile"] // GRID_Y),
        mesh=mesh,
        in_specs=placed,
        out_specs=(P("tile", None, None, None), P("view", "tile", None, None)),
        check_vma=False,
    )
```

```python
import functools

import jax
import jax.numpy as jnp
from jax import lax
from jax.experimental import pallas as pl
from jax.experimental.pallas import tpu as pltpu
from jax.sharding import PartitionSpec as P

PLANES = 16
VIEWS = 4
GRID_Y = 8
TX = 256
TY = 256
HX = 96
HY = 128
RX = TX + 2 * HX
RY = TY + 2 * HY
WINDOW = 288
STRIP = 160
GROUP = 4
BAND = (
    (0, 0, 0, 128), (0, 1, 96, 32), (1, 1, 0, 96), (1, 2, 64, 64),
    (2, 2, 0, 64), (2, 3, 32, 96), (3, 3, 0, 32), (3, 4, 0, 128),
)
FAR = 1 << 20
TINY = 1e-6
MESH = pl.DeviceIdType.MESH

X_SEMS = 6
Z_BASE = X_SEMS
Y_BASE = Z_BASE + 2 * VIEWS
N_SEMS = Y_BASE + 8 * VIEWS

PARTS = {"a": (HX, TX // 2), "b": (HX + TX // 2, TX // 2), "top": (0, HX), "bottom": (HX + TX, HX)}
PART_ID = {"a": 0, "b": 1, "top": 2, "bottom": 3}


def ring(index, step, size):
    return lax.rem(index + (step + size), size)


def solve_kernel(
    grid_x,
    meas_hbm, sh_hbm, tp_hbm,
    vol_ref, res_ref,
    meas_ref, sh_ref, tp_ref, e_refs, f_refs, y_ref, x_ref, q_ref, p_ref, back_refs, by_ref, bx_ref, strip_refs,
    sh_v, tp_v, sh_s, tp_s, ra_ref, rb_ref, rc_ref,
    send_sems, recv_sems, p_send, p_recv, p_local, a_send, a_recv,
):
    tile = lax.axis_index("tile")
    view = lax.axis_index("view")
    gx = tile // GRID_Y
    gy = lax.rem(tile, GRID_Y)

    def at(row, col, vw):
        return (row * GRID_Y + col, vw)

    def to_view(step):
        return at(gx, gy, ring(view, step, VIEWS))

    def to_row(step):
        return at(ring(gx, step, grid_x), gy, view)

    def to_col(step):
        return at(gx, ring(gy, step, GRID_Y), view)

    partners = (
        [to_view(s) for s in range(1, VIEWS)]
        + [to_row(s) for s in range(1, grid_x)]
        + [to_col(s) for s in range(1, GRID_Y)]
    )
    barrier = pltpu.get_barrier_semaphore()
    for partner in partners:
        pl.semaphore_signal(barrier, inc=1, device_id=partner, device_id_type=MESH)

    loading = [
        pltpu.make_async_copy(src.at[0], dst, p_local.at[k])
        for k, (src, dst) in enumerate(((meas_hbm.at[0], meas_ref), (sh_hbm, sh_ref), (tp_hbm, tp_ref)))
    ]
    for copy in loading:
        copy.start()
    for copy in loading:
        copy.wait()
    e_refs[0][pl.ds(HX, TX), pl.ds(HY, TY)] = meas_ref[...].astype(jnp.bfloat16)
    sh_v[0] = jnp.zeros((8, 128), jnp.int32)
    sh_v[0, 0:2, 0:PLANES] = sh_ref[...]
    tp_v[0] = jnp.zeros((8, 128), jnp.float32)
    tp_v[0, 0:4, 0:PLANES] = tp_ref[...].astype(jnp.float32)

    pl.semaphore_wait(barrier, len(partners))

    class Exchange:
        def __init__(self, bufs, which):
            self.bufs, self.which, self.copies = bufs, which, {}

        def send(self, key, sem, src, dst, device):
            copy = pltpu.make_async_remote_copy(
                src_ref=src, dst_ref=dst,
                send_sem=send_sems.at[self.which, sem], recv_sem=recv_sems.at[self.which, sem],
                device_id=device, device_id_type=MESH,
            )
            copy.start()
            self.copies[key] = copy

        def region(self, slot, rows, cols):
            return self.bufs[slot].at[pl.ds(*rows), pl.ds(*cols)]

        def along_view(self, src_slot, dst_slot, part, sem, step):
            rows = PARTS[part]
            self.send(
                ("x", dst_slot, part), sem,
                self.region(src_slot, rows, (HY, TY)), self.region(dst_slot, rows, (HY, TY)),
                to_view(step),
            )

        def along_views(self):
            self.along_view(0, 3, "a", 0, 1)
            self.along_view(0, 1, "b", 1, -1)
            self.along_view(0, 3, "b", 2, 1)
            self.along_view(0, 1, "a", 3, -1)

        def own(self):
            self.spread(0, "a")
            self.spread(0, "b")

        def columns(self, slot, part):
            rows = PARTS[part]
            sem = Y_BASE + 8 * slot + 2 * PART_ID[part]
            self.send(
                ("y", slot, part, 0), sem,
                self.region(slot, rows, (HY, HY)), self.region(slot, rows, (HY + TY, HY)), to_col(-1),
            )
            self.send(
                ("y", slot, part, 1), sem + 1,
                self.region(slot, rows, (TY, HY)), self.region(slot, rows, (0, HY)), to_col(1),
            )

        def spread(self, slot, part):
            if part == "a":
                self.send(
                    ("z", slot, "bottom"), Z_BASE + 2 * slot,
                    self.region(slot, (HX, HX), (HY, TY)),
                    self.region(slot, (HX + TX, HX), (HY, TY)), to_row(-1),
                )
            else:
                self.send(
                    ("z", slot, "top"), Z_BASE + 2 * slot + 1,
                    self.region(slot, (TX, HX), (HY, TY)),
                    self.region(slot, (0, HX), (HY, TY)), to_row(1),
                )
            self.columns(slot, part)

        def arrive(self, slot, part):
            self.copies["x", slot, part].wait_recv()
            if slot == 3 and part == "a":
                self.along_view(3, 2, "a", 4, 1)
            if slot == 1 and part == "b":
                self.along_view(1, 2, "b", 5, -1)
            self.spread(slot, part)

        def corners(self, slot):
            for part, edge in (("top", 0), ("bottom", grid_x - 1)):
                self.copies["z", slot, part].wait_recv()

                @pl.when(gx == edge)
                def _():
                    start, size = PARTS[part]
                    self.bufs[slot][pl.ds(start, size), pl.ds(HY, TY)] = jnp.zeros((size, TY), jnp.bfloat16)

                self.columns(slot, part)

        def complete(self, slot):
            for part in PARTS:
                for side in (0, 1):
                    self.copies["y", slot, part, side].wait_recv()
            for side, edge in ((0, 0), (HY + TY, GRID_Y - 1)):
                @pl.when(gy == edge)
                def _():
                    self.bufs[slot][:, pl.ds(side, HY)] = jnp.zeros((RX, HY), jnp.bfloat16)

        def finish(self):
            for copy in self.copies.values():
                copy.wait_send()

    first = Exchange(e_refs, 0)
    first.along_views()

    parameter_copies = []
    for step in range(1, VIEWS):
        slot = VIEWS - step
        for which, ref in ((0, sh_v), (1, tp_v)):
            copy = pltpu.make_async_remote_copy(
                src_ref=ref.at[0], dst_ref=ref.at[slot],
                send_sem=p_send.at[which, slot], recv_sem=p_recv.at[which, slot],
                device_id=to_view(step), device_id_type=MESH,
            )
            copy.start()
            parameter_copies.append(copy)

    def tables(first_slot, count):
        local = [
            pltpu.make_async_copy(src.at[pl.ds(first_slot, count)], dst.at[pl.ds(first_slot, count)], p_local.at[k])
            for k, (src, dst) in enumerate(((sh_v, sh_s), (tp_v, tp_s)))
        ]
        for copy in local:
            copy.start()
        for copy in local:
            copy.wait()

    first.own()
    tables(0, 1)

    column_low = jnp.where(gy == 0, 0, -FAR)
    column_high = jnp.where(gy == GRID_Y - 1, TY, FAR)
    row_low = jnp.where(gx == 0, 0, -FAR)
    row_high = jnp.where(gx == grid_x - 1, TX, FAR)

    row16 = lax.broadcasted_iota(jnp.int32, (16, 128), 0)
    col16 = lax.broadcasted_iota(jnp.int32, (16, 128), 1)

    def band(distance, first, before, middle, after):
        return jnp.where(
            distance == first, before,
            jnp.where(distance == first + 1, middle, jnp.where(distance == first + 2, after, 0.0)),
        ).astype(jnp.bfloat16)

    def build(slot):
        def one(z, carry):
            pair = slot * PLANES + z
            y_ref[pair, 0:32, 0:128] = jnp.zeros((32, 128), jnp.bfloat16)
            y_ref[pair, 352:512, 0:128] = jnp.zeros((160, 128), jnp.bfloat16)
            y_ref[pair, 0:160, 128:256] = jnp.zeros((160, 128), jnp.bfloat16)
            y_ref[pair, 480:512, 128:256] = jnp.zeros((32, 128), jnp.bfloat16)
            shear = sh_s[0, 1, z]
            first = sh_s[slot, 1, z] - shear - 1 + (HY - 32)
            a0, a1 = tp_s[0, 2, z], tp_s[0, 3, z]
            b0, b1 = tp_s[slot, 2, z], tp_s[slot, 3, z]
            low, high = shear + column_low, shear + column_high
            weights = []
            for in0, in1 in (
                (col16 >= low, col16 >= low - 1),
                (col16 + 128 < high, col16 + 128 < high - 1),
            ):
                weights.append((
                    jnp.where(in0, a0 * b1, 0.0),
                    jnp.where(in0, a0 * b0, 0.0) + jnp.where(in1, a1 * b1, 0.0),
                    jnp.where(in1, a1 * b0, 0.0),
                ))
            for r in range(0, 320, 16):
                distance = row16 - col16 + r
                y_ref[pair, pl.ds(32 + r, 16), 0:128] = band(distance, first, *weights[0])
                y_ref[pair, pl.ds(160 + r, 16), 128:256] = band(distance, first, *weights[1])
            return carry

        lax.fori_loop(0, PLANES, one, 0)

    def build_rows(slot):
        def one(g, carry):
            scalars = []
            for u in range(GROUP):
                z = GROUP * g + u
                shear = sh_s[0, 0, z]
                first_row = HX - 1 + sh_s[slot, 0, z] - shear
                m = first_row - lax.shift_right_logical(first_row, 4) * 16 + STRIP * u
                a0, a1 = tp_s[0, 0, z] * (1.0 / PLANES), tp_s[0, 1, z] * (1.0 / PLANES)
                b0, b1 = tp_s[slot, 0, z], tp_s[slot, 1, z]
                scalars.append((m, a0 * b1, a0 * b0, a1 * b1, a1 * b0, shear + row_low, shear + row_high))
            for u, block, row_start, size in BAND:
                m, am, az, bz, bp, low, high = scalars[u]
                plain = (am, az + bz, bp)
                for r in range(row_start, row_start + size, 16):
                    distance = col16 - row16 + (128 * block - r)
                    for half in (0, 1):
                        weights = plain
                        if (half == 0 and r < 48) or (half == 1 and r >= 80):
                            row = row16 + (r + 128 * half)
                            in0, in1 = (row >= low, row >= low - 1) if half == 0 else (row < high, row < high - 1)
                            weights = (
                                jnp.where(in0, am, 0.0),
                                jnp.where(in0, az, 0.0) + jnp.where(in1, bz, 0.0),
                                jnp.where(in1, bp, 0.0),
                            )
                        x_ref[slot, half, g, pl.ds(r, 16), pl.ds(128 * block, 128)] = band(distance, m, *weights)
            return carry

        lax.fori_loop(0, PLANES // GROUP, one, 0)

    def apply(src_ref, out_ref, slot):
        for z in range(PLANES):
            first_row = HX - 1 + sh_s[slot, 0, z] - sh_s[0, 0, z]
            start = lax.shift_right_logical(first_row, 4) * 16
            t = jnp.dot(
                src_ref[pl.ds(start, WINDOW), :], y_ref[slot * PLANES + z], preferred_element_type=jnp.float32
            ).astype(jnp.bfloat16)
            strip = pl.ds(STRIP * (z % GROUP), STRIP)
            strip_refs[0][z // GROUP, strip, :] = t[0:STRIP]
            strip_refs[1][z // GROUP, strip, :] = t[128 : 128 + STRIP]
        for half, t_ref in enumerate(strip_refs[0:2]):
            total = out_ref[pl.ds(128 * half, 128), :]
            for g in range(PLANES // GROUP):
                total = total + jnp.dot(
                    x_ref[slot, half, g],
                    t_ref[g],
                    preferred_element_type=jnp.float32,
                )
            out_ref[pl.ds(128 * half, 128), :] = total

    def lanes(x):
        s = jnp.sum(x, axis=0, keepdims=True)
        return s[:, 0:128] + s[:, 128:256]

    class Sum:
        def __init__(self, rows):
            self.stages = (
                (ra_ref, view, VIEWS, to_view, 0),
                (rb_ref, gy, GRID_Y, to_col, VIEWS),
                (rc_ref, gx, grid_x, to_row, VIEWS + GRID_Y),
            )
            self.copies = []
            pad = jnp.zeros((8 - len(rows), 128), jnp.float32)
            self.value = jnp.concatenate(list(rows) + [pad], axis=0)

        def send(self, stage):
            ref, me, size, to, base = self.stages[stage]
            ref[me] = self.value
            self.current = []
            for step in sorted(range(1, size), key=lambda k: -min(k, size - k)):
                copy = pltpu.make_async_remote_copy(
                    src_ref=ref.at[me], dst_ref=ref.at[me],
                    send_sem=a_send.at[base + step], recv_sem=a_recv.at[base + step],
                    device_id=to(step), device_id_type=MESH,
                )
                copy.start()
                self.current.append(copy)
            self.copies += self.current

        def receive(self, stage):
            ref, me, size, to, base = self.stages[stage]
            for copy in self.current:
                copy.wait_recv()
            total = ref[0]
            for i in range(1, size):
                total = total + ref[i]
            self.value = total

        def row(self, i):
            return jnp.sum(self.value[i : i + 1, :], axis=1, keepdims=True)

        def finish(self):
            for copy in self.copies:
                copy.wait_send()

    by_ref[...] = jnp.zeros(by_ref.shape, jnp.bfloat16)

    def back(chunk):
        for u in range(GROUP):
            z = GROUP * chunk + u
            for slot in range(VIEWS):
                place = lax.rem(view + slot, VIEWS)
                d = sh_s[slot, 1, z]
                distance = (
                    lax.broadcasted_iota(jnp.int32, (224, 128), 0)
                    - lax.broadcasted_iota(jnp.int32, (224, 128), 1)
                    + (80 - HY)
                )
                value = jnp.where(
                    distance == d, tp_s[slot, 2, z], jnp.where(distance == d - 1, tp_s[slot, 3, z], 0.0)
                ).astype(jnp.bfloat16)
                pair = VIEWS * u + slot
                by_ref[pair, 80:304, 0:128] = value
                by_ref[pair, 208:432, 128:256] = value
                start = lax.shift_right_logical(HX - 1 + sh_s[slot, 0, z], 4) * 16
                both = jnp.concatenate(
                    [e_refs[slot][pl.ds(start, WINDOW), :], f_refs[slot][pl.ds(start, WINDOW), :]], axis=0
                )
                t = jnp.dot(both, by_ref[pair], preferred_element_type=jnp.float32).astype(jnp.bfloat16)
                for k, first in enumerate((0, 128, WINDOW, WINDOW + 128)):
                    strip_refs[k][u, pl.ds(STRIP * place, STRIP), :] = t[first : first + STRIP]
            for v, block, row_start, size in BAND:
                slot = lax.rem(v - view + VIEWS, VIEWS)
                first_row = HX - 1 + sh_s[slot, 0, z]
                m = first_row - lax.shift_right_logical(first_row, 4) * 16 + STRIP * v
                b0, b1 = tp_s[slot, 0, z] * (PLANES**-0.5), tp_s[slot, 1, z] * (PLANES**-0.5)
                distance = (
                    lax.broadcasted_iota(jnp.int32, (size, 128), 1)
                    - lax.broadcasted_iota(jnp.int32, (size, 128), 0)
                    + (128 * block - row_start)
                )
                bx_ref[u, pl.ds(row_start, size), pl.ds(128 * block, 128)] = jnp.where(
                    distance == m, b1, jnp.where(distance == m + 1, b0, 0.0)
                ).astype(jnp.bfloat16)
        for u in range(GROUP):
            z = GROUP * chunk + u
            for k, (ref, first) in enumerate(((0, 0), (0, 128), (1, 0), (1, 128))):
                back_refs[ref][z, pl.ds(first, 128), :] = jnp.dot(
                    bx_ref[u], strip_refs[k][u], preferred_element_type=jnp.float32
                )

    q_ref[...] = jnp.zeros((TX, TY), jnp.float32)
    p_ref[...] = jnp.zeros((TX, TY), jnp.float32)

    build(0)
    build_rows(0)
    for copy in parameter_copies:
        copy.wait_recv()
    tables(1, VIEWS - 1)
    for slot, part in ((3, "a"), (1, "b"), (3, "b"), (1, "a")):
        first.arrive(slot, part)
    first.corners(0)
    build(3)
    build_rows(3)
    first.arrive(2, "a")
    first.arrive(2, "b")
    first.corners(3)
    first.corners(1)
    build(1)
    build_rows(1)
    first.corners(2)
    build(2)
    build_rows(2)
    for slot in (0, 3, 1, 2):
        first.complete(slot)
        apply(e_refs[slot], q_ref, slot)

    second = Exchange(f_refs, 1)
    f_refs[0][pl.ds(HX, TX), pl.ds(HY, TY)] = q_ref[...].astype(jnp.bfloat16)
    second.along_views()
    second.own()
    second.corners(0)
    for slot, part in ((3, "a"), (1, "b"), (3, "b"), (1, "a")):
        second.arrive(slot, part)
    second.complete(0)
    apply(f_refs[0], p_ref, 0)
    second.arrive(2, "a")
    second.arrive(2, "b")
    second.corners(3)
    second.corners(1)
    second.corners(2)
    for slot in (3, 1, 2):
        second.complete(slot)
        apply(f_refs[slot], p_ref, slot)

    r0 = e_refs[0][pl.ds(HX, TX), pl.ds(HY, TY)].astype(jnp.float32)
    q0, p = q_ref[...], p_ref[...]
    sums = Sum([lanes(r0 * q0), lanes(q0 * q0), lanes(r0 * p), lanes(q0 * p), lanes(p * p)])
    for stage in range(3):
        sums.send(stage)
        back(stage)
        sums.receive(stage)
    back(3)
    r0q0, q0q0, r0p, q0p, pp = [sums.row(i) for i in range(5)]
    gamma0 = r0q0
    alpha0 = gamma0 / (q0q0 + TINY)
    gamma1 = r0q0 - alpha0 * (r0p + q0q0) + alpha0 * alpha0 * q0p
    beta = gamma1 / (gamma0 + TINY)
    h1h1 = q0q0 - 2.0 * alpha0 * q0p + alpha0 * alpha0 * pp
    h1q0 = q0q0 - alpha0 * q0p
    alpha1 = gamma1 / (h1h1 + 2.0 * beta * h1q0 + beta * beta * q0q0 + TINY)

    weight0 = alpha0 + alpha1 * beta + alpha1
    weight1 = alpha1 * alpha0

    def combine(z, carry):
        vol_ref[0, z] = (weight0 * back_refs[0][z] - weight1 * back_refs[1][z]).astype(jnp.bfloat16)
        return carry

    lax.fori_loop(0, PLANES, combine, 0)
    q0, p = q_ref[...], p_ref[...]
    res_ref[0, 0] = meas_ref[...] - alpha0 * q0 - alpha1 * ((q0 - alpha0 * p) + beta * q0)

    for copy in parameter_copies:
        copy.wait_send()
    first.finish()
    second.finish()
    sums.finish()


def write_kernel(vol_ref, res_ref, vol_out, res_out):
    vol_out[...] = vol_ref[...].astype(jnp.float32)
    res_out[...] = res_ref[...]


def local(grid_x, measured, shears, taps):
    f32, bf16 = jnp.float32, jnp.bfloat16
    vmem = pl.BlockSpec(memory_space=pltpu.VMEM)
    partners = VIEWS + GRID_Y + grid_x
    hbm = pl.BlockSpec(memory_space=pltpu.HBM)
    volume, residual = pl.pallas_call(
        functools.partial(solve_kernel, grid_x),
        name="solve",
        out_shape=(
            jax.ShapeDtypeStruct((1, PLANES, TX, TY), bf16),
            jax.ShapeDtypeStruct((1, 1, TX, TY), f32),
        ),
        in_specs=[hbm, hbm, hbm],
        out_specs=(vmem, vmem),
        scratch_shapes=[
            pltpu.VMEM((TX, TY), f32),
            pltpu.VMEM((2, PLANES), jnp.int32),
            pltpu.VMEM((4, PLANES), bf16),
            [pltpu.VMEM((RX, RY), bf16)] * VIEWS,
            [pltpu.VMEM((RX, RY), bf16)] * VIEWS,
            pltpu.VMEM((VIEWS * PLANES, RY, TY), bf16),
            pltpu.VMEM((VIEWS, 2, PLANES // GROUP, 128, GROUP * STRIP), bf16),
            pltpu.VMEM((TX, TY), f32),
            pltpu.VMEM((TX, TY), f32),
            [pltpu.VMEM((PLANES, TX, TY), f32)] * 2,
            pltpu.VMEM((GROUP * VIEWS, RY, TY), bf16),
            pltpu.VMEM((GROUP, 128, VIEWS * STRIP), bf16),
            [pltpu.VMEM((GROUP, VIEWS * STRIP, TY), bf16)] * 4,
            pltpu.VMEM((VIEWS, 8, 128), jnp.int32),
            pltpu.VMEM((VIEWS, 8, 128), f32),
            pltpu.SMEM((VIEWS, 8, 128), jnp.int32),
            pltpu.SMEM((VIEWS, 8, 128), f32),
            pltpu.VMEM((VIEWS, 8, 128), f32),
            pltpu.VMEM((GRID_Y, 8, 128), f32),
            pltpu.VMEM((grid_x, 8, 128), f32),
            pltpu.SemaphoreType.DMA((2, N_SEMS)),
            pltpu.SemaphoreType.DMA((2, N_SEMS)),
            pltpu.SemaphoreType.DMA((2, VIEWS)),
            pltpu.SemaphoreType.DMA((2, VIEWS)),
            pltpu.SemaphoreType.DMA((3,)),
            pltpu.SemaphoreType.DMA((partners,)),
            pltpu.SemaphoreType.DMA((partners,)),
        ],
        compiler_params=pltpu.CompilerParams(
            collective_id=0, has_side_effects=True, vmem_limit_bytes=50 * 1024 * 1024
        ),
    )(measured, jnp.transpose(shears, (0, 2, 1)), jnp.transpose(taps, (0, 2, 1)))
    return pl.pallas_call(
        write_kernel,
        name="write",
        grid=(4,),
        out_shape=(
            jax.ShapeDtypeStruct((1, PLANES, TX, TY), f32),
            jax.ShapeDtypeStruct((1, 1, TX, TY), f32),
        ),
        in_specs=[
            pl.BlockSpec((1, PLANES // 4, TX, TY), lambda i: (0, i, 0, 0)),
            pl.BlockSpec((1, 1, TX // 4, TY), lambda i: (0, 0, i, 0)),
        ],
        out_specs=(
            pl.BlockSpec((1, PLANES // 4, TX, TY), lambda i: (0, i, 0, 0)),
            pl.BlockSpec((1, 1, TX // 4, TY), lambda i: (0, 0, i, 0)),
        ),
    )(volume, residual)


def solution(mesh):
    placed = (P("view", "tile", None, None), P("view", None, None), P("view", None, None))
    return jax.shard_map(
        functools.partial(local, mesh.shape["tile"] // GRID_Y),
        mesh=mesh,
        in_specs=placed,
        out_specs=(P("tile", None, None, None), P("view", "tile", None, None)),
        check_vma=False,
    )
```

```python
import functools

import jax
import jax.numpy as jnp
from jax import lax
from jax.experimental import pallas as pl
from jax.experimental.pallas import tpu as pltpu
from jax.sharding import PartitionSpec as P

PLANES = 16
VIEWS = 4
GRID_Y = 8
TX = 256
TY = 256
HX = 96
HY = 128
RX = TX + 2 * HX
RY = TY + 2 * HY
WINDOW = 288
STRIP = 160
WRITE_PLANES = 2
GROUP = 4
BAND = (
    (0, 0, 0, 128), (0, 1, 96, 32), (1, 1, 0, 96), (1, 2, 64, 64),
    (2, 2, 0, 64), (2, 3, 32, 96), (3, 3, 0, 32), (3, 4, 0, 128),
)
FAR = 1 << 20
TINY = 1e-6
MESH = pl.DeviceIdType.MESH

X_SEMS = 6
Z_BASE = X_SEMS
Y_BASE = Z_BASE + 2 * VIEWS
N_SEMS = Y_BASE + 8 * VIEWS

PARTS = {"a": (HX, TX // 2), "b": (HX + TX // 2, TX // 2), "top": (0, HX), "bottom": (HX + TX, HX)}
PART_ID = {"a": 0, "b": 1, "top": 2, "bottom": 3}


def ring(index, step, size):
    return lax.rem(index + (step + size), size)


def solve_kernel(
    grid_x,
    meas_hbm, sh_hbm, tp_hbm,
    vol_ref, res_ref,
    meas_ref, sh_ref, tp_ref, e_refs, f_refs, y_ref, x_ref, q_ref, p_ref, back_refs, by_ref, bx_ref, strip_refs,
    sh_v, tp_v, sh_s, tp_s, ra_ref, rb_ref, rc_ref,
    send_sems, recv_sems, p_send, p_recv, p_local, a_send, a_recv,
):
    tile = lax.axis_index("tile")
    view = lax.axis_index("view")
    gx = tile // GRID_Y
    gy = lax.rem(tile, GRID_Y)

    def at(row, col, vw):
        return (row * GRID_Y + col, vw)

    def to_view(step):
        return at(gx, gy, ring(view, step, VIEWS))

    def to_row(step):
        return at(ring(gx, step, grid_x), gy, view)

    def to_col(step):
        return at(gx, ring(gy, step, GRID_Y), view)

    partners = (
        [to_view(s) for s in range(1, VIEWS)]
        + [to_row(s) for s in range(1, grid_x)]
        + [to_col(s) for s in range(1, GRID_Y)]
    )
    barrier = pltpu.get_barrier_semaphore()
    for partner in partners:
        pl.semaphore_signal(barrier, inc=1, device_id=partner, device_id_type=MESH)

    loading = [
        pltpu.make_async_copy(src.at[0], dst, p_local.at[k])
        for k, (src, dst) in enumerate(((meas_hbm.at[0], meas_ref), (sh_hbm, sh_ref), (tp_hbm, tp_ref)))
    ]
    for copy in loading:
        copy.start()
    for copy in loading:
        copy.wait()
    e_refs[0][pl.ds(HX, TX), pl.ds(HY, TY)] = meas_ref[...].astype(jnp.bfloat16)
    sh_v[0] = jnp.zeros((8, 128), jnp.int32)
    sh_v[0, 0:2, 0:PLANES] = sh_ref[...]
    tp_v[0] = jnp.zeros((8, 128), jnp.float32)
    tp_v[0, 0:4, 0:PLANES] = tp_ref[...].astype(jnp.float32)

    pl.semaphore_wait(barrier, len(partners))

    class Exchange:
        def __init__(self, bufs, which):
            self.bufs, self.which, self.copies = bufs, which, {}

        def send(self, key, sem, src, dst, device):
            copy = pltpu.make_async_remote_copy(
                src_ref=src, dst_ref=dst,
                send_sem=send_sems.at[self.which, sem], recv_sem=recv_sems.at[self.which, sem],
                device_id=device, device_id_type=MESH,
            )
            copy.start()
            self.copies[key] = copy

        def region(self, slot, rows, cols):
            return self.bufs[slot].at[pl.ds(*rows), pl.ds(*cols)]

        def along_view(self, src_slot, dst_slot, part, sem, step):
            rows = PARTS[part]
            self.send(
                ("x", dst_slot, part), sem,
                self.region(src_slot, rows, (HY, TY)), self.region(dst_slot, rows, (HY, TY)),
                to_view(step),
            )

        def along_views(self):
            self.along_view(0, 3, "a", 0, 1)
            self.along_view(0, 1, "b", 1, -1)
            self.along_view(0, 3, "b", 2, 1)
            self.along_view(0, 1, "a", 3, -1)

        def own(self):
            self.spread(0, "a")
            self.spread(0, "b")

        def columns(self, slot, part):
            rows = PARTS[part]
            sem = Y_BASE + 8 * slot + 2 * PART_ID[part]
            self.send(
                ("y", slot, part, 0), sem,
                self.region(slot, rows, (HY, HY)), self.region(slot, rows, (HY + TY, HY)), to_col(-1),
            )
            self.send(
                ("y", slot, part, 1), sem + 1,
                self.region(slot, rows, (TY, HY)), self.region(slot, rows, (0, HY)), to_col(1),
            )

        def spread(self, slot, part):
            if part == "a":
                self.send(
                    ("z", slot, "bottom"), Z_BASE + 2 * slot,
                    self.region(slot, (HX, HX), (HY, TY)),
                    self.region(slot, (HX + TX, HX), (HY, TY)), to_row(-1),
                )
            else:
                self.send(
                    ("z", slot, "top"), Z_BASE + 2 * slot + 1,
                    self.region(slot, (TX, HX), (HY, TY)),
                    self.region(slot, (0, HX), (HY, TY)), to_row(1),
                )
            self.columns(slot, part)

        def arrive(self, slot, part):
            self.copies["x", slot, part].wait_recv()
            if slot == 3 and part == "a":
                self.along_view(3, 2, "a", 4, 1)
            if slot == 1 and part == "b":
                self.along_view(1, 2, "b", 5, -1)
            self.spread(slot, part)

        def corners(self, slot):
            for part, edge in (("top", 0), ("bottom", grid_x - 1)):
                self.copies["z", slot, part].wait_recv()

                @pl.when(gx == edge)
                def _():
                    start, size = PARTS[part]
                    self.bufs[slot][pl.ds(start, size), pl.ds(HY, TY)] = jnp.zeros((size, TY), jnp.bfloat16)

                self.columns(slot, part)

        def complete(self, slot):
            for part in PARTS:
                for side in (0, 1):
                    self.copies["y", slot, part, side].wait_recv()
            for side, edge in ((0, 0), (HY + TY, GRID_Y - 1)):
                @pl.when(gy == edge)
                def _():
                    self.bufs[slot][:, pl.ds(side, HY)] = jnp.zeros((RX, HY), jnp.bfloat16)

        def finish(self):
            for copy in self.copies.values():
                copy.wait_send()

    first = Exchange(e_refs, 0)

    parameter_copies = []
    for step in range(1, VIEWS):
        slot = VIEWS - step
        for which, ref in ((0, sh_v), (1, tp_v)):
            copy = pltpu.make_async_remote_copy(
                src_ref=ref.at[0], dst_ref=ref.at[slot],
                send_sem=p_send.at[which, slot], recv_sem=p_recv.at[which, slot],
                device_id=to_view(step), device_id_type=MESH,
            )
            copy.start()
            parameter_copies.append(copy)

    first.along_views()

    def tables(first_slot, count):
        local = [
            pltpu.make_async_copy(src.at[pl.ds(first_slot, count)], dst.at[pl.ds(first_slot, count)], p_local.at[k])
            for k, (src, dst) in enumerate(((sh_v, sh_s), (tp_v, tp_s)))
        ]
        for copy in local:
            copy.start()
        for copy in local:
            copy.wait()

    first.own()
    tables(0, 1)

    column_low = jnp.where(gy == 0, 0, -FAR)
    column_high = jnp.where(gy == GRID_Y - 1, TY, FAR)
    row_low = jnp.where(gx == 0, 0, -FAR)
    row_high = jnp.where(gx == grid_x - 1, TX, FAR)

    row16 = lax.broadcasted_iota(jnp.int32, (16, 128), 0)
    col16 = lax.broadcasted_iota(jnp.int32, (16, 128), 1)
    below = (row16 - col16).astype(jnp.int16)
    beyond = (col16 - row16).astype(jnp.int16)

    def spread16(x):
        return jnp.full((16, 128), x, jnp.int32).astype(jnp.int16)

    def narrow(weights):
        return [jnp.broadcast_to(w, (16, 128)).astype(jnp.bfloat16) for w in weights]

    def band(distance, first, weights):
        value = jnp.zeros((16, 128), jnp.bfloat16)
        for at, weight in zip(first, weights):
            value = jnp.where(distance == at, weight, value)
        return value

    def build(slot):
        def one(z, carry):
            pair = slot * PLANES + z
            y_ref[pair, 0:32, 0:128] = jnp.zeros((32, 128), jnp.bfloat16)
            y_ref[pair, 352:512, 0:128] = jnp.zeros((160, 128), jnp.bfloat16)
            y_ref[pair, 0:160, 128:256] = jnp.zeros((160, 128), jnp.bfloat16)
            y_ref[pair, 480:512, 128:256] = jnp.zeros((32, 128), jnp.bfloat16)
            shear = sh_s[0, 1, z]
            first = [spread16(sh_s[slot, 1, z] - shear + (HY - 32 + k)) for k in (-1, 0, 1)]
            a0, a1 = tp_s[0, 2, z], tp_s[0, 3, z]
            b0, b1 = tp_s[slot, 2, z], tp_s[slot, 3, z]
            low, high = shear + column_low, shear + column_high
            weights = []
            for in0, in1 in (
                (col16 >= low, col16 >= low - 1),
                (col16 + 128 < high, col16 + 128 < high - 1),
            ):
                weights.append(narrow((
                    jnp.where(in0, a0 * b1, 0.0),
                    jnp.where(in0, a0 * b0, 0.0) + jnp.where(in1, a1 * b1, 0.0),
                    jnp.where(in1, a1 * b0, 0.0),
                )))
            for r in range(0, 320, 16):
                distance = below + jnp.int16(r)
                y_ref[pair, pl.ds(32 + r, 16), 0:128] = band(distance, first, weights[0])
                y_ref[pair, pl.ds(160 + r, 16), 128:256] = band(distance, first, weights[1])
            return carry

        lax.fori_loop(0, PLANES, one, 0)

    def build_rows(slot):
        def one(g, carry):
            scalars = []
            for u in range(GROUP):
                z = GROUP * g + u
                shear = sh_s[0, 0, z]
                first_row = HX - 1 + sh_s[slot, 0, z] - shear
                m = first_row - lax.shift_right_logical(first_row, 4) * 16 + STRIP * u
                a0, a1 = tp_s[0, 0, z] * (1.0 / PLANES), tp_s[0, 1, z] * (1.0 / PLANES)
                b0, b1 = tp_s[slot, 0, z], tp_s[slot, 1, z]
                scalars.append((m, a0 * b1, a0 * b0, a1 * b1, a1 * b0, shear + row_low, shear + row_high))
            for u, block, row_start, size in BAND:
                m, am, az, bz, bp, low, high = scalars[u]
                plain = narrow((am, az + bz, bp))
                first = [spread16(m + k) for k in (0, 1, 2)]
                for r in range(row_start, row_start + size, 16):
                    distance = beyond + jnp.int16(128 * block - r)
                    for half in (0, 1):
                        weights = plain
                        if (half == 0 and r < 48) or (half == 1 and r >= 80):
                            row = row16 + (r + 128 * half)
                            in0, in1 = (row >= low, row >= low - 1) if half == 0 else (row < high, row < high - 1)
                            weights = narrow((
                                jnp.where(in0, am, 0.0),
                                jnp.where(in0, az, 0.0) + jnp.where(in1, bz, 0.0),
                                jnp.where(in1, bp, 0.0),
                            ))
                        x_ref[slot, half, g, pl.ds(r, 16), pl.ds(128 * block, 128)] = band(distance, first, weights)
            return carry

        lax.fori_loop(0, PLANES // GROUP, one, 0)

    def apply(src_ref, out_ref, slot):
        for z in range(PLANES):
            first_row = HX - 1 + sh_s[slot, 0, z] - sh_s[0, 0, z]
            start = lax.shift_right_logical(first_row, 4) * 16
            t = jnp.dot(
                src_ref[pl.ds(start, WINDOW), :], y_ref[slot * PLANES + z], preferred_element_type=jnp.float32
            ).astype(jnp.bfloat16)
            strip = pl.ds(STRIP * (z % GROUP), STRIP)
            strip_refs[0][z // GROUP, strip, :] = t[0:STRIP]
            strip_refs[1][z // GROUP, strip, :] = t[128 : 128 + STRIP]
        for half, t_ref in enumerate(strip_refs[0:2]):
            total = out_ref[pl.ds(128 * half, 128), :]
            for g in range(PLANES // GROUP):
                total = total + jnp.dot(
                    x_ref[slot, half, g],
                    t_ref[g],
                    preferred_element_type=jnp.float32,
                )
            out_ref[pl.ds(128 * half, 128), :] = total

    def lanes(x):
        s = jnp.sum(x, axis=0, keepdims=True)
        return s[:, 0:128] + s[:, 128:256]

    class Sum:
        def __init__(self, rows):
            self.stages = (
                (ra_ref, view, VIEWS, to_view, 0),
                (rb_ref, gy, GRID_Y, to_col, VIEWS),
                (rc_ref, gx, grid_x, to_row, VIEWS + GRID_Y),
            )
            self.copies = []
            pad = jnp.zeros((8 - len(rows), 128), jnp.float32)
            self.value = jnp.concatenate(list(rows) + [pad], axis=0)

        def send(self, stage):
            ref, me, size, to, base = self.stages[stage]
            ref[me] = self.value
            self.current = []
            for step in sorted(range(1, size), key=lambda k: -min(k, size - k)):
                copy = pltpu.make_async_remote_copy(
                    src_ref=ref.at[me], dst_ref=ref.at[me],
                    send_sem=a_send.at[base + step], recv_sem=a_recv.at[base + step],
                    device_id=to(step), device_id_type=MESH,
                )
                copy.start()
                self.current.append(copy)
            self.copies += self.current

        def receive(self, stage):
            ref, me, size, to, base = self.stages[stage]
            for copy in self.current:
                copy.wait_recv()
            total = ref[0]
            for i in range(1, size):
                total = total + ref[i]
            self.value = total

        def row(self, i):
            return jnp.sum(self.value[i : i + 1, :], axis=1, keepdims=True)

        def finish(self):
            for copy in self.copies:
                copy.wait_send()

    by_ref[...] = jnp.zeros(by_ref.shape, jnp.bfloat16)

    def back(chunk, sources):
        refs = [(e_refs, f_refs)[k] for k in sources]
        for u in range(GROUP):
            z = GROUP * chunk + u
            for slot in range(VIEWS):
                place = lax.rem(view + slot, VIEWS)
                d = sh_s[slot, 1, z]
                weights = narrow((tp_s[slot, 3, z], tp_s[slot, 2, z]))
                at = [spread16(d + (HY - 80 + k)) for k in (-1, 0)]
                pair = VIEWS * u + slot
                for r in range(0, 224, 16):
                    value = band(below + jnp.int16(r), at, weights)
                    by_ref[pair, pl.ds(80 + r, 16), 0:128] = value
                    by_ref[pair, pl.ds(208 + r, 16), 128:256] = value
                start = lax.shift_right_logical(HX - 1 + sh_s[slot, 0, z], 4) * 16
                rows = [ref[slot][pl.ds(start, WINDOW), :] for ref in refs]
                t = jnp.dot(
                    jnp.concatenate(rows, axis=0) if len(rows) > 1 else rows[0],
                    by_ref[pair], preferred_element_type=jnp.float32,
                ).astype(jnp.bfloat16)
                for k in range(2 * len(refs)):
                    first = WINDOW * (k // 2) + 128 * (k % 2)
                    strip_refs[k][u, pl.ds(STRIP * place, STRIP), :] = t[first : first + STRIP]
            for v, block, row_start, size in BAND:
                slot = lax.rem(v - view + VIEWS, VIEWS)
                first_row = HX - 1 + sh_s[slot, 0, z]
                m = first_row - lax.shift_right_logical(first_row, 4) * 16 + STRIP * v
                weights = narrow((tp_s[slot, 1, z] * (PLANES**-0.5), tp_s[slot, 0, z] * (PLANES**-0.5)))
                at = [spread16(m + k) for k in (0, 1)]
                for r in range(row_start, row_start + size, 16):
                    bx_ref[u, pl.ds(r, 16), pl.ds(128 * block, 128)] = band(
                        beyond + jnp.int16(128 * block - r), at, weights
                    )
        for u in range(GROUP):
            z = GROUP * chunk + u
            for k in range(2 * len(refs)):
                back_refs[sources[k // 2]][z, pl.ds(128 * (k % 2), 128), :] = jnp.dot(
                    bx_ref[u], strip_refs[k][u], preferred_element_type=jnp.float32
                )

    q_ref[...] = jnp.zeros((TX, TY), jnp.float32)
    p_ref[...] = jnp.zeros((TX, TY), jnp.float32)

    build(0)
    build_rows(0)
    for copy in parameter_copies:
        copy.wait_recv()
    tables(1, VIEWS - 1)
    first.corners(0)
    first.arrive(3, "a")
    first.arrive(1, "b")
    build(3)
    build_rows(3)
    first.arrive(3, "b")
    first.arrive(1, "a")
    first.complete(0)
    apply(e_refs[0], q_ref, 0)
    first.arrive(2, "a")
    first.arrive(2, "b")
    first.corners(3)
    first.corners(1)
    build(1)
    build_rows(1)
    first.corners(2)
    build(2)
    build_rows(2)
    for slot in (3, 1, 2):
        first.complete(slot)
        apply(e_refs[slot], q_ref, slot)

    second = Exchange(f_refs, 1)
    f_refs[0][pl.ds(HX, TX), pl.ds(HY, TY)] = q_ref[...].astype(jnp.bfloat16)
    second.along_views()
    second.own()
    back(0, (0,))
    second.corners(0)
    for slot, part in ((3, "a"), (1, "b"), (3, "b"), (1, "a")):
        second.arrive(slot, part)
    second.complete(0)
    apply(f_refs[0], p_ref, 0)
    second.arrive(2, "a")
    second.arrive(2, "b")
    second.corners(3)
    second.corners(1)
    back(1, (0,))
    second.corners(2)
    for slot in (3, 1, 2):
        second.complete(slot)
        apply(f_refs[slot], p_ref, slot)

    r0 = e_refs[0][pl.ds(HX, TX), pl.ds(HY, TY)].astype(jnp.float32)
    q0, p = q_ref[...], p_ref[...]
    sums = Sum([lanes(r0 * q0), lanes(q0 * q0), lanes(r0 * p), lanes(q0 * p), lanes(p * p)])
    sums.send(0)
    back(2, (0, 1))
    sums.receive(0)
    sums.send(1)
    back(3, (0, 1))
    sums.receive(1)
    sums.send(2)
    back(0, (1,))
    back(1, (1,))
    sums.receive(2)
    r0q0, q0q0, r0p, q0p, pp = [sums.row(i) for i in range(5)]
    gamma0 = r0q0
    alpha0 = gamma0 / (q0q0 + TINY)
    gamma1 = r0q0 - alpha0 * (r0p + q0q0) + alpha0 * alpha0 * q0p
    beta = gamma1 / (gamma0 + TINY)
    h1h1 = q0q0 - 2.0 * alpha0 * q0p + alpha0 * alpha0 * pp
    h1q0 = q0q0 - alpha0 * q0p
    alpha1 = gamma1 / (h1h1 + 2.0 * beta * h1q0 + beta * beta * q0q0 + TINY)

    weight0 = alpha0 + alpha1 * beta + alpha1
    weight1 = alpha1 * alpha0

    def combine(z, carry):
        vol_ref[0, z] = (weight0 * back_refs[0][z] - weight1 * back_refs[1][z]).astype(jnp.bfloat16)
        return carry

    lax.fori_loop(0, PLANES, combine, 0)
    q0, p = q_ref[...], p_ref[...]
    res_ref[0, 0] = meas_ref[...] - alpha0 * q0 - alpha1 * ((q0 - alpha0 * p) + beta * q0)

    for copy in parameter_copies:
        copy.wait_send()
    first.finish()
    second.finish()
    sums.finish()


def write_kernel(vol_ref, res_ref, vol_out, res_out):
    step = pl.program_id(0)
    planes = pl.ds(step * WRITE_PLANES, WRITE_PLANES)
    vol_out[0] = vol_ref[0, planes].astype(jnp.float32)

    @pl.when(step == 0)
    def _():
        res_out[...] = res_ref[...]


def local(grid_x, measured, shears, taps):
    f32, bf16 = jnp.float32, jnp.bfloat16
    vmem = pl.BlockSpec(memory_space=pltpu.VMEM)
    partners = VIEWS + GRID_Y + grid_x
    hbm = pl.BlockSpec(memory_space=pltpu.HBM)
    volume, residual = pl.pallas_call(
        functools.partial(solve_kernel, grid_x),
        name="solve",
        out_shape=(
            jax.ShapeDtypeStruct((1, PLANES, TX, TY), bf16),
            jax.ShapeDtypeStruct((1, 1, TX, TY), f32),
        ),
        in_specs=[hbm, hbm, hbm],
        out_specs=(vmem, vmem),
        scratch_shapes=[
            pltpu.VMEM((TX, TY), f32),
            pltpu.VMEM((2, PLANES), jnp.int32),
            pltpu.VMEM((4, PLANES), bf16),
            [pltpu.VMEM((RX, RY), bf16)] * VIEWS,
            [pltpu.VMEM((RX, RY), bf16)] * VIEWS,
            pltpu.VMEM((VIEWS * PLANES, RY, TY), bf16),
            pltpu.VMEM((VIEWS, 2, PLANES // GROUP, 128, GROUP * STRIP), bf16),
            pltpu.VMEM((TX, TY), f32),
            pltpu.VMEM((TX, TY), f32),
            [pltpu.VMEM((PLANES, TX, TY), f32)] * 2,
            pltpu.VMEM((GROUP * VIEWS, RY, TY), bf16),
            pltpu.VMEM((GROUP, 128, VIEWS * STRIP), bf16),
            [pltpu.VMEM((GROUP, VIEWS * STRIP, TY), bf16)] * 4,
            pltpu.VMEM((VIEWS, 8, 128), jnp.int32),
            pltpu.VMEM((VIEWS, 8, 128), f32),
            pltpu.SMEM((VIEWS, 8, 128), jnp.int32),
            pltpu.SMEM((VIEWS, 8, 128), f32),
            pltpu.VMEM((VIEWS, 8, 128), f32),
            pltpu.VMEM((GRID_Y, 8, 128), f32),
            pltpu.VMEM((grid_x, 8, 128), f32),
            pltpu.SemaphoreType.DMA((2, N_SEMS)),
            pltpu.SemaphoreType.DMA((2, N_SEMS)),
            pltpu.SemaphoreType.DMA((2, VIEWS)),
            pltpu.SemaphoreType.DMA((2, VIEWS)),
            pltpu.SemaphoreType.DMA((3,)),
            pltpu.SemaphoreType.DMA((partners,)),
            pltpu.SemaphoreType.DMA((partners,)),
        ],
        compiler_params=pltpu.CompilerParams(
            collective_id=0, has_side_effects=True, vmem_limit_bytes=50 * 1024 * 1024
        ),
    )(measured, jnp.transpose(shears, (0, 2, 1)), jnp.transpose(taps, (0, 2, 1)))
    return pl.pallas_call(
        write_kernel,
        name="write",
        grid=(PLANES // WRITE_PLANES,),
        out_shape=(
            jax.ShapeDtypeStruct((1, PLANES, TX, TY), f32),
            jax.ShapeDtypeStruct((1, 1, TX, TY), f32),
        ),
        in_specs=[vmem, vmem],
        out_specs=(
            pl.BlockSpec((1, WRITE_PLANES, TX, TY), lambda i: (0, i, 0, 0)),
            pl.BlockSpec((1, 1, TX, TY), lambda i: (0, 0, 0, 0)),
        ),
    )(volume, residual)


def solution(mesh):
    placed = (P("view", "tile", None, None), P("view", None, None), P("view", None, None))
    return jax.shard_map(
        functools.partial(local, mesh.shape["tile"] // GRID_Y),
        mesh=mesh,
        in_specs=placed,
        out_specs=(P("tile", None, None, None), P("view", "tile", None, None)),
        check_vma=False,
    )
```

```python
import functools

import jax
import jax.numpy as jnp
from jax import lax
from jax.experimental import pallas as pl
from jax.experimental.pallas import tpu as pltpu
from jax.sharding import PartitionSpec as P

PLANES = 16
VIEWS = 4
GRID_Y = 8
TX = 256
TY = 256
HX = 96
HY = 128
RX = TX + 2 * HX
RY = TY + 2 * HY
WINDOW = 288
STRIP = 160
WRITE_PLANES = 2
GROUP = 4
BAND = (
    (0, 0, 0, 128), (0, 1, 96, 32), (1, 1, 0, 96), (1, 2, 64, 64),
    (2, 2, 0, 64), (2, 3, 32, 96), (3, 3, 0, 32), (3, 4, 0, 128),
)
FAR = 1 << 20
TINY = 1e-6
MESH = pl.DeviceIdType.MESH

Z_BASE = 9
Y_BASE = Z_BASE + 2 * VIEWS
D_BASE = Y_BASE + 10 * VIEWS
N_SEMS = D_BASE + 4

PARTS = {
    "first": (HX, HX), "last": (TX, HX), "middle": (2 * HX, TX - 2 * HX),
    "top": (0, HX), "bottom": (HX + TX, HX),
}
PART_ID = {"first": 0, "last": 1, "middle": 2, "top": 3, "bottom": 4}


def ring(index, step, size):
    return lax.rem(index + (step + size), size)


def solve_kernel(
    grid_x,
    meas_hbm, sh_hbm, tp_hbm,
    vol_ref, res_ref,
    meas_ref, sh_ref, tp_ref, e_refs, f_refs, y_ref, x_ref, q_ref, p_ref, back_refs, by_ref, bx_ref, strip_refs,
    sh_v, tp_v, sh_s, tp_s, ra_ref, rb_ref, rc_ref,
    send_sems, recv_sems, p_send, p_recv, p_local, a_send, a_recv,
):
    tile = lax.axis_index("tile")
    view = lax.axis_index("view")
    gx = tile // GRID_Y
    gy = lax.rem(tile, GRID_Y)

    def at(row, col, vw):
        return (row * GRID_Y + col, vw)

    def to_view(step):
        return at(gx, gy, ring(view, step, VIEWS))

    def to_row(step):
        return at(ring(gx, step, grid_x), gy, view)

    def to_col(step):
        return at(gx, ring(gy, step, GRID_Y), view)

    def to_corner(row_step, col_step):
        return at(ring(gx, row_step, grid_x), ring(gy, col_step, GRID_Y), view)

    partners = (
        [to_view(s) for s in range(1, VIEWS)]
        + [to_row(s) for s in range(1, grid_x)]
        + [to_col(s) for s in range(1, GRID_Y)]
        + [to_corner(r, c) for r in (-1, 1) for c in (-1, 1)]
    )
    barrier = pltpu.get_barrier_semaphore()
    for partner in partners:
        pl.semaphore_signal(barrier, inc=1, device_id=partner, device_id_type=MESH)

    loading = [
        pltpu.make_async_copy(src.at[0], dst, p_local.at[k])
        for k, (src, dst) in enumerate(((meas_hbm.at[0], meas_ref), (sh_hbm, sh_ref), (tp_hbm, tp_ref)))
    ]
    for copy in loading:
        copy.start()
    for copy in loading:
        copy.wait()
    e_refs[0][pl.ds(HX, TX), pl.ds(HY, TY)] = meas_ref[...].astype(jnp.bfloat16)
    sh_v[0] = jnp.zeros((8, 128), jnp.int32)
    sh_v[0, 0:2, 0:PLANES] = sh_ref[...]
    tp_v[0] = jnp.zeros((8, 128), jnp.float32)
    tp_v[0, 0:4, 0:PLANES] = tp_ref[...].astype(jnp.float32)

    pl.semaphore_wait(barrier, len(partners))

    class Exchange:
        def __init__(self, bufs, which):
            self.bufs, self.which, self.copies = bufs, which, {}

        def send(self, key, sem, src, dst, device):
            copy = pltpu.make_async_remote_copy(
                src_ref=src, dst_ref=dst,
                send_sem=send_sems.at[self.which, sem], recv_sem=recv_sems.at[self.which, sem],
                device_id=device, device_id_type=MESH,
            )
            copy.start()
            self.copies[key] = copy

        def region(self, slot, rows, cols):
            return self.bufs[slot].at[pl.ds(*rows), pl.ds(*cols)]

        def along_view(self, src_slot, dst_slot, part, sem, step):
            rows = PARTS[part]
            self.send(
                ("x", dst_slot, part), sem,
                self.region(src_slot, rows, (HY, TY)), self.region(dst_slot, rows, (HY, TY)),
                to_view(step),
            )

        def along_views(self):
            self.along_view(0, 3, "first", 0, 1)
            self.along_view(0, 1, "last", 1, -1)
            self.along_view(0, 3, "last", 2, 1)
            self.along_view(0, 1, "first", 3, -1)
            self.along_view(0, 3, "middle", 4, 1)
            self.along_view(0, 1, "middle", 5, -1)

        def own(self):
            for part in ("first", "last", "middle"):
                self.spread(0, part)

        def columns(self, slot, part):
            rows = PARTS[part]
            sem = Y_BASE + 10 * slot + 2 * PART_ID[part]
            self.send(
                ("y", slot, part, 0), sem,
                self.region(slot, rows, (HY, HY)), self.region(slot, rows, (HY + TY, HY)), to_col(-1),
            )
            self.send(
                ("y", slot, part, 1), sem + 1,
                self.region(slot, rows, (TY, HY)), self.region(slot, rows, (0, HY)), to_col(1),
            )

        def spread(self, slot, part):
            for k, (rim, halo, step) in enumerate((("first", "bottom", -1), ("last", "top", 1))):
                if part == rim:
                    self.send(
                        ("z", slot, halo), Z_BASE + 2 * slot + k,
                        self.region(slot, PARTS[rim], (HY, TY)),
                        self.region(slot, PARTS[halo], (HY, TY)), to_row(step),
                    )
                    if slot == 2:
                        for side, (src, dst, turn) in enumerate(((HY, HY + TY, -1), (TY, 0, 1))):
                            self.send(
                                ("d", halo, side), D_BASE + 2 * k + side,
                                self.region(slot, PARTS[rim], (src, HY)),
                                self.region(slot, PARTS[halo], (dst, HY)), to_corner(step, turn),
                            )
            self.columns(slot, part)

        def arrive(self, slot, part):
            self.copies["x", slot, part].wait_recv()
            if slot == 3 and part == "first":
                self.along_view(3, 2, part, 6, 1)
            if slot == 1 and part == "last":
                self.along_view(1, 2, part, 7, -1)
            if slot == 3 and part == "middle":
                self.along_view(3, 2, part, 8, 1)
            self.spread(slot, part)

        def corners(self, slot):
            for part, edge in (("top", 0), ("bottom", grid_x - 1)):
                self.copies["z", slot, part].wait_recv()

                @pl.when(gx == edge)
                def _():
                    start, size = PARTS[part]
                    self.bufs[slot][pl.ds(start, size), pl.ds(HY, TY)] = jnp.zeros((size, TY), jnp.bfloat16)

                self.columns(slot, part)

        def complete(self, slot):
            if slot == 2:
                for halo in ("top", "bottom"):
                    self.copies["z", slot, halo].wait_recv()
                    for side in (0, 1):
                        self.copies["d", halo, side].wait_recv()
                for halo, edge in (("top", 0), ("bottom", grid_x - 1)):
                    @pl.when(gx == edge)
                    def _():
                        start, size = PARTS[halo]
                        self.bufs[slot][pl.ds(start, size), :] = jnp.zeros((size, RY), jnp.bfloat16)
            for part in PARTS:
                for side in (0, 1):
                    if ("y", slot, part, side) in self.copies:
                        self.copies["y", slot, part, side].wait_recv()
            for side, edge in ((0, 0), (HY + TY, GRID_Y - 1)):
                @pl.when(gy == edge)
                def _():
                    self.bufs[slot][:, pl.ds(side, HY)] = jnp.zeros((RX, HY), jnp.bfloat16)

        def finish(self):
            for copy in self.copies.values():
                copy.wait_send()

    first = Exchange(e_refs, 0)

    parameter_copies = []
    for step in range(1, VIEWS):
        slot = VIEWS - step
        for which, ref in ((0, sh_v), (1, tp_v)):
            copy = pltpu.make_async_remote_copy(
                src_ref=ref.at[0], dst_ref=ref.at[slot],
                send_sem=p_send.at[which, slot], recv_sem=p_recv.at[which, slot],
                device_id=to_view(step), device_id_type=MESH,
            )
            copy.start()
            parameter_copies.append(copy)

    first.along_views()

    def tables(first_slot, count):
        local = [
            pltpu.make_async_copy(src.at[pl.ds(first_slot, count)], dst.at[pl.ds(first_slot, count)], p_local.at[k])
            for k, (src, dst) in enumerate(((sh_v, sh_s), (tp_v, tp_s)))
        ]
        for copy in local:
            copy.start()
        for copy in local:
            copy.wait()

    first.own()
    tables(0, 1)

    column_low = jnp.where(gy == 0, 0, -FAR)
    column_high = jnp.where(gy == GRID_Y - 1, TY, FAR)
    row_low = jnp.where(gx == 0, 0, -FAR)
    row_high = jnp.where(gx == grid_x - 1, TX, FAR)

    row16 = lax.broadcasted_iota(jnp.int32, (16, 128), 0)
    col16 = lax.broadcasted_iota(jnp.int32, (16, 128), 1)
    below = (row16 - col16).astype(jnp.int16)
    beyond = (col16 - row16).astype(jnp.int16)

    def spread16(x):
        return jnp.full((16, 128), x, jnp.int32).astype(jnp.int16)

    def narrow(weights):
        return [jnp.broadcast_to(w, (16, 128)).astype(jnp.bfloat16) for w in weights]

    def band(distance, first, weights):
        value = jnp.zeros((16, 128), jnp.bfloat16)
        for at, weight in zip(first, weights):
            value = jnp.where(distance == at, weight, value)
        return value

    def build(slot):
        def one(z, carry):
            pair = slot * PLANES + z
            y_ref[pair, 0:32, 0:128] = jnp.zeros((32, 128), jnp.bfloat16)
            y_ref[pair, 352:512, 0:128] = jnp.zeros((160, 128), jnp.bfloat16)
            y_ref[pair, 0:160, 128:256] = jnp.zeros((160, 128), jnp.bfloat16)
            y_ref[pair, 480:512, 128:256] = jnp.zeros((32, 128), jnp.bfloat16)
            shear = sh_s[0, 1, z]
            first = [spread16(sh_s[slot, 1, z] - shear + (HY - 32 + k)) for k in (-1, 0, 1)]
            a0, a1 = tp_s[0, 2, z], tp_s[0, 3, z]
            b0, b1 = tp_s[slot, 2, z], tp_s[slot, 3, z]
            low, high = shear + column_low, shear + column_high
            weights = []
            for in0, in1 in (
                (col16 >= low, col16 >= low - 1),
                (col16 + 128 < high, col16 + 128 < high - 1),
            ):
                weights.append(narrow((
                    jnp.where(in0, a0 * b1, 0.0),
                    jnp.where(in0, a0 * b0, 0.0) + jnp.where(in1, a1 * b1, 0.0),
                    jnp.where(in1, a1 * b0, 0.0),
                )))
            for r in range(0, 320, 16):
                distance = below + jnp.int16(r)
                y_ref[pair, pl.ds(32 + r, 16), 0:128] = band(distance, first, weights[0])
                y_ref[pair, pl.ds(160 + r, 16), 128:256] = band(distance, first, weights[1])
            return carry

        lax.fori_loop(0, PLANES, one, 0)

    def build_rows(slot):
        def one(g, carry):
            scalars = []
            for u in range(GROUP):
                z = GROUP * g + u
                shear = sh_s[0, 0, z]
                first_row = HX - 1 + sh_s[slot, 0, z] - shear
                m = first_row - lax.shift_right_logical(first_row, 4) * 16 + STRIP * u
                a0, a1 = tp_s[0, 0, z] * (1.0 / PLANES), tp_s[0, 1, z] * (1.0 / PLANES)
                b0, b1 = tp_s[slot, 0, z], tp_s[slot, 1, z]
                scalars.append((m, a0 * b1, a0 * b0, a1 * b1, a1 * b0, shear + row_low, shear + row_high))
            for u, block, row_start, size in BAND:
                m, am, az, bz, bp, low, high = scalars[u]
                plain = narrow((am, az + bz, bp))
                first = [spread16(m + k) for k in (0, 1, 2)]
                for r in range(row_start, row_start + size, 16):
                    distance = beyond + jnp.int16(128 * block - r)
                    for half in (0, 1):
                        weights = plain
                        if (half == 0 and r < 48) or (half == 1 and r >= 80):
                            row = row16 + (r + 128 * half)
                            in0, in1 = (row >= low, row >= low - 1) if half == 0 else (row < high, row < high - 1)
                            weights = narrow((
                                jnp.where(in0, am, 0.0),
                                jnp.where(in0, az, 0.0) + jnp.where(in1, bz, 0.0),
                                jnp.where(in1, bp, 0.0),
                            ))
                        x_ref[slot, half, g, pl.ds(r, 16), pl.ds(128 * block, 128)] = band(distance, first, weights)
            return carry

        lax.fori_loop(0, PLANES // GROUP, one, 0)

    def apply(src_ref, out_ref, slot):
        for z in range(PLANES):
            first_row = HX - 1 + sh_s[slot, 0, z] - sh_s[0, 0, z]
            start = lax.shift_right_logical(first_row, 4) * 16
            t = jnp.dot(
                src_ref[pl.ds(start, WINDOW), :], y_ref[slot * PLANES + z], preferred_element_type=jnp.float32
            ).astype(jnp.bfloat16)
            strip = pl.ds(STRIP * (z % GROUP), STRIP)
            strip_refs[0][z // GROUP, strip, :] = t[0:STRIP]
            strip_refs[1][z // GROUP, strip, :] = t[128 : 128 + STRIP]
        for half, t_ref in enumerate(strip_refs[0:2]):
            total = out_ref[pl.ds(128 * half, 128), :]
            for g in range(PLANES // GROUP):
                total = total + jnp.dot(
                    x_ref[slot, half, g],
                    t_ref[g],
                    preferred_element_type=jnp.float32,
                )
            out_ref[pl.ds(128 * half, 128), :] = total

    def lanes(x):
        s = jnp.sum(x, axis=0, keepdims=True)
        return s[:, 0:128] + s[:, 128:256]

    class Sum:
        def __init__(self, rows):
            self.stages = (
                (ra_ref, view, VIEWS, to_view, 0),
                (rb_ref, gy, GRID_Y, to_col, VIEWS),
                (rc_ref, gx, grid_x, to_row, VIEWS + GRID_Y),
            )
            self.copies = []
            pad = jnp.zeros((8 - len(rows), 128), jnp.float32)
            self.value = jnp.concatenate(list(rows) + [pad], axis=0)

        def send(self, stage):
            ref, me, size, to, base = self.stages[stage]
            ref[me] = self.value
            self.current = []
            for step in sorted(range(1, size), key=lambda k: -min(k, size - k)):
                copy = pltpu.make_async_remote_copy(
                    src_ref=ref.at[me], dst_ref=ref.at[me],
                    send_sem=a_send.at[base + step], recv_sem=a_recv.at[base + step],
                    device_id=to(step), device_id_type=MESH,
                )
                copy.start()
                self.current.append(copy)
            self.copies += self.current

        def receive(self, stage):
            ref, me, size, to, base = self.stages[stage]
            for copy in self.current:
                copy.wait_recv()
            total = ref[0]
            for i in range(1, size):
                total = total + ref[i]
            self.value = total

        def row(self, i):
            return jnp.sum(self.value[i : i + 1, :], axis=1, keepdims=True)

        def finish(self):
            for copy in self.copies:
                copy.wait_send()

    by_ref[...] = jnp.zeros(by_ref.shape, jnp.bfloat16)

    def back(chunk, sources):
        refs = [(e_refs, f_refs)[k] for k in sources]
        for u in range(GROUP):
            z = GROUP * chunk + u
            for slot in range(VIEWS):
                place = lax.rem(view + slot, VIEWS)
                d = sh_s[slot, 1, z]
                weights = narrow((tp_s[slot, 3, z], tp_s[slot, 2, z]))
                at = [spread16(d + (HY - 80 + k)) for k in (-1, 0)]
                pair = VIEWS * u + slot
                for r in range(0, 224, 16):
                    value = band(below + jnp.int16(r), at, weights)
                    by_ref[pair, pl.ds(80 + r, 16), 0:128] = value
                    by_ref[pair, pl.ds(208 + r, 16), 128:256] = value
                start = lax.shift_right_logical(HX - 1 + sh_s[slot, 0, z], 4) * 16
                rows = [ref[slot][pl.ds(start, WINDOW), :] for ref in refs]
                t = jnp.dot(
                    jnp.concatenate(rows, axis=0) if len(rows) > 1 else rows[0],
                    by_ref[pair], preferred_element_type=jnp.float32,
                ).astype(jnp.bfloat16)
                for k in range(2 * len(refs)):
                    first = WINDOW * (k // 2) + 128 * (k % 2)
                    strip_refs[k][u, pl.ds(STRIP * place, STRIP), :] = t[first : first + STRIP]
            for v, block, row_start, size in BAND:
                slot = lax.rem(v - view + VIEWS, VIEWS)
                first_row = HX - 1 + sh_s[slot, 0, z]
                m = first_row - lax.shift_right_logical(first_row, 4) * 16 + STRIP * v
                weights = narrow((tp_s[slot, 1, z] * (PLANES**-0.5), tp_s[slot, 0, z] * (PLANES**-0.5)))
                at = [spread16(m + k) for k in (0, 1)]
                for r in range(row_start, row_start + size, 16):
                    bx_ref[u, pl.ds(r, 16), pl.ds(128 * block, 128)] = band(
                        beyond + jnp.int16(128 * block - r), at, weights
                    )
        for u in range(GROUP):
            z = GROUP * chunk + u
            for k in range(2 * len(refs)):
                back_refs[sources[k // 2]][z, pl.ds(128 * (k % 2), 128), :] = jnp.dot(
                    bx_ref[u], strip_refs[k][u], preferred_element_type=jnp.float32
                )

    q_ref[...] = jnp.zeros((TX, TY), jnp.float32)
    p_ref[...] = jnp.zeros((TX, TY), jnp.float32)

    build(0)
    build_rows(0)
    for copy in parameter_copies:
        copy.wait_recv()
    tables(1, VIEWS - 1)
    first.corners(0)
    first.arrive(3, "first")
    first.arrive(1, "last")
    build(3)
    build_rows(3)
    first.arrive(3, "last")
    first.arrive(1, "first")
    first.arrive(3, "middle")
    first.arrive(1, "middle")
    first.complete(0)
    apply(e_refs[0], q_ref, 0)
    first.arrive(2, "first")
    first.arrive(2, "last")
    first.arrive(2, "middle")
    first.corners(3)
    first.corners(1)
    build(1)
    build_rows(1)
    build(2)
    build_rows(2)
    for slot in (3, 1, 2):
        first.complete(slot)
        apply(e_refs[slot], q_ref, slot)

    second = Exchange(f_refs, 1)
    f_refs[0][pl.ds(HX, TX), pl.ds(HY, TY)] = q_ref[...].astype(jnp.bfloat16)
    second.along_views()
    second.own()
    back(0, (0,))
    second.corners(0)
    for part in ("first", "last", "middle"):
        second.arrive(3, part)
        second.arrive(1, {"first": "last", "last": "first", "middle": "middle"}[part])
    second.complete(0)
    apply(f_refs[0], p_ref, 0)
    second.arrive(2, "first")
    second.arrive(2, "last")
    second.corners(3)
    second.corners(1)
    second.arrive(2, "middle")
    back(1, (0,))
    for slot in (3, 1, 2):
        second.complete(slot)
        apply(f_refs[slot], p_ref, slot)

    r0 = e_refs[0][pl.ds(HX, TX), pl.ds(HY, TY)].astype(jnp.float32)
    q0, p = q_ref[...], p_ref[...]
    sums = Sum([lanes(r0 * q0), lanes(q0 * q0), lanes(r0 * p), lanes(q0 * p), lanes(p * p)])
    sums.send(0)
    back(2, (0, 1))
    sums.receive(0)
    sums.send(1)
    back(3, (0, 1))
    sums.receive(1)
    sums.send(2)
    back(0, (1,))
    back(1, (1,))
    sums.receive(2)
    r0q0, q0q0, r0p, q0p, pp = [sums.row(i) for i in range(5)]
    gamma0 = r0q0
    alpha0 = gamma0 / (q0q0 + TINY)
    gamma1 = r0q0 - alpha0 * (r0p + q0q0) + alpha0 * alpha0 * q0p
    beta = gamma1 / (gamma0 + TINY)
    h1h1 = q0q0 - 2.0 * alpha0 * q0p + alpha0 * alpha0 * pp
    h1q0 = q0q0 - alpha0 * q0p
    alpha1 = gamma1 / (h1h1 + 2.0 * beta * h1q0 + beta * beta * q0q0 + TINY)

    weight0 = alpha0 + alpha1 * beta + alpha1
    weight1 = alpha1 * alpha0

    def combine(z, carry):
        vol_ref[0, z] = (weight0 * back_refs[0][z] - weight1 * back_refs[1][z]).astype(jnp.bfloat16)
        return carry

    lax.fori_loop(0, PLANES, combine, 0)
    q0, p = q_ref[...], p_ref[...]
    res_ref[0, 0] = meas_ref[...] - alpha0 * q0 - alpha1 * ((q0 - alpha0 * p) + beta * q0)

    for copy in parameter_copies:
        copy.wait_send()
    first.finish()
    second.finish()
    sums.finish()


def write_kernel(vol_ref, res_ref, vol_out, res_out):
    step = pl.program_id(0)
    planes = pl.ds(step * WRITE_PLANES, WRITE_PLANES)
    vol_out[0] = vol_ref[0, planes].astype(jnp.float32)

    @pl.when(step == 0)
    def _():
        res_out[...] = res_ref[...]


def local(grid_x, measured, shears, taps):
    f32, bf16 = jnp.float32, jnp.bfloat16
    vmem = pl.BlockSpec(memory_space=pltpu.VMEM)
    partners = VIEWS + GRID_Y + grid_x
    hbm = pl.BlockSpec(memory_space=pltpu.HBM)
    volume, residual = pl.pallas_call(
        functools.partial(solve_kernel, grid_x),
        name="solve",
        out_shape=(
            jax.ShapeDtypeStruct((1, PLANES, TX, TY), bf16),
            jax.ShapeDtypeStruct((1, 1, TX, TY), f32),
        ),
        in_specs=[hbm, hbm, hbm],
        out_specs=(vmem, vmem),
        scratch_shapes=[
            pltpu.VMEM((TX, TY), f32),
            pltpu.VMEM((2, PLANES), jnp.int32),
            pltpu.VMEM((4, PLANES), bf16),
            [pltpu.VMEM((RX, RY), bf16)] * VIEWS,
            [pltpu.VMEM((RX, RY), bf16)] * VIEWS,
            pltpu.VMEM((VIEWS * PLANES, RY, TY), bf16),
            pltpu.VMEM((VIEWS, 2, PLANES // GROUP, 128, GROUP * STRIP), bf16),
            pltpu.VMEM((TX, TY), f32),
            pltpu.VMEM((TX, TY), f32),
            [pltpu.VMEM((PLANES, TX, TY), f32)] * 2,
            pltpu.VMEM((GROUP * VIEWS, RY, TY), bf16),
            pltpu.VMEM((GROUP, 128, VIEWS * STRIP), bf16),
            [pltpu.VMEM((GROUP, VIEWS * STRIP, TY), bf16)] * 4,
            pltpu.VMEM((VIEWS, 8, 128), jnp.int32),
            pltpu.VMEM((VIEWS, 8, 128), f32),
            pltpu.SMEM((VIEWS, 8, 128), jnp.int32),
            pltpu.SMEM((VIEWS, 8, 128), f32),
            pltpu.VMEM((VIEWS, 8, 128), f32),
            pltpu.VMEM((GRID_Y, 8, 128), f32),
            pltpu.VMEM((grid_x, 8, 128), f32),
            pltpu.SemaphoreType.DMA((2, N_SEMS)),
            pltpu.SemaphoreType.DMA((2, N_SEMS)),
            pltpu.SemaphoreType.DMA((2, VIEWS)),
            pltpu.SemaphoreType.DMA((2, VIEWS)),
            pltpu.SemaphoreType.DMA((3,)),
            pltpu.SemaphoreType.DMA((partners,)),
            pltpu.SemaphoreType.DMA((partners,)),
        ],
        compiler_params=pltpu.CompilerParams(
            collective_id=0, has_side_effects=True, vmem_limit_bytes=50 * 1024 * 1024
        ),
    )(measured, jnp.transpose(shears, (0, 2, 1)), jnp.transpose(taps, (0, 2, 1)))
    return pl.pallas_call(
        write_kernel,
        name="write",
        grid=(PLANES // WRITE_PLANES,),
        out_shape=(
            jax.ShapeDtypeStruct((1, PLANES, TX, TY), f32),
            jax.ShapeDtypeStruct((1, 1, TX, TY), f32),
        ),
        in_specs=[vmem, vmem],
        out_specs=(
            pl.BlockSpec((1, WRITE_PLANES, TX, TY), lambda i: (0, i, 0, 0)),
            pl.BlockSpec((1, 1, TX, TY), lambda i: (0, 0, 0, 0)),
        ),
        compiler_params=pltpu.CompilerParams(vmem_limit_bytes=16 * 1024 * 1024),
    )(volume, residual)


def solution(mesh):
    placed = (P("view", "tile", None, None), P("view", None, None), P("view", None, None))
    return jax.shard_map(
        functools.partial(local, mesh.shape["tile"] // GRID_Y),
        mesh=mesh,
        in_specs=placed,
        out_specs=(P("tile", None, None, None), P("view", "tile", None, None)),
        check_vma=False,
    )
```

```python
import functools

import jax
import jax.numpy as jnp
from jax import lax
from jax.experimental import pallas as pl
from jax.experimental.pallas import tpu as pltpu
from jax.sharding import PartitionSpec as P

PLANES = 16
VIEWS = 4
GRID_Y = 8
TX = 256
TY = 256
HX = 96
HY = 128
RX = TX + 2 * HX
RY = TY + 2 * HY
WINDOW = 288
STRIP = 160
GROUP = 4
BAND = (
    (0, 0, 0, 128), (0, 1, 96, 32), (1, 1, 0, 96), (1, 2, 64, 64),
    (2, 2, 0, 64), (2, 3, 32, 96), (3, 3, 0, 32), (3, 4, 0, 128),
)
FAR = 1 << 20
TINY = 1e-6
MESH = pl.DeviceIdType.MESH

Z_BASE = 9
Y_BASE = Z_BASE + 2 * VIEWS
D_BASE = Y_BASE + 10 * VIEWS
N_SEMS = D_BASE + 4

PARTS = {
    "first": (HX, HX), "last": (TX, HX), "middle": (2 * HX, TX - 2 * HX),
    "top": (0, HX), "bottom": (HX + TX, HX),
}
PART_ID = {"first": 0, "last": 1, "middle": 2, "top": 3, "bottom": 4}


def ring(index, step, size):
    return lax.rem(index + (step + size), size)


def solve_kernel(
    grid_x,
    meas_hbm, sh_hbm, tp_hbm,
    vol_ref, res_ref,
    meas_ref, sh_ref, tp_ref, e_refs, f_refs, field_ref, y_ref, x_ref, q_ref, p_ref, back_refs, by_ref, bx_ref, strip_refs,
    sh_v, tp_v, sh_s, tp_s, ra_ref, rb_ref, rc_ref,
    send_sems, recv_sems, p_send, p_recv, p_local, a_send, a_recv,
):
    tile = lax.axis_index("tile")
    view = lax.axis_index("view")
    gx = tile // GRID_Y
    gy = lax.rem(tile, GRID_Y)

    def at(row, col, vw):
        return (row * GRID_Y + col, vw)

    def to_view(step):
        return at(gx, gy, ring(view, step, VIEWS))

    def to_row(step):
        return at(ring(gx, step, grid_x), gy, view)

    def to_col(step):
        return at(gx, ring(gy, step, GRID_Y), view)

    def to_corner(row_step, col_step):
        return at(ring(gx, row_step, grid_x), ring(gy, col_step, GRID_Y), view)

    partners = (
        [to_view(s) for s in range(1, VIEWS)]
        + [to_row(s) for s in range(1, grid_x)]
        + [to_col(s) for s in range(1, GRID_Y)]
        + [to_corner(r, c) for r in (-1, 1) for c in (-1, 1)]
    )
    barrier = pltpu.get_barrier_semaphore()
    for partner in partners:
        pl.semaphore_signal(barrier, inc=1, device_id=partner, device_id_type=MESH)

    loading = [
        pltpu.make_async_copy(src.at[0], dst, p_local.at[k])
        for k, (src, dst) in enumerate(((meas_hbm.at[0], meas_ref), (sh_hbm, sh_ref), (tp_hbm, tp_ref)))
    ]
    for copy in loading:
        copy.start()
    for copy in loading:
        copy.wait()
    e_refs[0][pl.ds(HX, TX), pl.ds(HY, TY)] = meas_ref[...].astype(jnp.bfloat16)
    sh_v[0] = jnp.zeros((8, 128), jnp.int32)
    sh_v[0, 0:2, 0:PLANES] = sh_ref[...]
    tp_v[0] = jnp.zeros((8, 128), jnp.float32)
    tp_v[0, 0:4, 0:PLANES] = tp_ref[...].astype(jnp.float32)

    pl.semaphore_wait(barrier, len(partners))

    class Exchange:
        def __init__(self, bufs, which):
            self.bufs, self.which, self.copies = bufs, which, {}

        def send(self, key, sem, src, dst, device):
            copy = pltpu.make_async_remote_copy(
                src_ref=src, dst_ref=dst,
                send_sem=send_sems.at[self.which, sem], recv_sem=recv_sems.at[self.which, sem],
                device_id=device, device_id_type=MESH,
            )
            copy.start()
            self.copies[key] = copy

        def region(self, slot, rows, cols):
            return self.bufs[slot].at[pl.ds(*rows), pl.ds(*cols)]

        def along_view(self, src_slot, dst_slot, part, sem, step):
            rows = PARTS[part]
            self.send(
                ("x", dst_slot, part), sem,
                self.region(src_slot, rows, (HY, TY)), self.region(dst_slot, rows, (HY, TY)),
                to_view(step),
            )

        def along_views(self):
            self.along_view(0, 3, "first", 0, 1)
            self.along_view(0, 1, "last", 1, -1)
            self.along_view(0, 3, "last", 2, 1)
            self.along_view(0, 1, "first", 3, -1)
            self.along_view(0, 3, "middle", 4, 1)
            self.along_view(0, 1, "middle", 5, -1)

        def own(self):
            for part in ("first", "last", "middle"):
                self.spread(0, part)

        def columns(self, slot, part):
            rows = PARTS[part]
            sem = Y_BASE + 10 * slot + 2 * PART_ID[part]
            self.send(
                ("y", slot, part, 0), sem,
                self.region(slot, rows, (HY, HY)), self.region(slot, rows, (HY + TY, HY)), to_col(-1),
            )
            self.send(
                ("y", slot, part, 1), sem + 1,
                self.region(slot, rows, (TY, HY)), self.region(slot, rows, (0, HY)), to_col(1),
            )

        def spread(self, slot, part):
            for k, (rim, halo, step) in enumerate((("first", "bottom", -1), ("last", "top", 1))):
                if part == rim:
                    self.send(
                        ("z", slot, halo), Z_BASE + 2 * slot + k,
                        self.region(slot, PARTS[rim], (HY, TY)),
                        self.region(slot, PARTS[halo], (HY, TY)), to_row(step),
                    )
                    if slot == 2:
                        for side, (src, dst, turn) in enumerate(((HY, HY + TY, -1), (TY, 0, 1))):
                            self.send(
                                ("d", halo, side), D_BASE + 2 * k + side,
                                self.region(slot, PARTS[rim], (src, HY)),
                                self.region(slot, PARTS[halo], (dst, HY)), to_corner(step, turn),
                            )
            self.columns(slot, part)

        def arrive(self, slot, part):
            self.copies["x", slot, part].wait_recv()
            if slot == 3 and part == "first":
                self.along_view(3, 2, part, 6, 1)
            if slot == 1 and part == "last":
                self.along_view(1, 2, part, 7, -1)
            if slot == 3 and part == "middle":
                self.along_view(3, 2, part, 8, 1)
            self.spread(slot, part)

        def corners(self, slot):
            for part, edge in (("top", 0), ("bottom", grid_x - 1)):
                self.copies["z", slot, part].wait_recv()

                @pl.when(gx == edge)
                def _():
                    start, size = PARTS[part]
                    self.bufs[slot][pl.ds(start, size), pl.ds(HY, TY)] = jnp.zeros((size, TY), jnp.bfloat16)

                self.columns(slot, part)

        def complete(self, slot):
            if slot == 2:
                for halo in ("top", "bottom"):
                    self.copies["z", slot, halo].wait_recv()
                    for side in (0, 1):
                        self.copies["d", halo, side].wait_recv()
                for halo, edge in (("top", 0), ("bottom", grid_x - 1)):
                    @pl.when(gx == edge)
                    def _():
                        start, size = PARTS[halo]
                        self.bufs[slot][pl.ds(start, size), :] = jnp.zeros((size, RY), jnp.bfloat16)
            for part in PARTS:
                for side in (0, 1):
                    if ("y", slot, part, side) in self.copies:
                        self.copies["y", slot, part, side].wait_recv()
            for side, edge in ((0, 0), (HY + TY, GRID_Y - 1)):
                @pl.when(gy == edge)
                def _():
                    self.bufs[slot][:, pl.ds(side, HY)] = jnp.zeros((RX, HY), jnp.bfloat16)

        def finish(self):
            for copy in self.copies.values():
                copy.wait_send()

    first = Exchange(e_refs, 0)

    parameter_copies = []
    for step in range(1, VIEWS):
        slot = VIEWS - step
        for which, ref in ((0, sh_v), (1, tp_v)):
            copy = pltpu.make_async_remote_copy(
                src_ref=ref.at[0], dst_ref=ref.at[slot],
                send_sem=p_send.at[which, slot], recv_sem=p_recv.at[which, slot],
                device_id=to_view(step), device_id_type=MESH,
            )
            copy.start()
            parameter_copies.append(copy)

    first.along_views()

    def tables(first_slot, count):
        local = [
            pltpu.make_async_copy(src.at[pl.ds(first_slot, count)], dst.at[pl.ds(first_slot, count)], p_local.at[k])
            for k, (src, dst) in enumerate(((sh_v, sh_s), (tp_v, tp_s)))
        ]
        for copy in local:
            copy.start()
        for copy in local:
            copy.wait()

    first.own()

    column_low = jnp.where(gy == 0, 0, -FAR)
    column_high = jnp.where(gy == GRID_Y - 1, TY, FAR)
    row_low = jnp.where(gx == 0, 0, -FAR)
    row_high = jnp.where(gx == grid_x - 1, TX, FAR)

    row16 = lax.broadcasted_iota(jnp.int32, (16, 128), 0)
    col16 = lax.broadcasted_iota(jnp.int32, (16, 128), 1)
    below = (row16 - col16).astype(jnp.int16)
    beyond = (col16 - row16).astype(jnp.int16)

    def spread16(x):
        return jnp.full((16, 128), x, jnp.int32).astype(jnp.int16)

    def narrow(weights):
        return [jnp.broadcast_to(w, (16, 128)).astype(jnp.bfloat16) for w in weights]

    def band(distance, first, weights):
        value = jnp.zeros((16, 128), jnp.bfloat16)
        for at, weight in zip(first, weights):
            value = jnp.where(distance == at, weight, value)
        return value

    def build(slot):
        def one(z, carry):
            pair = (slot - 1) * PLANES + z
            y_ref[pair, 0:32, 0:128] = jnp.zeros((32, 128), jnp.bfloat16)
            y_ref[pair, 352:512, 0:128] = jnp.zeros((160, 128), jnp.bfloat16)
            y_ref[pair, 0:160, 128:256] = jnp.zeros((160, 128), jnp.bfloat16)
            y_ref[pair, 480:512, 128:256] = jnp.zeros((32, 128), jnp.bfloat16)
            shear = sh_s[0, 1, z]
            first = [spread16(sh_s[slot, 1, z] - shear + (HY - 32 + k)) for k in (-1, 0, 1)]
            a0, a1 = tp_s[0, 2, z], tp_s[0, 3, z]
            b0, b1 = tp_s[slot, 2, z], tp_s[slot, 3, z]
            low, high = shear + column_low, shear + column_high
            weights = []
            for in0, in1 in (
                (col16 >= low, col16 >= low - 1),
                (col16 + 128 < high, col16 + 128 < high - 1),
            ):
                weights.append(narrow((
                    jnp.where(in0, a0 * b1, 0.0),
                    jnp.where(in0, a0 * b0, 0.0) + jnp.where(in1, a1 * b1, 0.0),
                    jnp.where(in1, a1 * b0, 0.0),
                )))
            for r in range(0, 320, 16):
                distance = below + jnp.int16(r)
                y_ref[pair, pl.ds(32 + r, 16), 0:128] = band(distance, first, weights[0])
                y_ref[pair, pl.ds(160 + r, 16), 128:256] = band(distance, first, weights[1])
            return carry

        lax.fori_loop(0, PLANES, one, 0)

    def build_rows(slot):
        def one(g, carry):
            scalars = []
            for u in range(GROUP):
                z = GROUP * g + u
                shear = sh_s[0, 0, z]
                first_row = HX - 1 + sh_s[slot, 0, z] - shear
                m = first_row - lax.shift_right_logical(first_row, 4) * 16 + STRIP * u
                a0, a1 = tp_s[0, 0, z] * (1.0 / PLANES), tp_s[0, 1, z] * (1.0 / PLANES)
                b0, b1 = tp_s[slot, 0, z], tp_s[slot, 1, z]
                scalars.append((m, a0 * b1, a0 * b0, a1 * b1, a1 * b0, shear + row_low, shear + row_high))
            for u, block, row_start, size in BAND:
                m, am, az, bz, bp, low, high = scalars[u]
                plain = narrow((am, az + bz, bp))
                first = [spread16(m + k) for k in (0, 1, 2)]
                for r in range(row_start, row_start + size, 16):
                    distance = beyond + jnp.int16(128 * block - r)
                    for half in (0, 1):
                        weights = plain
                        if (half == 0 and r < 48) or (half == 1 and r >= 80):
                            row = row16 + (r + 128 * half)
                            in0, in1 = (row >= low, row >= low - 1) if half == 0 else (row < high, row < high - 1)
                            weights = narrow((
                                jnp.where(in0, am, 0.0),
                                jnp.where(in0, az, 0.0) + jnp.where(in1, bz, 0.0),
                                jnp.where(in1, bp, 0.0),
                            ))
                        x_ref[slot - 1, half, g, pl.ds(r, 16), pl.ds(128 * block, 128)] = band(distance, first, weights)
            return carry

        lax.fori_loop(0, PLANES // GROUP, one, 0)

    def fields():
        row = lax.broadcasted_iota(jnp.int32, (TX, 128), 0)

        def factors(shear, w0, w1, low, high, scale):
            in0 = (row >= shear + low) & (row < shear + high)
            in1 = (row >= shear + low - 1) & (row < shear + high - 1)
            cross = w0 * w1 * scale
            return jnp.concatenate([
                jnp.where(in0, cross, 0.0),
                jnp.where(in0, w0 * w0 * scale, 0.0) + jnp.where(in1, w1 * w1 * scale, 0.0),
                jnp.where(in1, cross, 0.0),
            ], axis=0).astype(jnp.bfloat16)

        along_x = factors(sh_v[0, 0:1, :], tp_v[0, 0:1, :], tp_v[0, 1:2, :], row_low, row_high, 1.0 / PLANES)
        along_y = factors(sh_v[0, 1:2, :], tp_v[0, 2:3, :], tp_v[0, 3:4, :], column_low, column_high, 1.0)
        field_ref[...] = lax.dot_general(
            along_x, along_y, (((1,), (1,)), ((), ())), preferred_element_type=jnp.float32
        )

    def stencil(src_ref, out_ref):
        def rows(i, carry):
            start = i * 64
            x = src_ref[pl.ds(pl.multiple_of(HX - 16 + start, 16), 96), :].astype(jnp.float32)
            total = jnp.zeros((64, TY), jnp.float32)
            for l in range(3):
                shifted = pltpu.roll(x, (RY + 1 - l) % RY, 1)[:, HY : HY + TY]
                for k in range(3):
                    term = pltpu.roll(shifted, (96 + 1 - k) % 96, 0)[16:80]
                    total = total + term * field_ref[pl.ds(pl.multiple_of(TX * k + start, 64), 64), TY * l : TY * (l + 1)]
            out_ref[pl.ds(pl.multiple_of(start, 64), 64), :] = total
            return carry

        lax.fori_loop(0, TX // 64, rows, 0)

    def apply(src_ref, out_ref, slot):
        for z in range(PLANES):
            first_row = HX - 1 + sh_s[slot, 0, z] - sh_s[0, 0, z]
            start = lax.shift_right_logical(first_row, 4) * 16
            t = jnp.dot(
                src_ref[pl.ds(start, WINDOW), :], y_ref[(slot - 1) * PLANES + z], preferred_element_type=jnp.float32
            ).astype(jnp.bfloat16)
            strip = pl.ds(STRIP * (z % GROUP), STRIP)
            strip_refs[0][z // GROUP, strip, :] = t[0:STRIP]
            strip_refs[1][z // GROUP, strip, :] = t[128 : 128 + STRIP]
        for half, t_ref in enumerate(strip_refs[0:2]):
            total = out_ref[pl.ds(128 * half, 128), :]
            for g in range(PLANES // GROUP):
                total = total + jnp.dot(
                    x_ref[slot - 1, half, g],
                    t_ref[g],
                    preferred_element_type=jnp.float32,
                )
            out_ref[pl.ds(128 * half, 128), :] = total

    def lanes(x):
        s = jnp.sum(x, axis=0, keepdims=True)
        return s[:, 0:128] + s[:, 128:256]

    class Sum:
        def __init__(self, rows):
            self.stages = (
                (ra_ref, view, VIEWS, to_view, 0),
                (rb_ref, gy, GRID_Y, to_col, VIEWS),
                (rc_ref, gx, grid_x, to_row, VIEWS + GRID_Y),
            )
            self.copies = []
            pad = jnp.zeros((8 - len(rows), 128), jnp.float32)
            self.value = jnp.concatenate(list(rows) + [pad], axis=0)

        def send(self, stage):
            ref, me, size, to, base = self.stages[stage]
            ref[me] = self.value
            self.current = []
            for step in sorted(range(1, size), key=lambda k: -min(k, size - k)):
                copy = pltpu.make_async_remote_copy(
                    src_ref=ref.at[me], dst_ref=ref.at[me],
                    send_sem=a_send.at[base + step], recv_sem=a_recv.at[base + step],
                    device_id=to(step), device_id_type=MESH,
                )
                copy.start()
                self.current.append(copy)
            self.copies += self.current

        def receive(self, stage):
            ref, me, size, to, base = self.stages[stage]
            for copy in self.current:
                copy.wait_recv()
            total = ref[0]
            for i in range(1, size):
                total = total + ref[i]
            self.value = total

        def row(self, i):
            return jnp.sum(self.value[i : i + 1, :], axis=1, keepdims=True)

        def finish(self):
            for copy in self.copies:
                copy.wait_send()

    by_ref[...] = jnp.zeros(by_ref.shape, jnp.bfloat16)

    def back(chunk, sources):
        refs = [(e_refs, f_refs)[k] for k in sources]
        for u in range(GROUP):
            z = GROUP * chunk + u
            for slot in range(VIEWS):
                place = lax.rem(view + slot, VIEWS)
                d = sh_s[slot, 1, z]
                weights = narrow((tp_s[slot, 3, z], tp_s[slot, 2, z]))
                at = [spread16(d + (HY - 80 + k)) for k in (-1, 0)]
                pair = VIEWS * u + slot
                for r in range(0, 224, 16):
                    value = band(below + jnp.int16(r), at, weights)
                    by_ref[pair, pl.ds(80 + r, 16), 0:128] = value
                    by_ref[pair, pl.ds(208 + r, 16), 128:256] = value
                start = lax.shift_right_logical(HX - 1 + sh_s[slot, 0, z], 4) * 16
                rows = [ref[slot][pl.ds(start, WINDOW), :] for ref in refs]
                t = jnp.dot(
                    jnp.concatenate(rows, axis=0) if len(rows) > 1 else rows[0],
                    by_ref[pair], preferred_element_type=jnp.float32,
                ).astype(jnp.bfloat16)
                for k in range(2 * len(refs)):
                    first = WINDOW * (k // 2) + 128 * (k % 2)
                    strip_refs[k][u, pl.ds(STRIP * place, STRIP), :] = t[first : first + STRIP]
            for v, block, row_start, size in BAND:
                slot = lax.rem(v - view + VIEWS, VIEWS)
                first_row = HX - 1 + sh_s[slot, 0, z]
                m = first_row - lax.shift_right_logical(first_row, 4) * 16 + STRIP * v
                weights = narrow((tp_s[slot, 1, z] * (PLANES**-0.5), tp_s[slot, 0, z] * (PLANES**-0.5)))
                at = [spread16(m + k) for k in (0, 1)]
                for r in range(row_start, row_start + size, 16):
                    bx_ref[u, pl.ds(r, 16), pl.ds(128 * block, 128)] = band(
                        beyond + jnp.int16(128 * block - r), at, weights
                    )
        for u in range(GROUP):
            z = GROUP * chunk + u
            for k in range(2 * len(refs)):
                back_refs[sources[k // 2]][z, pl.ds(128 * (k % 2), 128), :] = jnp.dot(
                    bx_ref[u], strip_refs[k][u], preferred_element_type=jnp.float32
                )

    fields()
    for copy in parameter_copies:
        copy.wait_recv()
    tables(0, VIEWS)
    first.corners(0)
    first.arrive(3, "first")
    first.arrive(1, "last")
    build(3)
    build_rows(3)
    first.arrive(3, "last")
    first.arrive(1, "first")
    first.arrive(3, "middle")
    first.arrive(1, "middle")
    first.complete(0)
    stencil(e_refs[0], q_ref)
    first.arrive(2, "first")
    first.arrive(2, "last")
    first.arrive(2, "middle")
    first.corners(3)
    first.corners(1)
    build(1)
    build_rows(1)
    build(2)
    build_rows(2)
    for slot in (3, 1, 2):
        first.complete(slot)
        apply(e_refs[slot], q_ref, slot)

    second = Exchange(f_refs, 1)
    f_refs[0][pl.ds(HX, TX), pl.ds(HY, TY)] = q_ref[...].astype(jnp.bfloat16)
    second.along_views()
    second.own()
    back(0, (0,))
    second.corners(0)
    for part in ("first", "last", "middle"):
        second.arrive(3, part)
        second.arrive(1, {"first": "last", "last": "first", "middle": "middle"}[part])
    second.complete(0)
    stencil(f_refs[0], p_ref)
    second.arrive(2, "first")
    second.arrive(2, "last")
    second.corners(3)
    second.corners(1)
    second.arrive(2, "middle")
    back(1, (0,))
    for slot in (3, 1, 2):
        second.complete(slot)
        apply(f_refs[slot], p_ref, slot)

    r0 = e_refs[0][pl.ds(HX, TX), pl.ds(HY, TY)].astype(jnp.float32)
    q0, p = q_ref[...], p_ref[...]
    sums = Sum([lanes(r0 * q0), lanes(q0 * q0), lanes(r0 * p), lanes(q0 * p), lanes(p * p)])
    sums.send(0)
    back(2, (0, 1))
    sums.receive(0)
    sums.send(1)
    back(3, (0, 1))
    sums.receive(1)
    sums.send(2)
    back(0, (1,))
    back(1, (1,))
    sums.receive(2)
    r0q0, q0q0, r0p, q0p, pp = [sums.row(i) for i in range(5)]
    gamma0 = r0q0
    alpha0 = gamma0 / (q0q0 + TINY)
    gamma1 = r0q0 - alpha0 * (r0p + q0q0) + alpha0 * alpha0 * q0p
    beta = gamma1 / (gamma0 + TINY)
    h1h1 = q0q0 - 2.0 * alpha0 * q0p + alpha0 * alpha0 * pp
    h1q0 = q0q0 - alpha0 * q0p
    alpha1 = gamma1 / (h1h1 + 2.0 * beta * h1q0 + beta * beta * q0q0 + TINY)

    weight0 = alpha0 + alpha1 * beta + alpha1
    weight1 = alpha1 * alpha0

    def combine(z, carry):
        vol_ref[0, z] = (weight0 * back_refs[0][z] - weight1 * back_refs[1][z]).astype(jnp.bfloat16)
        return carry

    lax.fori_loop(0, PLANES, combine, 0)
    q0, p = q_ref[...], p_ref[...]
    res_ref[0, 0] = meas_ref[...] - alpha0 * q0 - alpha1 * ((q0 - alpha0 * p) + beta * q0)

    for copy in parameter_copies:
        copy.wait_send()
    first.finish()
    second.finish()
    sums.finish()


def write_kernel(vol_ref, res_ref, vol_out, res_out, wide_ref, sems):
    copies = [pltpu.make_async_copy(res_ref, res_out, sems.at[PLANES])]
    copies[0].start()
    for z in range(PLANES):
        wide_ref[z] = vol_ref[0, z].astype(jnp.float32)
        copies.append(pltpu.make_async_copy(wide_ref.at[z], vol_out.at[0, z], sems.at[z]))
        copies[-1].start()
    for copy in copies:
        copy.wait()


def local(grid_x, measured, shears, taps):
    f32, bf16 = jnp.float32, jnp.bfloat16
    vmem = pl.BlockSpec(memory_space=pltpu.VMEM)
    partners = VIEWS + GRID_Y + grid_x
    hbm = pl.BlockSpec(memory_space=pltpu.HBM)
    volume, residual = pl.pallas_call(
        functools.partial(solve_kernel, grid_x),
        name="solve",
        out_shape=(
            jax.ShapeDtypeStruct((1, PLANES, TX, TY), bf16),
            jax.ShapeDtypeStruct((1, 1, TX, TY), f32),
        ),
        in_specs=[hbm, hbm, hbm],
        out_specs=(vmem, vmem),
        scratch_shapes=[
            pltpu.VMEM((TX, TY), f32),
            pltpu.VMEM((2, PLANES), jnp.int32),
            pltpu.VMEM((4, PLANES), bf16),
            [pltpu.VMEM((RX, RY), bf16)] * VIEWS,
            [pltpu.VMEM((RX, RY), bf16)] * VIEWS,
            pltpu.VMEM((3 * TX, 3 * TY), f32),
            pltpu.VMEM(((VIEWS - 1) * PLANES, RY, TY), bf16),
            pltpu.VMEM((VIEWS - 1, 2, PLANES // GROUP, 128, GROUP * STRIP), bf16),
            pltpu.VMEM((TX, TY), f32),
            pltpu.VMEM((TX, TY), f32),
            [pltpu.VMEM((PLANES, TX, TY), f32)] * 2,
            pltpu.VMEM((GROUP * VIEWS, RY, TY), bf16),
            pltpu.VMEM((GROUP, 128, VIEWS * STRIP), bf16),
            [pltpu.VMEM((GROUP, VIEWS * STRIP, TY), bf16)] * 4,
            pltpu.VMEM((VIEWS, 8, 128), jnp.int32),
            pltpu.VMEM((VIEWS, 8, 128), f32),
            pltpu.SMEM((VIEWS, 8, 128), jnp.int32),
            pltpu.SMEM((VIEWS, 8, 128), f32),
            pltpu.VMEM((VIEWS, 8, 128), f32),
            pltpu.VMEM((GRID_Y, 8, 128), f32),
            pltpu.VMEM((grid_x, 8, 128), f32),
            pltpu.SemaphoreType.DMA((2, N_SEMS)),
            pltpu.SemaphoreType.DMA((2, N_SEMS)),
            pltpu.SemaphoreType.DMA((2, VIEWS)),
            pltpu.SemaphoreType.DMA((2, VIEWS)),
            pltpu.SemaphoreType.DMA((3,)),
            pltpu.SemaphoreType.DMA((partners,)),
            pltpu.SemaphoreType.DMA((partners,)),
        ],
        compiler_params=pltpu.CompilerParams(
            collective_id=0, has_side_effects=True, vmem_limit_bytes=50 * 1024 * 1024
        ),
    )(measured, jnp.transpose(shears, (0, 2, 1)), jnp.transpose(taps, (0, 2, 1)))
    return pl.pallas_call(
        write_kernel,
        name="write",
        out_shape=(
            jax.ShapeDtypeStruct((1, PLANES, TX, TY), f32),
            jax.ShapeDtypeStruct((1, 1, TX, TY), f32),
        ),
        in_specs=[vmem, vmem],
        out_specs=(hbm, hbm),
        scratch_shapes=[pltpu.VMEM((PLANES, TX, TY), f32), pltpu.SemaphoreType.DMA((PLANES + 1,))],
        compiler_params=pltpu.CompilerParams(vmem_limit_bytes=16 * 1024 * 1024),
    )(volume, residual)


def solution(mesh):
    placed = (P("view", "tile", None, None), P("view", None, None), P("view", None, None))
    return jax.shard_map(
        functools.partial(local, mesh.shape["tile"] // GRID_Y),
        mesh=mesh,
        in_specs=placed,
        out_specs=(P("tile", None, None, None), P("view", "tile", None, None)),
        check_vma=False,
    )
```

```python
import functools

import jax
import jax.numpy as jnp
from jax import lax
from jax.experimental import pallas as pl
from jax.experimental.pallas import tpu as pltpu
from jax.sharding import PartitionSpec as P

PLANES = 16
VIEWS = 4
GRID_Y = 8
TX = 256
TY = 256
HX = 96
HY = 128
RX = TX + 2 * HX
RY = TY + 2 * HY
WINDOW = 288
STRIP = 160
GROUP = 4
BAND = (
    (0, 0, 0, 128), (0, 1, 96, 32), (1, 1, 0, 96), (1, 2, 64, 64),
    (2, 2, 0, 64), (2, 3, 32, 96), (3, 3, 0, 32), (3, 4, 0, 128),
)
FAR = 1 << 20
TINY = 1e-6
MESH = pl.DeviceIdType.MESH

Z_BASE = 9
Y_BASE = Z_BASE + 2 * VIEWS
D_BASE = Y_BASE + 10 * VIEWS
N_SEMS = D_BASE + 4 * VIEWS

PARTS = {
    "first": (HX, HX), "last": (TX, HX), "middle": (2 * HX, TX - 2 * HX),
    "top": (0, HX), "bottom": (HX + TX, HX),
}
DIRECT = {(2, "top"), (2, "bottom"), (3, "top"), (1, "bottom")}
PART_ID = {"first": 0, "last": 1, "middle": 2, "top": 3, "bottom": 4}


def ring(index, step, size):
    return lax.rem(index + (step + size), size)


def solve_kernel(
    grid_x,
    meas_hbm, sh_hbm, tp_hbm,
    vol_ref, res_ref,
    meas_ref, sh_ref, tp_ref, e_refs, f_refs, field_ref, y_ref, x_ref, q_ref, p_ref, back_refs, by_ref, bx_ref, strip_refs,
    sh_v, tp_v, sh_s, tp_s, ra_ref, rb_ref, rc_ref,
    send_sems, recv_sems, p_send, p_recv, p_local, a_send, a_recv,
):
    tile = lax.axis_index("tile")
    view = lax.axis_index("view")
    gx = tile // GRID_Y
    gy = lax.rem(tile, GRID_Y)

    def at(row, col, vw):
        return (row * GRID_Y + col, vw)

    def to_view(step):
        return at(gx, gy, ring(view, step, VIEWS))

    def to_row(step):
        return at(ring(gx, step, grid_x), gy, view)

    def to_col(step):
        return at(gx, ring(gy, step, GRID_Y), view)

    def to_corner(row_step, col_step):
        return at(ring(gx, row_step, grid_x), ring(gy, col_step, GRID_Y), view)

    partners = (
        [to_view(s) for s in range(1, VIEWS)]
        + [to_row(s) for s in range(1, grid_x)]
        + [to_col(s) for s in range(1, GRID_Y)]
        + [to_corner(r, c) for r in (-1, 1) for c in (-1, 1)]
    )
    barrier = pltpu.get_barrier_semaphore()
    for partner in partners:
        pl.semaphore_signal(barrier, inc=1, device_id=partner, device_id_type=MESH)

    loading = [
        pltpu.make_async_copy(src.at[0], dst, p_local.at[k])
        for k, (src, dst) in enumerate(((meas_hbm.at[0], meas_ref), (sh_hbm, sh_ref), (tp_hbm, tp_ref)))
    ]
    for copy in loading:
        copy.start()
    for copy in loading:
        copy.wait()
    e_refs[0][pl.ds(HX, TX), pl.ds(HY, TY)] = meas_ref[...].astype(jnp.bfloat16)
    sh_v[0] = jnp.zeros((8, 128), jnp.int32)
    sh_v[0, 0:2, 0:PLANES] = sh_ref[...]
    tp_v[0] = jnp.zeros((8, 128), jnp.float32)
    tp_v[0, 0:4, 0:PLANES] = tp_ref[...].astype(jnp.float32)

    pl.semaphore_wait(barrier, len(partners))

    class Exchange:
        def __init__(self, bufs, which):
            self.bufs, self.which, self.copies = bufs, which, {}

        def send(self, key, sem, src, dst, device):
            copy = pltpu.make_async_remote_copy(
                src_ref=src, dst_ref=dst,
                send_sem=send_sems.at[self.which, sem], recv_sem=recv_sems.at[self.which, sem],
                device_id=device, device_id_type=MESH,
            )
            copy.start()
            self.copies[key] = copy

        def region(self, slot, rows, cols):
            return self.bufs[slot].at[pl.ds(*rows), pl.ds(*cols)]

        def along_view(self, src_slot, dst_slot, part, sem, step):
            rows = PARTS[part]
            self.send(
                ("x", dst_slot, part), sem,
                self.region(src_slot, rows, (HY, TY)), self.region(dst_slot, rows, (HY, TY)),
                to_view(step),
            )

        def along_views(self):
            self.along_view(0, 3, "first", 0, 1)
            self.along_view(0, 1, "last", 1, -1)
            self.along_view(0, 3, "last", 2, 1)
            self.along_view(0, 1, "first", 3, -1)
            self.along_view(0, 3, "middle", 4, 1)
            self.along_view(0, 1, "middle", 5, -1)

        def own(self):
            for part in ("first", "last", "middle"):
                self.spread(0, part)

        def columns(self, slot, part):
            rows = PARTS[part]
            sem = Y_BASE + 10 * slot + 2 * PART_ID[part]
            self.send(
                ("y", slot, part, 0), sem,
                self.region(slot, rows, (HY, HY)), self.region(slot, rows, (HY + TY, HY)), to_col(-1),
            )
            self.send(
                ("y", slot, part, 1), sem + 1,
                self.region(slot, rows, (TY, HY)), self.region(slot, rows, (0, HY)), to_col(1),
            )

        def spread(self, slot, part):
            for k, (rim, halo, step) in enumerate((("first", "bottom", -1), ("last", "top", 1))):
                if part == rim:
                    self.send(
                        ("z", slot, halo), Z_BASE + 2 * slot + k,
                        self.region(slot, PARTS[rim], (HY, TY)),
                        self.region(slot, PARTS[halo], (HY, TY)), to_row(step),
                    )
                    if (slot, halo) in DIRECT:
                        for side, (src, dst, turn) in enumerate(((HY, HY + TY, -1), (TY, 0, 1))):
                            self.send(
                                ("d", slot, halo, side), D_BASE + 4 * slot + 2 * k + side,
                                self.region(slot, PARTS[rim], (src, HY)),
                                self.region(slot, PARTS[halo], (dst, HY)), to_corner(step, turn),
                            )
            self.columns(slot, part)

        def arrive(self, slot, part):
            self.copies["x", slot, part].wait_recv()
            if slot == 3 and part == "first":
                self.along_view(3, 2, part, 6, 1)
            if slot == 1 and part == "last":
                self.along_view(1, 2, part, 7, -1)
            if slot == 3 and part == "middle":
                self.along_view(3, 2, part, 8, 1)
            self.spread(slot, part)

        def corners(self, slot):
            for halo, edge in (("top", 0), ("bottom", grid_x - 1)):
                if (slot, halo) not in DIRECT:
                    self.copies["z", slot, halo].wait_recv()
                    start, size = PARTS[halo]

                    @pl.when(gx == edge)
                    def _():
                        self.bufs[slot][pl.ds(start, size), pl.ds(HY, TY)] = jnp.zeros((size, TY), jnp.bfloat16)

                    self.columns(slot, halo)

        def complete(self, slot):
            for halo, edge in (("top", 0), ("bottom", grid_x - 1)):
                if (slot, halo) in DIRECT:
                    self.copies["z", slot, halo].wait_recv()
                    for side in (0, 1):
                        self.copies["d", slot, halo, side].wait_recv()
                    start, size = PARTS[halo]

                    @pl.when(gx == edge)
                    def _():
                        self.bufs[slot][pl.ds(start, size), :] = jnp.zeros((size, RY), jnp.bfloat16)

            for part in PARTS:
                for side in (0, 1):
                    if ("y", slot, part, side) in self.copies:
                        self.copies["y", slot, part, side].wait_recv()
            for side, edge in ((0, 0), (HY + TY, GRID_Y - 1)):
                @pl.when(gy == edge)
                def _():
                    self.bufs[slot][:, pl.ds(side, HY)] = jnp.zeros((RX, HY), jnp.bfloat16)

        def finish(self):
            for copy in self.copies.values():
                copy.wait_send()

    first = Exchange(e_refs, 0)

    parameter_copies = []
    for step in range(1, VIEWS):
        slot = VIEWS - step
        for which, ref in ((0, sh_v), (1, tp_v)):
            copy = pltpu.make_async_remote_copy(
                src_ref=ref.at[0], dst_ref=ref.at[slot],
                send_sem=p_send.at[which, slot], recv_sem=p_recv.at[which, slot],
                device_id=to_view(step), device_id_type=MESH,
            )
            copy.start()
            parameter_copies.append(copy)

    first.along_views()

    def tables(first_slot, count):
        local = [
            pltpu.make_async_copy(src.at[pl.ds(first_slot, count)], dst.at[pl.ds(first_slot, count)], p_local.at[k])
            for k, (src, dst) in enumerate(((sh_v, sh_s), (tp_v, tp_s)))
        ]
        for copy in local:
            copy.start()
        for copy in local:
            copy.wait()

    first.own()

    column_low = jnp.where(gy == 0, 0, -FAR)
    column_high = jnp.where(gy == GRID_Y - 1, TY, FAR)
    row_low = jnp.where(gx == 0, 0, -FAR)
    row_high = jnp.where(gx == grid_x - 1, TX, FAR)

    row16 = lax.broadcasted_iota(jnp.int32, (16, 128), 0)
    col16 = lax.broadcasted_iota(jnp.int32, (16, 128), 1)
    below = (row16 - col16).astype(jnp.int16)
    beyond = (col16 - row16).astype(jnp.int16)

    def spread16(x):
        return jnp.full((16, 128), x, jnp.int32).astype(jnp.int16)

    def narrow(weights):
        return [jnp.broadcast_to(w, (16, 128)).astype(jnp.bfloat16) for w in weights]

    def band(distance, first, weights):
        value = jnp.zeros((16, 128), jnp.bfloat16)
        for at, weight in zip(first, weights):
            value = jnp.where(distance == at, weight, value)
        return value

    def build(slot):
        def one(z, carry):
            pair = (slot - 1) * PLANES + z
            y_ref[pair, 0:32, 0:128] = jnp.zeros((32, 128), jnp.bfloat16)
            y_ref[pair, 352:512, 0:128] = jnp.zeros((160, 128), jnp.bfloat16)
            y_ref[pair, 0:160, 128:256] = jnp.zeros((160, 128), jnp.bfloat16)
            y_ref[pair, 480:512, 128:256] = jnp.zeros((32, 128), jnp.bfloat16)
            shear = sh_s[0, 1, z]
            first = [spread16(sh_s[slot, 1, z] - shear + (HY - 32 + k)) for k in (-1, 0, 1)]
            a0, a1 = tp_s[0, 2, z], tp_s[0, 3, z]
            b0, b1 = tp_s[slot, 2, z], tp_s[slot, 3, z]
            low, high = shear + column_low, shear + column_high
            weights = []
            for in0, in1 in (
                (col16 >= low, col16 >= low - 1),
                (col16 + 128 < high, col16 + 128 < high - 1),
            ):
                weights.append(narrow((
                    jnp.where(in0, a0 * b1, 0.0),
                    jnp.where(in0, a0 * b0, 0.0) + jnp.where(in1, a1 * b1, 0.0),
                    jnp.where(in1, a1 * b0, 0.0),
                )))
            for r in range(0, 320, 16):
                distance = below + jnp.int16(r)
                y_ref[pair, pl.ds(32 + r, 16), 0:128] = band(distance, first, weights[0])
                y_ref[pair, pl.ds(160 + r, 16), 128:256] = band(distance, first, weights[1])
            return carry

        lax.fori_loop(0, PLANES, one, 0)

    def build_rows(slot):
        def one(g, carry):
            scalars = []
            for u in range(GROUP):
                z = GROUP * g + u
                shear = sh_s[0, 0, z]
                first_row = HX - 1 + sh_s[slot, 0, z] - shear
                m = first_row - lax.shift_right_logical(first_row, 4) * 16 + STRIP * u
                a0, a1 = tp_s[0, 0, z] * (1.0 / PLANES), tp_s[0, 1, z] * (1.0 / PLANES)
                b0, b1 = tp_s[slot, 0, z], tp_s[slot, 1, z]
                scalars.append((m, a0 * b1, a0 * b0, a1 * b1, a1 * b0, shear + row_low, shear + row_high))
            for u, block, row_start, size in BAND:
                m, am, az, bz, bp, low, high = scalars[u]
                plain = narrow((am, az + bz, bp))
                first = [spread16(m + k) for k in (0, 1, 2)]
                for r in range(row_start, row_start + size, 16):
                    distance = beyond + jnp.int16(128 * block - r)
                    for half in (0, 1):
                        weights = plain
                        if (half == 0 and r < 48) or (half == 1 and r >= 80):
                            row = row16 + (r + 128 * half)
                            in0, in1 = (row >= low, row >= low - 1) if half == 0 else (row < high, row < high - 1)
                            weights = narrow((
                                jnp.where(in0, am, 0.0),
                                jnp.where(in0, az, 0.0) + jnp.where(in1, bz, 0.0),
                                jnp.where(in1, bp, 0.0),
                            ))
                        x_ref[slot - 1, half, g, pl.ds(r, 16), pl.ds(128 * block, 128)] = band(distance, first, weights)
            return carry

        lax.fori_loop(0, PLANES // GROUP, one, 0)

    def fields():
        row = lax.broadcasted_iota(jnp.int32, (TX, 128), 0)

        def factors(shear, w0, w1, low, high, scale):
            in0 = (row >= shear + low) & (row < shear + high)
            in1 = (row >= shear + low - 1) & (row < shear + high - 1)
            cross = w0 * w1 * scale
            return jnp.concatenate([
                jnp.where(in0, cross, 0.0),
                jnp.where(in0, w0 * w0 * scale, 0.0) + jnp.where(in1, w1 * w1 * scale, 0.0),
                jnp.where(in1, cross, 0.0),
            ], axis=0).astype(jnp.bfloat16)

        along_x = factors(sh_v[0, 0:1, :], tp_v[0, 0:1, :], tp_v[0, 1:2, :], row_low, row_high, 1.0 / PLANES)
        along_y = factors(sh_v[0, 1:2, :], tp_v[0, 2:3, :], tp_v[0, 3:4, :], column_low, column_high, 1.0)
        field_ref[...] = lax.dot_general(
            along_x, along_y, (((1,), (1,)), ((), ())), preferred_element_type=jnp.float32
        )

    def stencil(src_ref, out_ref):
        def rows(i, carry):
            start = i * 64
            x = src_ref[pl.ds(pl.multiple_of(HX - 16 + start, 16), 96), :].astype(jnp.float32)
            total = jnp.zeros((64, TY), jnp.float32)
            for l in range(3):
                shifted = pltpu.roll(x, (RY + 1 - l) % RY, 1)[:, HY : HY + TY]
                for k in range(3):
                    term = pltpu.roll(shifted, (96 + 1 - k) % 96, 0)[16:80]
                    total = total + term * field_ref[pl.ds(pl.multiple_of(TX * k + start, 64), 64), TY * l : TY * (l + 1)]
            out_ref[pl.ds(pl.multiple_of(start, 64), 64), :] = total
            return carry

        lax.fori_loop(0, TX // 64, rows, 0)

    def apply(src_ref, out_ref, slot):
        for z in range(PLANES):
            first_row = HX - 1 + sh_s[slot, 0, z] - sh_s[0, 0, z]
            start = lax.shift_right_logical(first_row, 4) * 16
            t = jnp.dot(
                src_ref[pl.ds(start, WINDOW), :], y_ref[(slot - 1) * PLANES + z], preferred_element_type=jnp.float32
            ).astype(jnp.bfloat16)
            strip = pl.ds(STRIP * (z % GROUP), STRIP)
            strip_refs[0][z // GROUP, strip, :] = t[0:STRIP]
            strip_refs[1][z // GROUP, strip, :] = t[128 : 128 + STRIP]
        for half, t_ref in enumerate(strip_refs[0:2]):
            total = out_ref[pl.ds(128 * half, 128), :]
            for g in range(PLANES // GROUP):
                total = total + jnp.dot(
                    x_ref[slot - 1, half, g],
                    t_ref[g],
                    preferred_element_type=jnp.float32,
                )
            out_ref[pl.ds(128 * half, 128), :] = total

    def lanes(x):
        s = jnp.sum(x, axis=0, keepdims=True)
        return s[:, 0:128] + s[:, 128:256]

    class Sum:
        def __init__(self, rows):
            self.stages = (
                (ra_ref, view, VIEWS, to_view, 0),
                (rb_ref, gy, GRID_Y, to_col, VIEWS),
                (rc_ref, gx, grid_x, to_row, VIEWS + GRID_Y),
            )
            self.copies = []
            pad = jnp.zeros((8 - len(rows), 128), jnp.float32)
            self.value = jnp.concatenate(list(rows) + [pad], axis=0)

        def send(self, stage):
            ref, me, size, to, base = self.stages[stage]
            ref[me] = self.value
            self.current = []
            for step in sorted(range(1, size), key=lambda k: -min(k, size - k)):
                copy = pltpu.make_async_remote_copy(
                    src_ref=ref.at[me], dst_ref=ref.at[me],
                    send_sem=a_send.at[base + step], recv_sem=a_recv.at[base + step],
                    device_id=to(step), device_id_type=MESH,
                )
                copy.start()
                self.current.append(copy)
            self.copies += self.current

        def receive(self, stage):
            ref, me, size, to, base = self.stages[stage]
            for copy in self.current:
                copy.wait_recv()
            total = ref[0]
            for i in range(1, size):
                total = total + ref[i]
            self.value = total

        def row(self, i):
            return jnp.sum(self.value[i : i + 1, :], axis=1, keepdims=True)

        def finish(self):
            for copy in self.copies:
                copy.wait_send()

    by_ref[...] = jnp.zeros(by_ref.shape, jnp.bfloat16)

    def back(chunk, sources):
        refs = [(e_refs, f_refs)[k] for k in sources]
        for u in range(GROUP):
            z = GROUP * chunk + u
            for slot in range(VIEWS):
                place = lax.rem(view + slot, VIEWS)
                d = sh_s[slot, 1, z]
                weights = narrow((tp_s[slot, 3, z], tp_s[slot, 2, z]))
                at = [spread16(d + (HY - 80 + k)) for k in (-1, 0)]
                pair = VIEWS * u + slot
                for r in range(0, 224, 16):
                    value = band(below + jnp.int16(r), at, weights)
                    by_ref[pair, pl.ds(80 + r, 16), 0:128] = value
                    by_ref[pair, pl.ds(208 + r, 16), 128:256] = value
                start = lax.shift_right_logical(HX - 1 + sh_s[slot, 0, z], 4) * 16
                rows = [ref[slot][pl.ds(start, WINDOW), :] for ref in refs]
                t = jnp.dot(
                    jnp.concatenate(rows, axis=0) if len(rows) > 1 else rows[0],
                    by_ref[pair], preferred_element_type=jnp.float32,
                ).astype(jnp.bfloat16)
                for k in range(2 * len(refs)):
                    first = WINDOW * (k // 2) + 128 * (k % 2)
                    strip_refs[k][u, pl.ds(STRIP * place, STRIP), :] = t[first : first + STRIP]
            for v, block, row_start, size in BAND:
                slot = lax.rem(v - view + VIEWS, VIEWS)
                first_row = HX - 1 + sh_s[slot, 0, z]
                m = first_row - lax.shift_right_logical(first_row, 4) * 16 + STRIP * v
                weights = narrow((tp_s[slot, 1, z] * (PLANES**-0.5), tp_s[slot, 0, z] * (PLANES**-0.5)))
                at = [spread16(m + k) for k in (0, 1)]
                for r in range(row_start, row_start + size, 16):
                    bx_ref[u, pl.ds(r, 16), pl.ds(128 * block, 128)] = band(
                        beyond + jnp.int16(128 * block - r), at, weights
                    )
        for u in range(GROUP):
            z = GROUP * chunk + u
            for k in range(2 * len(refs)):
                back_refs[sources[k // 2]][z, pl.ds(128 * (k % 2), 128), :] = jnp.dot(
                    bx_ref[u], strip_refs[k][u], preferred_element_type=jnp.float32
                )

    fields()
    for copy in parameter_copies:
        copy.wait_recv()
    tables(0, VIEWS)
    first.corners(0)
    first.arrive(3, "first")
    first.arrive(1, "last")
    build(3)
    build_rows(3)
    first.arrive(3, "last")
    first.arrive(1, "first")
    first.arrive(3, "middle")
    first.arrive(1, "middle")
    first.complete(0)
    stencil(e_refs[0], q_ref)
    first.corners(3)
    first.corners(1)
    first.arrive(2, "first")
    first.arrive(2, "last")
    build(1)
    build_rows(1)
    first.arrive(2, "middle")
    build(2)
    build_rows(2)
    for slot in (3, 1, 2):
        first.complete(slot)
        apply(e_refs[slot], q_ref, slot)

    second = Exchange(f_refs, 1)
    f_refs[0][pl.ds(HX, TX), pl.ds(HY, TY)] = q_ref[...].astype(jnp.bfloat16)
    second.along_views()
    second.own()
    back(0, (0,))
    second.corners(0)
    for part in ("first", "last", "middle"):
        second.arrive(3, part)
        second.arrive(1, {"first": "last", "last": "first", "middle": "middle"}[part])
    second.complete(0)
    stencil(f_refs[0], p_ref)
    second.corners(3)
    second.corners(1)
    second.arrive(2, "first")
    second.arrive(2, "last")
    second.arrive(2, "middle")
    back(1, (0,))
    for slot in (3, 1, 2):
        second.complete(slot)
        apply(f_refs[slot], p_ref, slot)

    r0 = e_refs[0][pl.ds(HX, TX), pl.ds(HY, TY)].astype(jnp.float32)
    q0, p = q_ref[...], p_ref[...]
    sums = Sum([lanes(r0 * q0), lanes(q0 * q0), lanes(r0 * p), lanes(q0 * p), lanes(p * p)])
    sums.send(0)
    back(2, (0, 1))
    sums.receive(0)
    sums.send(1)
    back(3, (0, 1))
    sums.receive(1)
    sums.send(2)
    back(0, (1,))
    back(1, (1,))
    sums.receive(2)
    r0q0, q0q0, r0p, q0p, pp = [sums.row(i) for i in range(5)]
    gamma0 = r0q0
    alpha0 = gamma0 / (q0q0 + TINY)
    gamma1 = r0q0 - alpha0 * (r0p + q0q0) + alpha0 * alpha0 * q0p
    beta = gamma1 / (gamma0 + TINY)
    h1h1 = q0q0 - 2.0 * alpha0 * q0p + alpha0 * alpha0 * pp
    h1q0 = q0q0 - alpha0 * q0p
    alpha1 = gamma1 / (h1h1 + 2.0 * beta * h1q0 + beta * beta * q0q0 + TINY)

    weight0 = alpha0 + alpha1 * beta + alpha1
    weight1 = alpha1 * alpha0

    def combine(z, carry):
        vol_ref[0, z] = (weight0 * back_refs[0][z] - weight1 * back_refs[1][z]).astype(jnp.bfloat16)
        return carry

    lax.fori_loop(0, PLANES, combine, 0)
    q0, p = q_ref[...], p_ref[...]
    res_ref[0, 0] = meas_ref[...] - alpha0 * q0 - alpha1 * ((q0 - alpha0 * p) + beta * q0)

    for copy in parameter_copies:
        copy.wait_send()
    first.finish()
    second.finish()
    sums.finish()


def write_kernel(vol_ref, res_ref, vol_out, res_out, wide_ref, sems):
    copies = [pltpu.make_async_copy(res_ref, res_out, sems.at[PLANES])]
    copies[0].start()
    for z in range(PLANES):
        wide_ref[z] = vol_ref[0, z].astype(jnp.float32)
        copies.append(pltpu.make_async_copy(wide_ref.at[z], vol_out.at[0, z], sems.at[z]))
        copies[-1].start()
    for copy in copies:
        copy.wait()


def local(grid_x, measured, shears, taps):
    f32, bf16 = jnp.float32, jnp.bfloat16
    vmem = pl.BlockSpec(memory_space=pltpu.VMEM)
    partners = VIEWS + GRID_Y + grid_x
    hbm = pl.BlockSpec(memory_space=pltpu.HBM)
    volume, residual = pl.pallas_call(
        functools.partial(solve_kernel, grid_x),
        name="solve",
        out_shape=(
            jax.ShapeDtypeStruct((1, PLANES, TX, TY), bf16),
            jax.ShapeDtypeStruct((1, 1, TX, TY), f32),
        ),
        in_specs=[hbm, hbm, hbm],
        out_specs=(vmem, vmem),
        scratch_shapes=[
            pltpu.VMEM((TX, TY), f32),
            pltpu.VMEM((2, PLANES), jnp.int32),
            pltpu.VMEM((4, PLANES), bf16),
            [pltpu.VMEM((RX, RY), bf16)] * VIEWS,
            [pltpu.VMEM((RX, RY), bf16)] * VIEWS,
            pltpu.VMEM((3 * TX, 3 * TY), f32),
            pltpu.VMEM(((VIEWS - 1) * PLANES, RY, TY), bf16),
            pltpu.VMEM((VIEWS - 1, 2, PLANES // GROUP, 128, GROUP * STRIP), bf16),
            pltpu.VMEM((TX, TY), f32),
            pltpu.VMEM((TX, TY), f32),
            [pltpu.VMEM((PLANES, TX, TY), f32)] * 2,
            pltpu.VMEM((GROUP * VIEWS, RY, TY), bf16),
            pltpu.VMEM((GROUP, 128, VIEWS * STRIP), bf16),
            [pltpu.VMEM((GROUP, VIEWS * STRIP, TY), bf16)] * 4,
            pltpu.VMEM((VIEWS, 8, 128), jnp.int32),
            pltpu.VMEM((VIEWS, 8, 128), f32),
            pltpu.SMEM((VIEWS, 8, 128), jnp.int32),
            pltpu.SMEM((VIEWS, 8, 128), f32),
            pltpu.VMEM((VIEWS, 8, 128), f32),
            pltpu.VMEM((GRID_Y, 8, 128), f32),
            pltpu.VMEM((grid_x, 8, 128), f32),
            pltpu.SemaphoreType.DMA((2, N_SEMS)),
            pltpu.SemaphoreType.DMA((2, N_SEMS)),
            pltpu.SemaphoreType.DMA((2, VIEWS)),
            pltpu.SemaphoreType.DMA((2, VIEWS)),
            pltpu.SemaphoreType.DMA((3,)),
            pltpu.SemaphoreType.DMA((partners,)),
            pltpu.SemaphoreType.DMA((partners,)),
        ],
        compiler_params=pltpu.CompilerParams(
            collective_id=0, has_side_effects=True, vmem_limit_bytes=50 * 1024 * 1024
        ),
    )(*[pltpu.with_memory_space_constraint(x, pltpu.HBM) for x in (measured, jnp.transpose(shears, (0, 2, 1)), jnp.transpose(taps, (0, 2, 1)))])
    return pl.pallas_call(
        write_kernel,
        name="write",
        out_shape=(
            jax.ShapeDtypeStruct((1, PLANES, TX, TY), f32),
            jax.ShapeDtypeStruct((1, 1, TX, TY), f32),
        ),
        in_specs=[vmem, vmem],
        out_specs=(hbm, hbm),
        scratch_shapes=[pltpu.VMEM((PLANES, TX, TY), f32), pltpu.SemaphoreType.DMA((PLANES + 1,))],
        compiler_params=pltpu.CompilerParams(vmem_limit_bytes=16 * 1024 * 1024),
    )(volume, residual)


def solution(mesh):
    placed = (P("view", "tile", None, None), P("view", None, None), P("view", None, None))
    return jax.shard_map(
        functools.partial(local, mesh.shape["tile"] // GRID_Y),
        mesh=mesh,
        in_specs=placed,
        out_specs=(P("tile", None, None, None), P("view", "tile", None, None)),
        check_vma=False,
    )
```

```python
import functools

import jax
import jax.numpy as jnp
from jax import lax
from jax.experimental import pallas as pl
from jax.experimental.pallas import tpu as pltpu
from jax.sharding import PartitionSpec as P

PLANES = 16
VIEWS = 4
GRID_Y = 8
TX = 256
TY = 256
HX = 96
HY = 128
RX = TX + 2 * HX
RY = TY + 2 * HY
WINDOW = 288
STRIP = 160
GROUP = 4
BAND = (
    (0, 0, 0, 128), (0, 1, 96, 32), (1, 1, 0, 96), (1, 2, 64, 64),
    (2, 2, 0, 64), (2, 3, 32, 96), (3, 3, 0, 32), (3, 4, 0, 128),
)
FAR = 1 << 20
TINY = 1e-6
MESH = pl.DeviceIdType.MESH

Z_BASE = 9
Y_BASE = Z_BASE + 2 * VIEWS
D_BASE = Y_BASE + 10 * VIEWS
N_SEMS = D_BASE + 4 * VIEWS

PARTS = {
    "first": (HX, HX), "last": (TX, HX), "middle": (2 * HX, TX - 2 * HX),
    "top": (0, HX), "bottom": (HX + TX, HX),
}
DIRECT = {(2, "top"), (2, "bottom"), (3, "top"), (1, "bottom")}
PART_ID = {"first": 0, "last": 1, "middle": 2, "top": 3, "bottom": 4}


def ring(index, step, size):
    return lax.rem(index + (step + size), size)


def solve_kernel(
    grid_x,
    meas_hbm, sh_hbm, tp_hbm,
    vol_ref, res_ref,
    meas_ref, sh_ref, tp_ref, e_refs, f_refs, field_ref, y_ref, x_ref, q_ref, p_ref, back_refs, by_ref, bx_ref, strip_refs,
    sh_v, tp_v, sh_s, tp_s, ra_ref, rb_ref, rc_ref,
    send_sems, recv_sems, p_send, p_recv, p_local, a_send, a_recv,
):
    tile = lax.axis_index("tile")
    view = lax.axis_index("view")
    gx = tile // GRID_Y
    gy = lax.rem(tile, GRID_Y)

    def at(row, col, vw):
        return (row * GRID_Y + col, vw)

    def to_view(step):
        return at(gx, gy, ring(view, step, VIEWS))

    def to_row(step):
        return at(ring(gx, step, grid_x), gy, view)

    def to_col(step):
        return at(gx, ring(gy, step, GRID_Y), view)

    def to_corner(row_step, col_step):
        return at(ring(gx, row_step, grid_x), ring(gy, col_step, GRID_Y), view)

    partners = (
        [to_view(s) for s in range(1, VIEWS)]
        + [to_row(s) for s in range(1, grid_x)]
        + [to_col(s) for s in range(1, GRID_Y)]
        + [to_corner(r, c) for r in (-1, 1) for c in (-1, 1)]
    )
    barrier = pltpu.get_barrier_semaphore()
    for partner in partners:
        pl.semaphore_signal(barrier, inc=1, device_id=partner, device_id_type=MESH)

    loading = [
        pltpu.make_async_copy(src.at[0], dst, p_local.at[k])
        for k, (src, dst) in enumerate(((meas_hbm.at[0], meas_ref), (sh_hbm, sh_ref), (tp_hbm, tp_ref)))
    ]
    for copy in loading:
        copy.start()
    for copy in loading:
        copy.wait()
    e_refs[0][pl.ds(HX, TX), pl.ds(HY, TY)] = meas_ref[...].astype(jnp.bfloat16)
    sh_v[0] = jnp.zeros((8, 128), jnp.int32)
    sh_v[0, 0:2, 0:PLANES] = sh_ref[...]
    tp_v[0] = jnp.zeros((8, 128), jnp.float32)
    tp_v[0, 0:4, 0:PLANES] = tp_ref[...].astype(jnp.float32)

    pl.semaphore_wait(barrier, len(partners))

    class Exchange:
        def __init__(self, bufs, which):
            self.bufs, self.which, self.copies = bufs, which, {}

        def send(self, key, sem, src, dst, device):
            copy = pltpu.make_async_remote_copy(
                src_ref=src, dst_ref=dst,
                send_sem=send_sems.at[self.which, sem], recv_sem=recv_sems.at[self.which, sem],
                device_id=device, device_id_type=MESH,
            )
            copy.start()
            self.copies[key] = copy

        def region(self, slot, rows, cols):
            return self.bufs[slot].at[pl.ds(*rows), pl.ds(*cols)]

        def along_view(self, src_slot, dst_slot, part, sem, step):
            rows = PARTS[part]
            self.send(
                ("x", dst_slot, part), sem,
                self.region(src_slot, rows, (HY, TY)), self.region(dst_slot, rows, (HY, TY)),
                to_view(step),
            )

        def along_views(self):
            self.along_view(0, 3, "first", 0, 1)
            self.along_view(0, 1, "last", 1, -1)
            self.along_view(0, 3, "last", 2, 1)
            self.along_view(0, 1, "first", 3, -1)
            self.along_view(0, 3, "middle", 4, 1)
            self.along_view(0, 1, "middle", 5, -1)

        def own(self):
            for part in ("first", "last", "middle"):
                self.spread(0, part)

        def columns(self, slot, part):
            rows = PARTS[part]
            sem = Y_BASE + 10 * slot + 2 * PART_ID[part]
            self.send(
                ("y", slot, part, 0), sem,
                self.region(slot, rows, (HY, HY)), self.region(slot, rows, (HY + TY, HY)), to_col(-1),
            )
            self.send(
                ("y", slot, part, 1), sem + 1,
                self.region(slot, rows, (TY, HY)), self.region(slot, rows, (0, HY)), to_col(1),
            )

        def spread(self, slot, part):
            for k, (rim, halo, step) in enumerate((("first", "bottom", -1), ("last", "top", 1))):
                if part == rim:
                    self.send(
                        ("z", slot, halo), Z_BASE + 2 * slot + k,
                        self.region(slot, PARTS[rim], (HY, TY)),
                        self.region(slot, PARTS[halo], (HY, TY)), to_row(step),
                    )
                    if (slot, halo) in DIRECT:
                        for side, (src, dst, turn) in enumerate(((HY, HY + TY, -1), (TY, 0, 1))):
                            self.send(
                                ("d", slot, halo, side), D_BASE + 4 * slot + 2 * k + side,
                                self.region(slot, PARTS[rim], (src, HY)),
                                self.region(slot, PARTS[halo], (dst, HY)), to_corner(step, turn),
                            )
            self.columns(slot, part)

        def arrive(self, slot, part):
            self.copies["x", slot, part].wait_recv()
            if slot == 3 and part == "first":
                self.along_view(3, 2, part, 6, 1)
            if slot == 1 and part == "last":
                self.along_view(1, 2, part, 7, -1)
            if slot == 3 and part == "middle":
                self.along_view(3, 2, part, 8, 1)
            self.spread(slot, part)

        def corners(self, slot):
            for halo, edge in (("top", 0), ("bottom", grid_x - 1)):
                if (slot, halo) not in DIRECT:
                    self.copies["z", slot, halo].wait_recv()
                    start, size = PARTS[halo]

                    @pl.when(gx == edge)
                    def _():
                        self.bufs[slot][pl.ds(start, size), pl.ds(HY, TY)] = jnp.zeros((size, TY), jnp.bfloat16)

                    self.columns(slot, halo)

        def complete(self, slot):
            for halo, edge in (("top", 0), ("bottom", grid_x - 1)):
                if (slot, halo) in DIRECT:
                    self.copies["z", slot, halo].wait_recv()
                    for side in (0, 1):
                        self.copies["d", slot, halo, side].wait_recv()
                    start, size = PARTS[halo]

                    @pl.when(gx == edge)
                    def _():
                        self.bufs[slot][pl.ds(start, size), :] = jnp.zeros((size, RY), jnp.bfloat16)

            for part in PARTS:
                for side in (0, 1):
                    if ("y", slot, part, side) in self.copies:
                        self.copies["y", slot, part, side].wait_recv()
            for side, edge in ((0, 0), (HY + TY, GRID_Y - 1)):
                @pl.when(gy == edge)
                def _():
                    self.bufs[slot][:, pl.ds(side, HY)] = jnp.zeros((RX, HY), jnp.bfloat16)

        def finish(self):
            for copy in self.copies.values():
                copy.wait_send()

    first = Exchange(e_refs, 0)

    parameter_copies = []
    for step in range(1, VIEWS):
        slot = VIEWS - step
        for which, ref in ((0, sh_v), (1, tp_v)):
            copy = pltpu.make_async_remote_copy(
                src_ref=ref.at[0], dst_ref=ref.at[slot],
                send_sem=p_send.at[which, slot], recv_sem=p_recv.at[which, slot],
                device_id=to_view(step), device_id_type=MESH,
            )
            copy.start()
            parameter_copies.append(copy)

    first.along_views()

    def tables(first_slot, count):
        local = [
            pltpu.make_async_copy(src.at[pl.ds(first_slot, count)], dst.at[pl.ds(first_slot, count)], p_local.at[k])
            for k, (src, dst) in enumerate(((sh_v, sh_s), (tp_v, tp_s)))
        ]
        for copy in local:
            copy.start()
        for copy in local:
            copy.wait()

    first.own()

    column_low = jnp.where(gy == 0, 0, -FAR)
    column_high = jnp.where(gy == GRID_Y - 1, TY, FAR)
    row_low = jnp.where(gx == 0, 0, -FAR)
    row_high = jnp.where(gx == grid_x - 1, TX, FAR)

    row16 = lax.broadcasted_iota(jnp.int32, (16, 128), 0)
    col16 = lax.broadcasted_iota(jnp.int32, (16, 128), 1)
    below = (row16 - col16).astype(jnp.int16)
    beyond = (col16 - row16).astype(jnp.int16)

    def spread16(x):
        return jnp.full((16, 128), x, jnp.int32).astype(jnp.int16)

    def narrow(weights):
        return [jnp.broadcast_to(w, (16, 128)).astype(jnp.bfloat16) for w in weights]

    def band(distance, first, weights):
        value = jnp.zeros((16, 128), jnp.bfloat16)
        for at, weight in zip(first, weights):
            value = jnp.where(distance == at, weight, value)
        return value

    def build(slot):
        def one(z, carry):
            pair = (slot - 1) * PLANES + z
            y_ref[pair, 0:32, 0:128] = jnp.zeros((32, 128), jnp.bfloat16)
            y_ref[pair, 352:512, 0:128] = jnp.zeros((160, 128), jnp.bfloat16)
            y_ref[pair, 0:160, 128:256] = jnp.zeros((160, 128), jnp.bfloat16)
            y_ref[pair, 480:512, 128:256] = jnp.zeros((32, 128), jnp.bfloat16)
            shear = sh_s[0, 1, z]
            first = [spread16(sh_s[slot, 1, z] - shear + (HY - 32 + k)) for k in (-1, 0, 1)]
            a0, a1 = tp_s[0, 2, z], tp_s[0, 3, z]
            b0, b1 = tp_s[slot, 2, z], tp_s[slot, 3, z]
            low, high = shear + column_low, shear + column_high
            weights = []
            for in0, in1 in (
                (col16 >= low, col16 >= low - 1),
                (col16 + 128 < high, col16 + 128 < high - 1),
            ):
                weights.append(narrow((
                    jnp.where(in0, a0 * b1, 0.0),
                    jnp.where(in0, a0 * b0, 0.0) + jnp.where(in1, a1 * b1, 0.0),
                    jnp.where(in1, a1 * b0, 0.0),
                )))
            for r in range(0, 320, 16):
                distance = below + jnp.int16(r)
                y_ref[pair, pl.ds(32 + r, 16), 0:128] = band(distance, first, weights[0])
                y_ref[pair, pl.ds(160 + r, 16), 128:256] = band(distance, first, weights[1])
            return carry

        lax.fori_loop(0, PLANES, one, 0)

    def build_rows(slot):
        def one(g, carry):
            scalars = []
            for u in range(GROUP):
                z = GROUP * g + u
                shear = sh_s[0, 0, z]
                first_row = HX - 1 + sh_s[slot, 0, z] - shear
                m = first_row - lax.shift_right_logical(first_row, 4) * 16 + STRIP * u
                a0, a1 = tp_s[0, 0, z] * (1.0 / PLANES), tp_s[0, 1, z] * (1.0 / PLANES)
                b0, b1 = tp_s[slot, 0, z], tp_s[slot, 1, z]
                scalars.append((m, a0 * b1, a0 * b0, a1 * b1, a1 * b0, shear + row_low, shear + row_high))
            for u, block, row_start, size in BAND:
                m, am, az, bz, bp, low, high = scalars[u]
                plain = narrow((am, az + bz, bp))
                first = [spread16(m + k) for k in (0, 1, 2)]
                for r in range(row_start, row_start + size, 16):
                    distance = beyond + jnp.int16(128 * block - r)
                    for half in (0, 1):
                        weights = plain
                        if (half == 0 and r < 48) or (half == 1 and r >= 80):
                            row = row16 + (r + 128 * half)
                            in0, in1 = (row >= low, row >= low - 1) if half == 0 else (row < high, row < high - 1)
                            weights = narrow((
                                jnp.where(in0, am, 0.0),
                                jnp.where(in0, az, 0.0) + jnp.where(in1, bz, 0.0),
                                jnp.where(in1, bp, 0.0),
                            ))
                        x_ref[slot - 1, half, g, pl.ds(r, 16), pl.ds(128 * block, 128)] = band(distance, first, weights)
            return carry

        lax.fori_loop(0, PLANES // GROUP, one, 0)

    def fields():
        row = lax.broadcasted_iota(jnp.int32, (TX, 128), 0)

        def factors(shear, w0, w1, low, high, scale):
            in0 = (row >= shear + low) & (row < shear + high)
            in1 = (row >= shear + low - 1) & (row < shear + high - 1)
            cross = w0 * w1 * scale
            return jnp.concatenate([
                jnp.where(in0, cross, 0.0),
                jnp.where(in0, w0 * w0 * scale, 0.0) + jnp.where(in1, w1 * w1 * scale, 0.0),
                jnp.where(in1, cross, 0.0),
            ], axis=0).astype(jnp.bfloat16)

        along_x = factors(sh_v[0, 0:1, :], tp_v[0, 0:1, :], tp_v[0, 1:2, :], row_low, row_high, 1.0 / PLANES)
        along_y = factors(sh_v[0, 1:2, :], tp_v[0, 2:3, :], tp_v[0, 3:4, :], column_low, column_high, 1.0)
        field_ref[...] = lax.dot_general(
            along_x, along_y, (((1,), (1,)), ((), ())), preferred_element_type=jnp.float32
        )

    def stencil(src_ref, out_ref):
        def rows(i, carry):
            start = i * 64
            x = src_ref[pl.ds(pl.multiple_of(HX - 16 + start, 16), 96), :].astype(jnp.float32)
            total = jnp.zeros((64, TY), jnp.float32)
            for l in range(3):
                shifted = pltpu.roll(x, (RY + 1 - l) % RY, 1)[:, HY : HY + TY]
                for k in range(3):
                    term = pltpu.roll(shifted, (96 + 1 - k) % 96, 0)[16:80]
                    total = total + term * field_ref[pl.ds(pl.multiple_of(TX * k + start, 64), 64), TY * l : TY * (l + 1)]
            out_ref[pl.ds(pl.multiple_of(start, 64), 64), :] = total
            return carry

        lax.fori_loop(0, TX // 64, rows, 0)

    def columns_of(src_ref, slot):
        for z in range(PLANES):
            first_row = HX - 1 + sh_s[slot, 0, z] - sh_s[0, 0, z]
            start = lax.shift_right_logical(first_row, 4) * 16
            t = jnp.dot(
                src_ref[pl.ds(start, WINDOW), :], y_ref[(slot - 1) * PLANES + z], preferred_element_type=jnp.float32
            ).astype(jnp.bfloat16)
            strip = pl.ds(STRIP * (z % GROUP), STRIP)
            strip_refs[2 * slot - 2][z // GROUP, strip, :] = t[0:STRIP]
            strip_refs[2 * slot - 1][z // GROUP, strip, :] = t[128 : 128 + STRIP]

    def rows_of(out_ref, slots):
        for half in (0, 1):
            total = out_ref[pl.ds(128 * half, 128), :]
            for slot in slots:
                for g in range(PLANES // GROUP):
                    total = total + jnp.dot(
                        x_ref[slot - 1, half, g],
                        strip_refs[2 * slot - 2 + half][g],
                        preferred_element_type=jnp.float32,
                    )
            out_ref[pl.ds(128 * half, 128), :] = total

    def others(exchange, out_ref):
        for slot in (3, 1, 2):
            exchange.complete(slot)
            columns_of(exchange.bufs[slot], slot)
        rows_of(out_ref, (3, 1, 2))

    def lanes(x):
        s = jnp.sum(x, axis=0, keepdims=True)
        return s[:, 0:128] + s[:, 128:256]

    class Sum:
        def __init__(self, rows):
            self.stages = (
                (ra_ref, view, VIEWS, to_view, 0),
                (rb_ref, gy, GRID_Y, to_col, VIEWS),
                (rc_ref, gx, grid_x, to_row, VIEWS + GRID_Y),
            )
            self.copies = []
            pad = jnp.zeros((8 - len(rows), 128), jnp.float32)
            self.value = jnp.concatenate(list(rows) + [pad], axis=0)

        def send(self, stage):
            ref, me, size, to, base = self.stages[stage]
            ref[me] = self.value
            self.current = []
            for step in sorted(range(1, size), key=lambda k: -min(k, size - k)):
                copy = pltpu.make_async_remote_copy(
                    src_ref=ref.at[me], dst_ref=ref.at[me],
                    send_sem=a_send.at[base + step], recv_sem=a_recv.at[base + step],
                    device_id=to(step), device_id_type=MESH,
                )
                copy.start()
                self.current.append(copy)
            self.copies += self.current

        def receive(self, stage):
            ref, me, size, to, base = self.stages[stage]
            for copy in self.current:
                copy.wait_recv()
            total = ref[0]
            for i in range(1, size):
                total = total + ref[i]
            self.value = total

        def row(self, i):
            return jnp.sum(self.value[i : i + 1, :], axis=1, keepdims=True)

        def finish(self):
            for copy in self.copies:
                copy.wait_send()

    by_ref[...] = jnp.zeros(by_ref.shape, jnp.bfloat16)

    def back(chunk, sources):
        refs = [(e_refs, f_refs)[k] for k in sources]
        for u in range(GROUP):
            z = GROUP * chunk + u
            for slot in range(VIEWS):
                place = lax.rem(view + slot, VIEWS)
                d = sh_s[slot, 1, z]
                weights = narrow((tp_s[slot, 3, z], tp_s[slot, 2, z]))
                at = [spread16(d + (HY - 80 + k)) for k in (-1, 0)]
                pair = VIEWS * u + slot
                for r in range(0, 224, 16):
                    value = band(below + jnp.int16(r), at, weights)
                    by_ref[pair, pl.ds(80 + r, 16), 0:128] = value
                    by_ref[pair, pl.ds(208 + r, 16), 128:256] = value
                start = lax.shift_right_logical(HX - 1 + sh_s[slot, 0, z], 4) * 16
                rows = [ref[slot][pl.ds(start, WINDOW), :] for ref in refs]
                t = jnp.dot(
                    jnp.concatenate(rows, axis=0) if len(rows) > 1 else rows[0],
                    by_ref[pair], preferred_element_type=jnp.float32,
                ).astype(jnp.bfloat16)
                for k in range(2 * len(refs)):
                    first = WINDOW * (k // 2) + 128 * (k % 2)
                    strip_refs[k][u, pl.ds(STRIP * place, STRIP), :] = t[first : first + STRIP]
            for v, block, row_start, size in BAND:
                slot = lax.rem(v - view + VIEWS, VIEWS)
                first_row = HX - 1 + sh_s[slot, 0, z]
                m = first_row - lax.shift_right_logical(first_row, 4) * 16 + STRIP * v
                weights = narrow((tp_s[slot, 1, z] * (PLANES**-0.5), tp_s[slot, 0, z] * (PLANES**-0.5)))
                at = [spread16(m + k) for k in (0, 1)]
                for r in range(row_start, row_start + size, 16):
                    bx_ref[u, pl.ds(r, 16), pl.ds(128 * block, 128)] = band(
                        beyond + jnp.int16(128 * block - r), at, weights
                    )
        for u in range(GROUP):
            z = GROUP * chunk + u
            for k in range(2 * len(refs)):
                back_refs[sources[k // 2]][z, pl.ds(128 * (k % 2), 128), :] = jnp.dot(
                    bx_ref[u], strip_refs[k][u], preferred_element_type=jnp.float32
                )

    fields()
    first.arrive(3, "first")
    first.arrive(1, "last")
    first.corners(0)
    for copy in parameter_copies:
        copy.wait_recv()
    tables(0, VIEWS)
    build(3)
    build_rows(3)
    first.arrive(3, "last")
    first.arrive(1, "first")
    first.arrive(3, "middle")
    first.arrive(1, "middle")
    first.complete(0)
    stencil(e_refs[0], q_ref)
    first.corners(3)
    first.corners(1)
    first.arrive(2, "first")
    first.arrive(2, "last")
    build(1)
    build_rows(1)
    first.arrive(2, "middle")
    build(2)
    build_rows(2)
    others(first, q_ref)

    second = Exchange(f_refs, 1)
    f_refs[0][pl.ds(HX, TX), pl.ds(HY, TY)] = q_ref[...].astype(jnp.bfloat16)
    second.along_views()
    second.own()
    r0, q0 = e_refs[0][pl.ds(HX, TX), pl.ds(HY, TY)].astype(jnp.float32), q_ref[...]
    known = [lanes(r0 * q0), lanes(q0 * q0)]
    back(0, (0,))
    second.corners(0)
    for part in ("first", "last", "middle"):
        second.arrive(3, part)
        second.arrive(1, {"first": "last", "last": "first", "middle": "middle"}[part])
    second.complete(0)
    stencil(f_refs[0], p_ref)
    second.corners(3)
    second.corners(1)
    second.arrive(2, "first")
    second.arrive(2, "last")
    second.arrive(2, "middle")
    back(1, (0,))
    others(second, p_ref)

    r0 = e_refs[0][pl.ds(HX, TX), pl.ds(HY, TY)].astype(jnp.float32)
    q0, p = q_ref[...], p_ref[...]
    sums = Sum(known + [lanes(r0 * p), lanes(q0 * p), lanes(p * p)])
    sums.send(0)
    back(2, (0, 1))
    sums.receive(0)
    sums.send(1)
    back(3, (0, 1))
    sums.receive(1)
    sums.send(2)
    back(0, (1,))
    back(1, (1,))
    sums.receive(2)
    r0q0, q0q0, r0p, q0p, pp = [sums.row(i) for i in range(5)]
    gamma0 = r0q0
    alpha0 = gamma0 / (q0q0 + TINY)
    gamma1 = r0q0 - alpha0 * (r0p + q0q0) + alpha0 * alpha0 * q0p
    beta = gamma1 / (gamma0 + TINY)
    h1h1 = q0q0 - 2.0 * alpha0 * q0p + alpha0 * alpha0 * pp
    h1q0 = q0q0 - alpha0 * q0p
    alpha1 = gamma1 / (h1h1 + 2.0 * beta * h1q0 + beta * beta * q0q0 + TINY)

    weight0 = alpha0 + alpha1 * beta + alpha1
    weight1 = alpha1 * alpha0

    def combine(z, carry):
        vol_ref[0, z] = (weight0 * back_refs[0][z] - weight1 * back_refs[1][z]).astype(jnp.bfloat16)
        return carry

    lax.fori_loop(0, PLANES, combine, 0)
    q0, p = q_ref[...], p_ref[...]
    res_ref[0, 0] = meas_ref[...] - alpha0 * q0 - alpha1 * ((q0 - alpha0 * p) + beta * q0)

    for copy in parameter_copies:
        copy.wait_send()
    first.finish()
    second.finish()
    sums.finish()


def write_kernel(vol_ref, res_ref, vol_out, res_out, wide_ref, sems):
    copies = [pltpu.make_async_copy(res_ref, res_out, sems.at[PLANES])]
    copies[0].start()
    for z in range(PLANES):
        wide_ref[z] = vol_ref[0, z].astype(jnp.float32)
        copies.append(pltpu.make_async_copy(wide_ref.at[z], vol_out.at[0, z], sems.at[z]))
        copies[-1].start()
    for copy in copies:
        copy.wait()


def local(grid_x, measured, shears, taps):
    f32, bf16 = jnp.float32, jnp.bfloat16
    vmem = pl.BlockSpec(memory_space=pltpu.VMEM)
    partners = VIEWS + GRID_Y + grid_x
    hbm = pl.BlockSpec(memory_space=pltpu.HBM)
    volume, residual = pl.pallas_call(
        functools.partial(solve_kernel, grid_x),
        name="solve",
        out_shape=(
            jax.ShapeDtypeStruct((1, PLANES, TX, TY), bf16),
            jax.ShapeDtypeStruct((1, 1, TX, TY), f32),
        ),
        in_specs=[hbm, hbm, hbm],
        out_specs=(vmem, vmem),
        scratch_shapes=[
            pltpu.VMEM((TX, TY), f32),
            pltpu.VMEM((2, PLANES), jnp.int32),
            pltpu.VMEM((4, PLANES), bf16),
            [pltpu.VMEM((RX, RY), bf16)] * VIEWS,
            [pltpu.VMEM((RX, RY), bf16)] * VIEWS,
            pltpu.VMEM((3 * TX, 3 * TY), f32),
            pltpu.VMEM(((VIEWS - 1) * PLANES, RY, TY), bf16),
            pltpu.VMEM((VIEWS - 1, 2, PLANES // GROUP, 128, GROUP * STRIP), bf16),
            pltpu.VMEM((TX, TY), f32),
            pltpu.VMEM((TX, TY), f32),
            [pltpu.VMEM((PLANES, TX, TY), f32)] * 2,
            pltpu.VMEM((GROUP * VIEWS, RY, TY), bf16),
            pltpu.VMEM((GROUP, 128, VIEWS * STRIP), bf16),
            [pltpu.VMEM((GROUP, VIEWS * STRIP, TY), bf16)] * 6,
            pltpu.VMEM((VIEWS, 8, 128), jnp.int32),
            pltpu.VMEM((VIEWS, 8, 128), f32),
            pltpu.SMEM((VIEWS, 8, 128), jnp.int32),
            pltpu.SMEM((VIEWS, 8, 128), f32),
            pltpu.VMEM((VIEWS, 8, 128), f32),
            pltpu.VMEM((GRID_Y, 8, 128), f32),
            pltpu.VMEM((grid_x, 8, 128), f32),
            pltpu.SemaphoreType.DMA((2, N_SEMS)),
            pltpu.SemaphoreType.DMA((2, N_SEMS)),
            pltpu.SemaphoreType.DMA((2, VIEWS)),
            pltpu.SemaphoreType.DMA((2, VIEWS)),
            pltpu.SemaphoreType.DMA((3,)),
            pltpu.SemaphoreType.DMA((partners,)),
            pltpu.SemaphoreType.DMA((partners,)),
        ],
        compiler_params=pltpu.CompilerParams(
            collective_id=0, has_side_effects=True, vmem_limit_bytes=50 * 1024 * 1024
        ),
    )(*[pltpu.with_memory_space_constraint(x, pltpu.HBM) for x in (measured, jnp.transpose(shears, (0, 2, 1)), jnp.transpose(taps, (0, 2, 1)))])
    return pl.pallas_call(
        write_kernel,
        name="write",
        out_shape=(
            jax.ShapeDtypeStruct((1, PLANES, TX, TY), f32),
            jax.ShapeDtypeStruct((1, 1, TX, TY), f32),
        ),
        in_specs=[vmem, vmem],
        out_specs=(hbm, hbm),
        scratch_shapes=[pltpu.VMEM((PLANES, TX, TY), f32), pltpu.SemaphoreType.DMA((PLANES + 1,))],
        compiler_params=pltpu.CompilerParams(vmem_limit_bytes=16 * 1024 * 1024),
    )(volume, residual)


def solution(mesh):
    placed = (P("view", "tile", None, None), P("view", None, None), P("view", None, None))
    return jax.shard_map(
        functools.partial(local, mesh.shape["tile"] // GRID_Y),
        mesh=mesh,
        in_specs=placed,
        out_specs=(P("tile", None, None, None), P("view", "tile", None, None)),
        check_vma=False,
    )
```

```python
import functools

import jax
import jax.numpy as jnp
from jax import lax
from jax.experimental import pallas as pl
from jax.experimental.pallas import tpu as pltpu
from jax.sharding import PartitionSpec as P

PLANES = 16
VIEWS = 4
GRID_Y = 8
TX = 256
TY = 256
HX = 96
HY = 128
RX = TX + 2 * HX
RY = TY + 2 * HY
WINDOW = 288
STRIP = 160
GROUP = 4
BAND = (
    (0, 0, 0, 128), (0, 1, 96, 32), (1, 1, 0, 96), (1, 2, 64, 64),
    (2, 2, 0, 64), (2, 3, 32, 96), (3, 3, 0, 32), (3, 4, 0, 128),
)
FAR = 1 << 20
TINY = 1e-6
MESH = pl.DeviceIdType.MESH

Z_BASE = 9
Y_BASE = Z_BASE + 2 * VIEWS
D_BASE = Y_BASE + 10 * VIEWS
N_SEMS = D_BASE + 4 * VIEWS

PARTS = {
    "first": (HX, HX), "last": (TX, HX), "middle": (2 * HX, TX - 2 * HX),
    "top": (0, HX), "bottom": (HX + TX, HX),
}
DIRECT = {(2, "top"), (2, "bottom"), (3, "top"), (1, "bottom")}
PART_ID = {"first": 0, "last": 1, "middle": 2, "top": 3, "bottom": 4}


def ring(index, step, size):
    return lax.rem(index + (step + size), size)


def solve_kernel(
    grid_x,
    meas_hbm, sh_hbm, tp_hbm,
    vol_ref, res_ref,
    meas_ref, sh_ref, tp_ref, e_refs, f_refs, field_ref, y_ref, x_ref, q_ref, p_ref, back_refs, by_ref, bx_ref, strip_refs,
    sh_v, tp_v, sh_s, tp_s, ra_ref, rb_ref,
    send_sems, recv_sems, p_send, p_recv, p_local, a_send, a_recv,
):
    tile = lax.axis_index("tile")
    view = lax.axis_index("view")
    gx = tile // GRID_Y
    gy = lax.rem(tile, GRID_Y)

    def at(row, col, vw):
        return (row * GRID_Y + col, vw)

    def to_view(step):
        return at(gx, gy, ring(view, step, VIEWS))

    def to_row(step):
        return at(ring(gx, step, grid_x), gy, view)

    def to_col(step):
        return at(gx, ring(gy, step, GRID_Y), view)

    def to_corner(row_step, col_step):
        return at(ring(gx, row_step, grid_x), ring(gy, col_step, GRID_Y), view)

    chips = GRID_Y // 2
    core = lax.rem(gy, 2)

    def to_view_chip(step):
        return at(gx, ring(gy, 2 * step[1], GRID_Y), ring(view, step[0], VIEWS))

    def to_row_core(step):
        return at(ring(gx, step[0], grid_x), gy + step[1] * (1 - 2 * core), view)

    def hops(step, sizes):
        return sum(min(k, n - k) for k, n in zip(step, sizes))

    def group(sizes):
        steps = [(a, b) for a in range(sizes[0]) for b in range(sizes[1]) if a + b]
        return sorted(steps, key=lambda step: -hops(step, sizes))

    view_chips, row_cores = group((VIEWS, chips)), group((grid_x, 2))

    next_chip = ring(gy, 2 * core - 1, GRID_Y)
    partners = (
        [to_view_chip(step) for step in view_chips]
        + [to_row_core(step) for step in row_cores]
        + [at(ring(gx, r, grid_x), next_chip, view) for r in (-1, 0, 1)]
    )
    barrier = pltpu.get_barrier_semaphore()
    for partner in partners:
        pl.semaphore_signal(barrier, inc=1, device_id=partner, device_id_type=MESH)

    loading = [
        pltpu.make_async_copy(src.at[0], dst, p_local.at[k])
        for k, (src, dst) in enumerate(((meas_hbm.at[0], meas_ref), (sh_hbm, sh_ref), (tp_hbm, tp_ref)))
    ]
    for copy in loading:
        copy.start()
    for copy in loading:
        copy.wait()
    e_refs[0][pl.ds(HX, TX), pl.ds(HY, TY)] = meas_ref[...].astype(jnp.bfloat16)
    sh_v[0] = jnp.zeros((8, 128), jnp.int32)
    sh_v[0, 0:2, 0:PLANES] = sh_ref[...]
    tp_v[0] = jnp.zeros((8, 128), jnp.float32)
    tp_v[0, 0:4, 0:PLANES] = tp_ref[...].astype(jnp.float32)

    pl.semaphore_wait(barrier, len(partners))

    class Exchange:
        def __init__(self, bufs, which):
            self.bufs, self.which, self.copies = bufs, which, {}

        def send(self, key, sem, src, dst, device):
            copy = pltpu.make_async_remote_copy(
                src_ref=src, dst_ref=dst,
                send_sem=send_sems.at[self.which, sem], recv_sem=recv_sems.at[self.which, sem],
                device_id=device, device_id_type=MESH,
            )
            copy.start()
            self.copies[key] = copy

        def region(self, slot, rows, cols):
            return self.bufs[slot].at[pl.ds(*rows), pl.ds(*cols)]

        def along_view(self, src_slot, dst_slot, part, sem, step):
            rows = PARTS[part]
            self.send(
                ("x", dst_slot, part), sem,
                self.region(src_slot, rows, (HY, TY)), self.region(dst_slot, rows, (HY, TY)),
                to_view(step),
            )

        def along_views(self):
            self.along_view(0, 3, "first", 0, 1)
            self.along_view(0, 1, "last", 1, -1)
            self.along_view(0, 3, "last", 2, 1)
            self.along_view(0, 1, "first", 3, -1)
            self.along_view(0, 3, "middle", 4, 1)
            self.along_view(0, 1, "middle", 5, -1)

        def own(self):
            for part in ("first", "last", "middle"):
                self.spread(0, part)

        def columns(self, slot, part):
            rows = PARTS[part]
            sem = Y_BASE + 10 * slot + 2 * PART_ID[part]
            self.send(
                ("y", slot, part, 0), sem,
                self.region(slot, rows, (HY, HY)), self.region(slot, rows, (HY + TY, HY)), to_col(-1),
            )
            self.send(
                ("y", slot, part, 1), sem + 1,
                self.region(slot, rows, (TY, HY)), self.region(slot, rows, (0, HY)), to_col(1),
            )

        def spread(self, slot, part):
            for k, (rim, halo, step) in enumerate((("first", "bottom", -1), ("last", "top", 1))):
                if part == rim:
                    self.send(
                        ("z", slot, halo), Z_BASE + 2 * slot + k,
                        self.region(slot, PARTS[rim], (HY, TY)),
                        self.region(slot, PARTS[halo], (HY, TY)), to_row(step),
                    )
                    if (slot, halo) in DIRECT:
                        for side, (src, dst, turn) in enumerate(((HY, HY + TY, -1), (TY, 0, 1))):
                            self.send(
                                ("d", slot, halo, side), D_BASE + 4 * slot + 2 * k + side,
                                self.region(slot, PARTS[rim], (src, HY)),
                                self.region(slot, PARTS[halo], (dst, HY)), to_corner(step, turn),
                            )
            self.columns(slot, part)

        def arrive(self, slot, part):
            self.copies["x", slot, part].wait_recv()
            if slot == 3 and part == "first":
                self.along_view(3, 2, part, 6, 1)
            if slot == 1 and part == "last":
                self.along_view(1, 2, part, 7, -1)
            if slot == 3 and part == "middle":
                self.along_view(3, 2, part, 8, 1)
            self.spread(slot, part)

        def corners(self, slot):
            for halo, edge in (("top", 0), ("bottom", grid_x - 1)):
                if (slot, halo) not in DIRECT:
                    self.copies["z", slot, halo].wait_recv()
                    start, size = PARTS[halo]

                    @pl.when(gx == edge)
                    def _():
                        self.bufs[slot][pl.ds(start, size), pl.ds(HY, TY)] = jnp.zeros((size, TY), jnp.bfloat16)

                    self.columns(slot, halo)

        def complete(self, slot):
            for halo, edge in (("top", 0), ("bottom", grid_x - 1)):
                if (slot, halo) in DIRECT:
                    self.copies["z", slot, halo].wait_recv()
                    for side in (0, 1):
                        self.copies["d", slot, halo, side].wait_recv()
                    start, size = PARTS[halo]

                    @pl.when(gx == edge)
                    def _():
                        self.bufs[slot][pl.ds(start, size), :] = jnp.zeros((size, RY), jnp.bfloat16)

            for part in PARTS:
                for side in (0, 1):
                    if ("y", slot, part, side) in self.copies:
                        self.copies["y", slot, part, side].wait_recv()
            for side, edge in ((0, 0), (HY + TY, GRID_Y - 1)):
                @pl.when(gy == edge)
                def _():
                    self.bufs[slot][:, pl.ds(side, HY)] = jnp.zeros((RX, HY), jnp.bfloat16)

        def finish(self):
            for copy in self.copies.values():
                copy.wait_send()

    first = Exchange(e_refs, 0)

    parameter_copies = []
    for step in range(1, VIEWS):
        slot = VIEWS - step
        for which, ref in ((0, sh_v), (1, tp_v)):
            copy = pltpu.make_async_remote_copy(
                src_ref=ref.at[0], dst_ref=ref.at[slot],
                send_sem=p_send.at[which, slot], recv_sem=p_recv.at[which, slot],
                device_id=to_view(step), device_id_type=MESH,
            )
            copy.start()
            parameter_copies.append(copy)

    first.along_views()

    def tables(first_slot, count):
        local = [
            pltpu.make_async_copy(src.at[pl.ds(first_slot, count)], dst.at[pl.ds(first_slot, count)], p_local.at[k])
            for k, (src, dst) in enumerate(((sh_v, sh_s), (tp_v, tp_s)))
        ]
        for copy in local:
            copy.start()
        for copy in local:
            copy.wait()

    first.own()

    column_low = jnp.where(gy == 0, 0, -FAR)
    column_high = jnp.where(gy == GRID_Y - 1, TY, FAR)
    row_low = jnp.where(gx == 0, 0, -FAR)
    row_high = jnp.where(gx == grid_x - 1, TX, FAR)

    row16 = lax.broadcasted_iota(jnp.int32, (16, 128), 0)
    col16 = lax.broadcasted_iota(jnp.int32, (16, 128), 1)
    below = (row16 - col16).astype(jnp.int16)
    beyond = (col16 - row16).astype(jnp.int16)

    def spread16(x):
        return jnp.full((16, 128), x, jnp.int32).astype(jnp.int16)

    def narrow(weights):
        return [jnp.broadcast_to(w, (16, 128)).astype(jnp.bfloat16) for w in weights]

    def band(distance, first, weights):
        value = jnp.zeros((16, 128), jnp.bfloat16)
        for at, weight in zip(first, weights):
            value = jnp.where(distance == at, weight, value)
        return value

    def build(slot):
        def one(z, carry):
            pair = (slot - 1) * PLANES + z
            y_ref[pair, 0:32, 0:128] = jnp.zeros((32, 128), jnp.bfloat16)
            y_ref[pair, 352:512, 0:128] = jnp.zeros((160, 128), jnp.bfloat16)
            y_ref[pair, 0:160, 128:256] = jnp.zeros((160, 128), jnp.bfloat16)
            y_ref[pair, 480:512, 128:256] = jnp.zeros((32, 128), jnp.bfloat16)
            shear = sh_s[0, 1, z]
            first = [spread16(sh_s[slot, 1, z] - shear + (HY - 32 + k)) for k in (-1, 0, 1)]
            a0, a1 = tp_s[0, 2, z], tp_s[0, 3, z]
            b0, b1 = tp_s[slot, 2, z], tp_s[slot, 3, z]
            low, high = shear + column_low, shear + column_high
            weights = []
            for in0, in1 in (
                (col16 >= low, col16 >= low - 1),
                (col16 + 128 < high, col16 + 128 < high - 1),
            ):
                weights.append(narrow((
                    jnp.where(in0, a0 * b1, 0.0),
                    jnp.where(in0, a0 * b0, 0.0) + jnp.where(in1, a1 * b1, 0.0),
                    jnp.where(in1, a1 * b0, 0.0),
                )))
            for r in range(0, 320, 16):
                distance = below + jnp.int16(r)
                y_ref[pair, pl.ds(32 + r, 16), 0:128] = band(distance, first, weights[0])
                y_ref[pair, pl.ds(160 + r, 16), 128:256] = band(distance, first, weights[1])
            return carry

        lax.fori_loop(0, PLANES, one, 0)

    def build_rows(slot):
        def one(g, carry):
            scalars = []
            for u in range(GROUP):
                z = GROUP * g + u
                shear = sh_s[0, 0, z]
                first_row = HX - 1 + sh_s[slot, 0, z] - shear
                m = first_row - lax.shift_right_logical(first_row, 4) * 16 + STRIP * u
                a0, a1 = tp_s[0, 0, z] * (1.0 / PLANES), tp_s[0, 1, z] * (1.0 / PLANES)
                b0, b1 = tp_s[slot, 0, z], tp_s[slot, 1, z]
                scalars.append((m, a0 * b1, a0 * b0, a1 * b1, a1 * b0, shear + row_low, shear + row_high))
            for u, block, row_start, size in BAND:
                m, am, az, bz, bp, low, high = scalars[u]
                plain = narrow((am, az + bz, bp))
                first = [spread16(m + k) for k in (0, 1, 2)]
                for r in range(row_start, row_start + size, 16):
                    distance = beyond + jnp.int16(128 * block - r)
                    for half in (0, 1):
                        weights = plain
                        if (half == 0 and r < 48) or (half == 1 and r >= 80):
                            row = row16 + (r + 128 * half)
                            in0, in1 = (row >= low, row >= low - 1) if half == 0 else (row < high, row < high - 1)
                            weights = narrow((
                                jnp.where(in0, am, 0.0),
                                jnp.where(in0, az, 0.0) + jnp.where(in1, bz, 0.0),
                                jnp.where(in1, bp, 0.0),
                            ))
                        x_ref[slot - 1, half, g, pl.ds(r, 16), pl.ds(128 * block, 128)] = band(distance, first, weights)
            return carry

        lax.fori_loop(0, PLANES // GROUP, one, 0)

    def fields():
        row = lax.broadcasted_iota(jnp.int32, (TX, 128), 0)

        def factors(shear, w0, w1, low, high, scale):
            in0 = (row >= shear + low) & (row < shear + high)
            in1 = (row >= shear + low - 1) & (row < shear + high - 1)
            cross = w0 * w1 * scale
            return jnp.concatenate([
                jnp.where(in0, cross, 0.0),
                jnp.where(in0, w0 * w0 * scale, 0.0) + jnp.where(in1, w1 * w1 * scale, 0.0),
                jnp.where(in1, cross, 0.0),
            ], axis=0).astype(jnp.bfloat16)

        along_x = factors(sh_v[0, 0:1, :], tp_v[0, 0:1, :], tp_v[0, 1:2, :], row_low, row_high, 1.0 / PLANES)
        along_y = factors(sh_v[0, 1:2, :], tp_v[0, 2:3, :], tp_v[0, 3:4, :], column_low, column_high, 1.0)
        field_ref[...] = lax.dot_general(
            along_x, along_y, (((1,), (1,)), ((), ())), preferred_element_type=jnp.float32
        )

    def stencil(src_ref, out_ref):
        def rows(i, carry):
            start = i * 64
            x = src_ref[pl.ds(pl.multiple_of(HX - 16 + start, 16), 96), :].astype(jnp.float32)
            total = jnp.zeros((64, TY), jnp.float32)
            for l in range(3):
                shifted = pltpu.roll(x, (RY + 1 - l) % RY, 1)[:, HY : HY + TY]
                for k in range(3):
                    term = pltpu.roll(shifted, (96 + 1 - k) % 96, 0)[16:80]
                    total = total + term * field_ref[pl.ds(pl.multiple_of(TX * k + start, 64), 64), TY * l : TY * (l + 1)]
            out_ref[pl.ds(pl.multiple_of(start, 64), 64), :] = total
            return carry

        lax.fori_loop(0, TX // 64, rows, 0)

    def apply(src_ref, out_ref, slot):
        for z in range(PLANES):
            first_row = HX - 1 + sh_s[slot, 0, z] - sh_s[0, 0, z]
            start = lax.shift_right_logical(first_row, 4) * 16
            t = jnp.dot(
                src_ref[pl.ds(start, WINDOW), :], y_ref[(slot - 1) * PLANES + z], preferred_element_type=jnp.float32
            ).astype(jnp.bfloat16)
            strip = pl.ds(STRIP * (z % GROUP), STRIP)
            strip_refs[0][z // GROUP, strip, :] = t[0:STRIP]
            strip_refs[1][z // GROUP, strip, :] = t[128 : 128 + STRIP]
        for half, t_ref in enumerate(strip_refs[0:2]):
            total = out_ref[pl.ds(128 * half, 128), :]
            for g in range(PLANES // GROUP):
                total = total + jnp.dot(
                    x_ref[slot - 1, half, g],
                    t_ref[g],
                    preferred_element_type=jnp.float32,
                )
            out_ref[pl.ds(128 * half, 128), :] = total

    def lanes(x):
        s = jnp.sum(x, axis=0, keepdims=True)
        return s[:, 0:128] + s[:, 128:256]

    class Sum:
        def __init__(self, rows):
            self.stages = (
                (ra_ref, view * chips + gy // 2, VIEWS * chips, view_chips, to_view_chip, 0),
                (rb_ref, gx * 2 + core, grid_x * 2, row_cores, to_row_core, VIEWS * chips),
            )
            self.copies = []
            pad = jnp.zeros((8 - len(rows), 128), jnp.float32)
            self.value = jnp.concatenate(list(rows) + [pad], axis=0)

        def send(self, stage):
            ref, me, size, steps, to, base = self.stages[stage]
            ref[me] = self.value
            self.current = []
            for k, step in enumerate(steps):
                copy = pltpu.make_async_remote_copy(
                    src_ref=ref.at[me], dst_ref=ref.at[me],
                    send_sem=a_send.at[base + k], recv_sem=a_recv.at[base + k],
                    device_id=to(step), device_id_type=MESH,
                )
                copy.start()
                self.current.append(copy)
            self.copies += self.current

        def receive(self, stage):
            ref, me, size, steps, to, base = self.stages[stage]
            for copy in self.current:
                copy.wait_recv()
            total = ref[0]
            for i in range(1, size):
                total = total + ref[i]
            self.value = total

        def row(self, i):
            return jnp.sum(self.value[i : i + 1, :], axis=1, keepdims=True)

        def finish(self):
            for copy in self.copies:
                copy.wait_send()

    by_ref[...] = jnp.zeros(by_ref.shape, jnp.bfloat16)

    def back(chunk, sources):
        refs = [(e_refs, f_refs)[k] for k in sources]
        for u in range(GROUP):
            z = GROUP * chunk + u
            for slot in range(VIEWS):
                place = lax.rem(view + slot, VIEWS)
                d = sh_s[slot, 1, z]
                weights = narrow((tp_s[slot, 3, z], tp_s[slot, 2, z]))
                at = [spread16(d + (HY - 80 + k)) for k in (-1, 0)]
                pair = VIEWS * u + slot
                for r in range(0, 224, 16):
                    value = band(below + jnp.int16(r), at, weights)
                    by_ref[pair, pl.ds(80 + r, 16), 0:128] = value
                    by_ref[pair, pl.ds(208 + r, 16), 128:256] = value
                start = lax.shift_right_logical(HX - 1 + sh_s[slot, 0, z], 4) * 16
                rows = [ref[slot][pl.ds(start, WINDOW), :] for ref in refs]
                t = jnp.dot(
                    jnp.concatenate(rows, axis=0) if len(rows) > 1 else rows[0],
                    by_ref[pair], preferred_element_type=jnp.float32,
                ).astype(jnp.bfloat16)
                for k in range(2 * len(refs)):
                    first = WINDOW * (k // 2) + 128 * (k % 2)
                    strip_refs[k][u, pl.ds(STRIP * place, STRIP), :] = t[first : first + STRIP]
            for v, block, row_start, size in BAND:
                slot = lax.rem(v - view + VIEWS, VIEWS)
                first_row = HX - 1 + sh_s[slot, 0, z]
                m = first_row - lax.shift_right_logical(first_row, 4) * 16 + STRIP * v
                weights = narrow((tp_s[slot, 1, z] * (PLANES**-0.5), tp_s[slot, 0, z] * (PLANES**-0.5)))
                at = [spread16(m + k) for k in (0, 1)]
                for r in range(row_start, row_start + size, 16):
                    bx_ref[u, pl.ds(r, 16), pl.ds(128 * block, 128)] = band(
                        beyond + jnp.int16(128 * block - r), at, weights
                    )
        for u in range(GROUP):
            z = GROUP * chunk + u
            for k in range(2 * len(refs)):
                back_refs[sources[k // 2]][z, pl.ds(128 * (k % 2), 128), :] = jnp.dot(
                    bx_ref[u], strip_refs[k][u], preferred_element_type=jnp.float32
                )

    fields()
    for copy in parameter_copies:
        copy.wait_recv()
    tables(0, VIEWS)
    first.corners(0)
    first.arrive(3, "first")
    first.arrive(1, "last")
    build(3)
    build_rows(3)
    first.arrive(3, "last")
    first.arrive(1, "first")
    first.arrive(3, "middle")
    first.arrive(1, "middle")
    first.complete(0)
    stencil(e_refs[0], q_ref)
    first.corners(3)
    first.corners(1)
    first.arrive(2, "first")
    first.arrive(2, "last")
    build(1)
    build_rows(1)
    first.arrive(2, "middle")
    build(2)
    build_rows(2)
    for slot in (3, 1, 2):
        first.complete(slot)
        apply(e_refs[slot], q_ref, slot)

    second = Exchange(f_refs, 1)
    f_refs[0][pl.ds(HX, TX), pl.ds(HY, TY)] = q_ref[...].astype(jnp.bfloat16)
    second.along_views()
    second.own()
    back(0, (0,))
    second.corners(0)
    for part in ("first", "last", "middle"):
        second.arrive(3, part)
        second.arrive(1, {"first": "last", "last": "first", "middle": "middle"}[part])
    second.complete(0)
    stencil(f_refs[0], p_ref)
    second.corners(3)
    second.corners(1)
    second.arrive(2, "first")
    second.arrive(2, "last")
    second.arrive(2, "middle")
    back(1, (0,))
    for slot in (3, 1, 2):
        second.complete(slot)
        apply(f_refs[slot], p_ref, slot)

    r0 = e_refs[0][pl.ds(HX, TX), pl.ds(HY, TY)].astype(jnp.float32)
    q0, p = q_ref[...], p_ref[...]
    sums = Sum([lanes(r0 * q0), lanes(q0 * q0), lanes(r0 * p), lanes(q0 * p), lanes(p * p)])
    sums.send(0)
    back(2, (0, 1))
    sums.receive(0)
    sums.send(1)
    back(3, (0, 1))
    back(0, (1,))
    back(1, (1,))
    sums.receive(1)
    r0q0, q0q0, r0p, q0p, pp = [sums.row(i) for i in range(5)]
    gamma0 = r0q0
    alpha0 = gamma0 / (q0q0 + TINY)
    gamma1 = r0q0 - alpha0 * (r0p + q0q0) + alpha0 * alpha0 * q0p
    beta = gamma1 / (gamma0 + TINY)
    h1h1 = q0q0 - 2.0 * alpha0 * q0p + alpha0 * alpha0 * pp
    h1q0 = q0q0 - alpha0 * q0p
    alpha1 = gamma1 / (h1h1 + 2.0 * beta * h1q0 + beta * beta * q0q0 + TINY)

    weight0 = alpha0 + alpha1 * beta + alpha1
    weight1 = alpha1 * alpha0

    def combine(z, carry):
        vol_ref[0, z] = (weight0 * back_refs[0][z] - weight1 * back_refs[1][z]).astype(jnp.bfloat16)
        return carry

    lax.fori_loop(0, PLANES, combine, 0)
    q0, p = q_ref[...], p_ref[...]
    res_ref[0, 0] = meas_ref[...] - alpha0 * q0 - alpha1 * ((q0 - alpha0 * p) + beta * q0)

    for copy in parameter_copies:
        copy.wait_send()
    first.finish()
    second.finish()
    sums.finish()


def write_kernel(vol_ref, res_ref, vol_out, res_out, wide_ref, sems):
    copies = [pltpu.make_async_copy(res_ref, res_out, sems.at[PLANES])]
    copies[0].start()
    for z in range(PLANES):
        wide_ref[z] = vol_ref[0, z].astype(jnp.float32)
        copies.append(pltpu.make_async_copy(wide_ref.at[z], vol_out.at[0, z], sems.at[z]))
        copies[-1].start()
    for copy in copies:
        copy.wait()


def local(grid_x, measured, shears, taps):
    f32, bf16 = jnp.float32, jnp.bfloat16
    vmem = pl.BlockSpec(memory_space=pltpu.VMEM)
    partners = VIEWS * GRID_Y // 2 + 2 * grid_x
    hbm = pl.BlockSpec(memory_space=pltpu.HBM)
    volume, residual = pl.pallas_call(
        functools.partial(solve_kernel, grid_x),
        name="solve",
        out_shape=(
            jax.ShapeDtypeStruct((1, PLANES, TX, TY), bf16),
            jax.ShapeDtypeStruct((1, 1, TX, TY), f32),
        ),
        in_specs=[hbm, hbm, hbm],
        out_specs=(vmem, vmem),
        scratch_shapes=[
            pltpu.VMEM((TX, TY), f32),
            pltpu.VMEM((2, PLANES), jnp.int32),
            pltpu.VMEM((4, PLANES), bf16),
            [pltpu.VMEM((RX, RY), bf16)] * VIEWS,
            [pltpu.VMEM((RX, RY), bf16)] * VIEWS,
            pltpu.VMEM((3 * TX, 3 * TY), f32),
            pltpu.VMEM(((VIEWS - 1) * PLANES, RY, TY), bf16),
            pltpu.VMEM((VIEWS - 1, 2, PLANES // GROUP, 128, GROUP * STRIP), bf16),
            pltpu.VMEM((TX, TY), f32),
            pltpu.VMEM((TX, TY), f32),
            [pltpu.VMEM((PLANES, TX, TY), f32)] * 2,
            pltpu.VMEM((GROUP * VIEWS, RY, TY), bf16),
            pltpu.VMEM((GROUP, 128, VIEWS * STRIP), bf16),
            [pltpu.VMEM((GROUP, VIEWS * STRIP, TY), bf16)] * 4,
            pltpu.VMEM((VIEWS, 8, 128), jnp.int32),
            pltpu.VMEM((VIEWS, 8, 128), f32),
            pltpu.SMEM((VIEWS, 8, 128), jnp.int32),
            pltpu.SMEM((VIEWS, 8, 128), f32),
            pltpu.VMEM((VIEWS * GRID_Y // 2, 8, 128), f32),
            pltpu.VMEM((grid_x * 2, 8, 128), f32),
            pltpu.SemaphoreType.DMA((2, N_SEMS)),
            pltpu.SemaphoreType.DMA((2, N_SEMS)),
            pltpu.SemaphoreType.DMA((2, VIEWS)),
            pltpu.SemaphoreType.DMA((2, VIEWS)),
            pltpu.SemaphoreType.DMA((3,)),
            pltpu.SemaphoreType.DMA((partners,)),
            pltpu.SemaphoreType.DMA((partners,)),
        ],
        compiler_params=pltpu.CompilerParams(
            collective_id=0, has_side_effects=True, vmem_limit_bytes=50 * 1024 * 1024
        ),
    )(*[pltpu.with_memory_space_constraint(x, pltpu.HBM) for x in (measured, jnp.transpose(shears, (0, 2, 1)), jnp.transpose(taps, (0, 2, 1)))])
    return pl.pallas_call(
        write_kernel,
        name="write",
        out_shape=(
            jax.ShapeDtypeStruct((1, PLANES, TX, TY), f32),
            jax.ShapeDtypeStruct((1, 1, TX, TY), f32),
        ),
        in_specs=[vmem, vmem],
        out_specs=(hbm, hbm),
        scratch_shapes=[pltpu.VMEM((PLANES, TX, TY), f32), pltpu.SemaphoreType.DMA((PLANES + 1,))],
        compiler_params=pltpu.CompilerParams(vmem_limit_bytes=16 * 1024 * 1024),
    )(volume, residual)


def solution(mesh):
    placed = (P("view", "tile", None, None), P("view", None, None), P("view", None, None))
    return jax.shard_map(
        functools.partial(local, mesh.shape["tile"] // GRID_Y),
        mesh=mesh,
        in_specs=placed,
        out_specs=(P("tile", None, None, None), P("view", "tile", None, None)),
        check_vma=False,
    )
```
